32 devices in a mesh: depth: 2 (over core), lx: 4 (over y, x), ly: 4 (over z).
Axes of the slice: x: 2, y: 2, z: 4, core: 2. Of those that a mesh axis runs over, the one named last changes fastest.
Arguments:
- iterate: float32 [32, 4, 32, 512], P('depth', None, 'lx', 'ly'), may hold values from -3 to 3
- right_side: float32 [32, 4, 32, 512], P('depth', None, 'lx', 'ly'), may hold values from -64 to 64
- storage: float32 [32, 32, 512], P('depth', 'lx', 'ly'), may hold values from 0.02 to 0.2
- zones: int32 [32, 32, 512], P('depth', 'lx', 'ly'), may hold values from 0 to 7
- counts: int32 [32, 512], P('lx', 'ly'), may hold values from 8 to 32
- materials: float32 [2, 8, 4, 4], replicated, as said below
Outputs:
- updated: float32 [32, 4, 32, 512], P('depth', None, 'lx', 'ly')
- coarse: float32 [16, 4, 32, 512], P('depth', None, 'lx', 'ly')
The draws below stay inside these ranges and needn't reach their ends.
Inputs may be any that keep to these rules, and one draw needn't show every extreme that they name: Nodes of column (x, y) with depth index below counts[x, y] are active. Each materials[t, k] is a symmetric matrix whose diagonal entries are positive and each larger than the sum of the magnitudes of the other entries in its row.
All inputs are finite; a program needn't handle non-finite values.
Results may differ from the reference program's by a relative error of at most 0.0003.
Values sent between devices are 32-bit elements; how exact they have to be, the bound alone decides.
No kernel may reach another device: no remote copies, remote signals or barrier semaphores. Data moves between devices by JAX's collectives and lax.ppermute only.
A program may use at most 64 MiB of HBM per device.

```python
import math
import jax
import jax.numpy as jnp
from jax import lax

CZ = 16
CX = 8
CY = 128
COMP = 4
NZONE = 8
NZ = 32
NX = 32
NY = 512
N_LX = 4
N_LY = 4


def draw_materials(key, part):
    key_diag, key_off = jax.random.split(jax.random.fold_in(key, 11))
    diagonal = jax.random.uniform(key_diag, (2, NZONE, 4), jnp.float32, 1.0, 1.6)
    coupling = jax.random.uniform(key_off, (2, NZONE, 4, 4), jnp.float32, -0.3, 0.3)
    coupling = 0.5 * (coupling + jnp.swapaxes(coupling, 2, 3))
    identity = jnp.eye(4, dtype=jnp.float32)
    matrix = coupling * (1.0 - identity) + diagonal[..., None] * identity
    scale = jnp.array([0.3, 64.0], jnp.float32)[:, None, None, None]
    return matrix * scale


def plant(result, own_key, least, top_value):
    extent = result.shape
    place = [jax.random.randint(jax.random.fold_in(own_key, axis), (), 0, extent[axis]) for axis in range(len(extent))]
    result = result.at[tuple(place)].set(least)
    longest = extent.index(max(extent))
    place[longest] = (place[longest] + 1) % extent[longest]
    return result.at[tuple(place)].set(top_value)


def block_levels(key, dims, cuts, least, top_value):
    def one(dim, shards_of):
        heights = jax.random.uniform(jax.random.fold_in(jax.random.fold_in(key, 6), dim), (shards_of,), jnp.float32, least / len(cuts), top_value / len(cuts))
        return jnp.repeat(jnp.exp(heights), dims[dim] // shards_of).reshape((-1,) + (1,) * (len(dims) - dim - 1))

    factor_of = one(*cuts[0])
    for cut in cuts[1:]:
        factor_of = factor_of * one(*cut)
    return factor_of


def bell_draw(stream_key, shape, width, limit, cuts=(), kind=jnp.bfloat16):
    values = jax.random.normal(stream_key, shape, jnp.float32) * width
    if len(cuts) > 0:
        values = block_levels(stream_key, shape, cuts, -0.22, 0.18) * values
    return jnp.clip(values, min=-limit, max=limit).astype(kind)


def setup_inputs(seed: int = 0) -> dict:
    arg_keys = jax.random.split(jax.random.key(seed), 7)
    iterate = bell_draw(arg_keys[0], (NZ, COMP, NX, NY), 0.5, 3.0, ((0, 2), (2, 4), (3, 4)), jnp.float32)
    right_side = bell_draw(arg_keys[1], (NZ, COMP, NX, NY), 10.0, 64.0, ((0, 2), (2, 4), (3, 4)), jnp.float32)
    storage = jnp.clip(jnp.exp(math.log(0.2) - 2.3025851 * jax.random.uniform(arg_keys[2], (NZ, NX, NY), jnp.float32) ** block_levels(arg_keys[2], (NZ, NX, NY), ((0, 2), (1, 4), (2, 4)), -0.2, 0.2)), 0.02, 0.2)
    zones = plant(jax.random.randint(arg_keys[3], (NZ, NX, NY), 0, NZONE), jax.random.fold_in(arg_keys[3], 1), 0, NZONE - 1).astype(jnp.int32)
    counts = plant(jax.random.randint(arg_keys[4], (NX, NY), CZ // 2, NZ + 1), jax.random.fold_in(arg_keys[4], 1), CZ // 2, NZ).astype(jnp.int32)
    materials = draw_materials(jax.random.fold_in(arg_keys[6], 71), 0)
    return {"iterate": iterate, "right_side": right_side, "storage": storage, "zones": zones, "counts": counts, "materials": materials}


def box_weights(values):
    values = 0.5 * values[:-2] + values[1:-1] + 0.5 * values[2:]
    values = 0.5 * values[..., :-2, :] + values[..., 1:-1, :] + 0.5 * values[..., 2:, :]
    return 0.5 * values[..., :-2] + values[..., 1:-1] + 0.5 * values[..., 2:]


def inner_part(values):
    return values[1:-1, ..., 1:-1, 1:-1]


def vertical_sum(values):
    return values[2:, ..., 1:-1, 1:-1] + values[:-2, ..., 1:-1, 1:-1]


def lateral_sum(values):
    return box_weights(values) - inner_part(values) - 0.5 * vertical_sum(values)


def lookup_table(weights, table):
    total = weights[0][:, None, None] * table[0][None, :, :, None, None]
    for index in range(1, len(weights)):
        total = total + weights[index][:, None, None] * table[index][None, :, :, None, None]
    return total


def block_apply(matrix, vector):
    total = matrix[..., :, 0, :, :] * vector[..., 0:1, :, :]
    for column in range(1, 4):
        total = total + matrix[..., :, column, :, :] * vector[..., column:column + 1, :, :]
    return total


def block_product(left, right):
    total = left[..., :, 0, :, :][..., :, None, :, :] * right[..., 0, :, :, :][..., None, :, :, :]
    for column in range(1, 4):
        total = total + left[..., :, column, :, :][..., :, None, :, :] * right[..., column, :, :, :][..., None, :, :, :]
    return total


def block_solve(matrix, right_part):
    rows = [[matrix[target, column] for column in range(4)] for target in range(4)]
    vectors = [right_part[target] for target in range(4)]
    for pivot_row in range(4):
        inverse = 1.0 / rows[pivot_row][pivot_row]
        for column in range(pivot_row + 1, 4):
            rows[pivot_row][column] = rows[pivot_row][column] * inverse
        vectors[pivot_row] = vectors[pivot_row] * inverse
        for target in range(4):
            if target != pivot_row:
                factor = rows[target][pivot_row]
                for column in range(pivot_row + 1, 4):
                    rows[target][column] = rows[target][column] - factor * rows[pivot_row][column]
                vectors[target] = vectors[target] - factor[None] * vectors[pivot_row]
    return jnp.stack(vectors)


def coefficients(codes_ext, materials, storage):
    zone_count = materials.shape[1]
    onehots = [(codes_ext == index + 1).astype(jnp.float32) for index in range(zone_count)]
    active_ext = (codes_ext > 0).astype(jnp.float32)
    lat_ext = lookup_table(onehots, materials[0])
    vert_ext = lookup_table(onehots, materials[1])
    lat_counts = [lateral_sum(item) for item in onehots]
    vert_counts = [vertical_sum(item) for item in onehots]
    lat_weight = lateral_sum(active_ext)
    vert_weight = vertical_sum(active_ext)
    active = inner_part(active_ext)
    beside_all = lookup_table(lat_counts, materials[0]) + lookup_table(vert_counts, materials[1])
    identity = jnp.eye(4, dtype=jnp.float32)[None, :, :, None, None]
    diagonal = storage[:, None, None] * identity + 0.5 * active[:, None, None] * (
        inner_part(lat_ext) * lat_weight[:, None, None] + inner_part(vert_ext) * vert_weight[:, None, None] + beside_all)
    column_codes = [item[:, 1:-1, 1:-1] for item in onehots]
    column_active = active_ext[:, 1:-1, 1:-1]
    link = column_active[:-1] * column_active[1:]
    pairs = 0.5 * lookup_table([(item[:-1] + item[1:]) * link for item in column_codes], materials[1])
    return active, active_ext, lat_ext, vert_ext, diagonal, pairs


def apply_operator(field_ext, coeffs):
    active, active_ext, lat_ext, vert_ext, diagonal, pairs = coeffs
    gated = field_ext * active_ext[:, None]
    lat_flow = block_apply(lat_ext, field_ext)
    vert_flow = block_apply(vert_ext, field_ext)
    off_part = block_apply(inner_part(lat_ext), lateral_sum(gated)) + lateral_sum(lat_flow)
    off_part = off_part + block_apply(inner_part(vert_ext), vertical_sum(gated)) + vertical_sum(vert_flow)
    return block_apply(diagonal, inner_part(field_ext)) - 0.5 * active[:, None] * off_part


def forward_sweep(diagonal, above, residual, carry_matrix, carry_columns):
    def advance(carry, level):
        coupled, columns = carry
        block, pair, value = level
        extra = jnp.concatenate([columns[:, :1] + value[:, None], columns[:, 1:]], axis=1)
        solved = block_solve(block - coupled, jnp.concatenate([pair, extra], axis=1))
        gain = solved[:, :4]
        rest = solved[:, 4:]
        return (block_product(pair, gain), block_product(pair, rest)), (gain, rest)

    (coupled, columns), (gains, rests) = lax.scan(advance, (carry_matrix, carry_columns), (diagonal, above, residual))
    return gains, rests, coupled, columns[:, 0]


def backward_sweep(gains, rests, incoming):
    def retreat(state, level):
        gain, rest = level
        width_gap = state.shape[1] - rest.shape[1]
        padding = jnp.zeros((4, width_gap) + rest.shape[2:], jnp.float32)
        state = jnp.concatenate([rest, padding], axis=1) + block_product(gain, state)
        return state, state

    return lax.scan(retreat, incoming, (gains, rests), reverse=True)[1]


def reference(iterate, right_side, storage, zones, counts, materials):
    depth_index = jnp.arange(NZ, dtype=jnp.int32)[:, None, None]
    codes = jnp.where(depth_index < counts[None], zones + 1, 0).astype(jnp.int32)
    codes_pad = jnp.pad(codes, 1)
    iterate_pad = jnp.pad(iterate, ((1, 1), (0, 0), (1, 1), (1, 1)))
    tiles = jnp.arange(N_LX * N_LY, dtype=jnp.int32)
    anchor = jnp.zeros((), jnp.int32)

    def tile_setup(tile):
        start_x = ((tile // N_LY) * CX).astype(jnp.int32)
        start_y = ((tile % N_LY) * CY).astype(jnp.int32)
        codes_ext = lax.dynamic_slice(codes_pad, (anchor, start_x, start_y), (NZ + 2, CX + 2, CY + 2))
        storage_tile = lax.dynamic_slice(storage, (anchor, start_x, start_y), (NZ, CX, CY))
        return start_x, start_y, coefficients(codes_ext, materials, storage_tile)

    def first_pass(tile):
        start_x, start_y, coeffs = tile_setup(tile)
        field_ext = lax.dynamic_slice(iterate_pad, (anchor, anchor, start_x, start_y), (NZ + 2, COMP, CX + 2, CY + 2))
        right_tile = lax.dynamic_slice(right_side, (anchor, anchor, start_x, start_y), (NZ, COMP, CX, CY))
        residual = coeffs[0][:, None] * (right_tile - apply_operator(field_ext, coeffs))
        gains, rests, coupled, vector = forward_sweep(coeffs[4], coeffs[5][1:], residual,
                                                      jnp.zeros((4, 4, CX, CY), jnp.float32),
                                                      jnp.zeros((4, 1, CX, CY), jnp.float32))
        states = backward_sweep(gains, rests, jnp.zeros((4, 1, CX, CY), jnp.float32))
        return residual, states[:, :, 0]

    def assemble(blocks):
        blocks = blocks.reshape(N_LX, N_LY, NZ, COMP, CX, CY)
        return blocks.transpose(2, 3, 0, 4, 1, 5).reshape(NZ, COMP, N_LX * CX, N_LY * CY)

    residual_tiles, correction_tiles = lax.map(first_pass, tiles)
    correction = assemble(correction_tiles)
    updated = iterate + correction
    correction_pad = jnp.pad(correction, ((1, 1), (0, 0), (1, 1), (1, 1)))

    def second_pass(inputs):
        tile, residual = inputs
        start_x, start_y, coeffs = tile_setup(tile)
        field_ext = lax.dynamic_slice(correction_pad, (anchor, anchor, start_x, start_y), (NZ + 2, COMP, CX + 2, CY + 2))
        return residual - apply_operator(field_ext, coeffs)

    smoothed = assemble(lax.map(second_pass, (tiles, residual_tiles)))
    odd_planes = smoothed[1::2]
    previous = jnp.concatenate([jnp.zeros_like(smoothed[:1]), odd_planes[:-1]], axis=0)
    coarse = 0.5 * previous + smoothed[0::2] + 0.5 * odd_planes
    return updated, coarse
```

```python
import functools

import jax
import jax.numpy as jnp
from jax import lax
from jax.experimental import pallas as pl
from jax.experimental.pallas import tpu as pltpu
from jax.sharding import PartitionSpec as P

PAIRS = [(i, j) for i in range(4) for j in range(i, 4)]
AT = {}
for _k, (_i, _j) in enumerate(PAIRS):
    AT[_i, _j] = AT[_j, _i] = _k

ROWS, LANES = 8, 128
SUMMED = 19
LINE = 24
F32 = jnp.float32
VMEM_LIMIT = 48 * 1024 * 1024


def row_index():
    return lax.broadcasted_iota(jnp.int32, (ROWS, LANES), 0)


def lane_index():
    return lax.broadcasted_iota(jnp.int32, (ROWS, LANES), 1)


def roll_rows(x, by):
    return pltpu.roll(x, by % x.shape[0], 0)


def roll_lanes(x, by):
    return pltpu.roll(x, by % LANES if isinstance(by, int) else lax.rem(by + LANES, LANES), 1)


def activity(codes):
    return jnp.where(codes > 0, 1.0, 0.0).astype(F32)


def lookup(tables, kind, codes, act):
    rows = jnp.maximum(codes - 1, 0)
    found = []
    for i, j in PAIRS:
        table = tables[kind * 16 + 4 * i + j]
        parts = [
            jnp.take_along_axis(table, rows[at : at + ROWS], axis=0, mode="promise_in_bounds")
            for at in range(0, rows.shape[0], ROWS)
        ]
        value = parts[0] if len(parts) == 1 else jnp.concatenate(parts, axis=0)
        found.append(value * act)
    return found


def apply_sym(matrix, vector):
    out = []
    for i in range(4):
        total = matrix[AT[i, 0]] * vector[0]
        for j in range(1, 4):
            total = total + matrix[AT[i, j]] * vector[j]
        out.append(total)
    return out


def summed_fields(tables, codes, field):
    act = activity(codes)
    lateral = lookup(tables, 0, codes, act)
    return [act] + lateral + [act * v for v in field] + apply_sym(lateral, field)


def level_of(side, n, levels):
    return side * (levels - 1) + (1 - 2 * side) * n


def pack_kernel(levels, iterate, right, storage, zones, counts, met, xm, ym, dm, codes_out):
    side = lax.axis_index("depth")
    lane = lane_index()
    counts_v = counts[...]
    xm[...] = jnp.zeros(xm.shape, F32)
    acc = [jnp.zeros((ROWS, LANES), F32) for _ in range(10)]
    for n in range(levels + 2):
        if n < levels:
            z = level_of(side, n, levels)
            code = jnp.where(z + side * levels < counts_v, zones[z] + 1, 0)
            fields = [code.astype(F32)] + [iterate[z, c] for c in range(4)]
            fields += [right[z, c] for c in range(4)] + [storage[z]]
        elif n == levels:
            fields = [met[4]] + [met[c] for c in range(4)]
            code = met[4].astype(jnp.int32)
        else:
            fields = [met[5]]
            code = met[5].astype(jnp.int32)
        codes_out[n] = code
        for k, value in enumerate(fields):
            xm[k, n : n + 1, :] = value[0:1]
            if k < 5:
                xm[10 + k, n : n + 1, :] = value[1:2]
            acc[k] = jnp.where(lane // 2 == n, roll_lanes(value, 2 * n), acc[k])
    for k in range(10):
        ym[k] = acc[k]
        dm[k] = acc[k][0:2]


def own_kernel(levels, iterate, codes, met, tables, out, u):
    side = lax.axis_index("depth")
    for k in range(SUMMED):
        u[0, k] = jnp.zeros((ROWS, LANES), F32)

    def fill(n, carry):
        z = level_of(side, n, levels)
        for k, value in enumerate(summed_fields(tables, codes[n], [iterate[z, c] for c in range(4)])):
            u[n + 1, k] = value
        return carry

    lax.fori_loop(0, levels, fill, 0)
    for k, value in enumerate(summed_fields(tables, codes[levels], [met[c] for c in range(4)])):
        u[levels + 1, k] = value

    def add(n, carry):
        for k in range(SUMMED):
            out[n, k] = u[n + 1, k] + 0.5 * (u[n, k] + u[n + 2, k])
        return carry

    lax.fori_loop(0, levels, add, 0)


def invert(m):
    d = lambda i, j: m[AT[i, j]]

    def small(a, b, c):
        ia = 1.0 / a
        l = b * ia
        ic = 1.0 / (c - l * b)
        lc = l * ic
        return ia + l * lc, -lc, ic

    a00, a01, a11 = small(d(0, 0), d(0, 1), d(1, 1))
    t00 = d(2, 0) * a00 + d(2, 1) * a01
    t01 = d(2, 0) * a01 + d(2, 1) * a11
    t10 = d(3, 0) * a00 + d(3, 1) * a01
    t11 = d(3, 0) * a01 + d(3, 1) * a11
    s00 = d(2, 2) - (t00 * d(2, 0) + t01 * d(2, 1))
    s01 = d(3, 2) - (t10 * d(2, 0) + t11 * d(2, 1))
    s11 = d(3, 3) - (t10 * d(3, 0) + t11 * d(3, 1))
    i22, i32, i33 = small(s00, s01, s11)
    u00 = i22 * t00 + i32 * t10
    u01 = i22 * t01 + i32 * t11
    u10 = i32 * t00 + i33 * t10
    u11 = i32 * t01 + i33 * t11
    i00 = a00 + (t00 * u00 + t10 * u10)
    i01 = a01 + (t00 * u01 + t10 * u11)
    i11 = a11 + (t01 * u01 + t11 * u11)
    return [i00, i01, -u00, -u10, i11, -u01, -u11, i22, i32, i33]


def sym_product(left, right):
    return [
        [
            (left[AT[i, 0]] * right[AT[0, j]] + left[AT[i, 1]] * right[AT[1, j]])
            + (left[AT[i, 2]] * right[AT[2, j]] + left[AT[i, 3]] * right[AT[3, j]])
            for j in range(4)
        ]
        for i in range(4)
    ]


def line_sum(values):
    return values + 0.5 * (roll_rows(values, 1) + roll_rows(values, -1))


def lane_sum(values):
    return values + 0.5 * (roll_lanes(values, 2) + roll_lanes(values, -2))


def widen(two_rows):
    return jnp.concatenate([two_rows, jnp.zeros((ROWS - 2, LANES), F32)], axis=0)


def sweep_kernel(
    levels, own, xm, ym, dm, iterate, right, storage, codes, met, tables,
    gains, rests, message, ends, codes_s,
    xw, yv, ys, fs, rs, ss, ps, ms, qs,
):
    side = lax.axis_index("depth")
    last_x = lax.axis_index("lx") == lax.axis_size("lx") - 1
    last_y = lax.axis_index("ly") == lax.axis_size("ly") - 1
    row, lane = row_index(), lane_index()
    wl = jnp.where(last_x & (row == 7), 0.0, 0.5).astype(F32)
    wu = jnp.where(last_x & (row == 6), 0.0, 0.5).astype(F32)
    vl = jnp.where(last_y & (lane == 127), 0.0, 0.5).astype(F32)
    vu = vl
    top = row == 7
    end = lane == 127
    start = lane == 0

    for r in range(2):
        line_codes = xm[10 * r].astype(jnp.int32)
        line_field = [xm[10 * r + 1 + c] for c in range(4)]
        for k, value in enumerate(summed_fields(tables, line_codes, line_field)):
            at = (2 * k + r) * LINE
            xw[at : at + LINE, :] = line_sum(value)

    corner = [widen(dm[k]) for k in range(10)]
    side_codes = ym[0].astype(jnp.int32)
    corner_codes = corner[0].astype(jnp.int32)
    side_u = summed_fields(tables, side_codes, [ym[1 + c] for c in range(4)])
    corner_u = summed_fields(tables, corner_codes, corner[1:5])
    for k in range(SUMMED):
        w0 = lane_sum(side_u[k])
        wd = lane_sum(corner_u[k])
        w1 = roll_rows(jnp.where(row < 1, wd, w0), -1)
        w2 = roll_rows(jnp.where(row < 2, wd, w0), -2)
        g = wl * w0 + wu * w2
        b = w1 + g
        h = g + 0.5 * roll_lanes(b, -1)
        yv[k] = jnp.where(lane % 2 == 0, b, roll_lanes(h, -1))
    for k in range(10):
        ys[k] = roll_rows(jnp.where(row < 1, corner[k], ym[k]), -1)

    def shift(value, k, n):
        up = jnp.where(top, xm[k, pl.ds(n, 1), :], roll_rows(value, -1))
        return jnp.where(end, roll_lanes(ys[k], 127 - 2 * n), roll_lanes(up, -1))

    def shift_level(n, carry):
        z = level_of(side, n, levels)
        codes_s[n] = shift(codes[n].astype(F32), 0, n).astype(jnp.int32)
        for c in range(4):
            fs[n + 1, c] = shift(iterate[z, c], 1 + c, n)
            rs[n, c] = shift(right[z, c], 5 + c, n)
        ss[n] = shift(storage[z], 9, n)
        return carry

    lax.fori_loop(0, levels, shift_level, 0)
    codes_s[levels] = shift(met[4], 0, levels).astype(jnp.int32)
    codes_s[levels + 1] = shift(met[5], 0, levels + 1).astype(jnp.int32)
    for c in range(4):
        fs[0, c] = jnp.zeros((ROWS, LANES), F32)
        fs[levels + 1, c] = shift(met[c], 1 + c, levels)
    for k in range(10):
        ms[0, k] = jnp.zeros((ROWS, LANES), F32)

    def assemble(n, carry):
        sums = []
        for k in range(SUMMED):
            w = own[n, k]
            beyond = xw[pl.ds(2 * k * LINE + n, ROWS, stride=LINE), :]
            w1 = roll_rows(jnp.where(row < 1, beyond, w), -1)
            w2 = roll_rows(jnp.where(row < 2, beyond, w), -2)
            g = wl * w + wu * w2
            b = w1 + g
            v = roll_lanes(yv[k], -2 * n)
            h = g + vu * roll_lanes(jnp.where(start, v, b), -1)
            sums.append(jnp.where(end, v, roll_lanes(h, -1)) + vl * b)
        act = activity(codes_s[n])
        act_next = activity(codes_s[n + 1])
        lateral = lookup(tables, 0, codes_s[n], act)
        here = lookup(tables, 1, codes_s[n], 0.5 * act * act_next)
        there = lookup(tables, 1, codes_s[n + 1], 0.5 * act * act_next)
        half = 0.5 * act
        below = [ms[n, k] for k in range(10)]
        above = [here[k] + there[k] for k in range(10)]
        half_sum = 0.5 * sums[0]
        block = []
        for k, (i, j) in enumerate(PAIRS):
            value = (lateral[k] * half_sum + half * sums[1 + k]) + (below[k] + above[k])
            block.append(value + ss[n] if i == j else value)
        for k in range(10):
            ms[n + 1, k] = above[k]
            ps[n, k] = block[k]
        field = [fs[n + 1, c] for c in range(4)]
        before = apply_sym(below, [fs[n, c] for c in range(4)])
        after = apply_sym(above, [fs[n + 2, c] for c in range(4)])
        diagonal = apply_sym(block, field)
        flow = apply_sym(lateral, sums[11:15])
        for c in range(4):
            around = (before[c] + after[c]) + (0.5 * flow[c] + half * sums[15 + c])
            qs[n, c] = act * (rs[n, c] - (diagonal[c] - around))
        return carry

    lax.fori_loop(0, levels, assemble, 0)

    def eliminate(n, carry):
        coupled, carried = carry
        block = [ps[n, k] - coupled[k] for k in range(10)]
        value = [qs[n, c] + carried[c] for c in range(4)]
        link = [ms[n + 1, k] for k in range(10)]
        inverse = invert(block)
        gain = sym_product(inverse, link)
        rest = apply_sym(inverse, value)
        for i in range(4):
            rests[n, i] = rest[i]
            for j in range(4):
                gains[n, 4 * i + j] = gain[i][j]
        new_coupled = []
        for i, j in PAIRS:
            new_coupled.append(
                (link[AT[i, 0]] * gain[0][j] + link[AT[i, 1]] * gain[1][j])
                + (link[AT[i, 2]] * gain[2][j] + link[AT[i, 3]] * gain[3][j])
            )
        return new_coupled, apply_sym(link, rest), block, value

    zeros = [jnp.zeros((ROWS, LANES), F32) for _ in range(10)]
    coupled, carried = lax.fori_loop(
        0, levels - 1, lambda n, c: eliminate(n, c)[:2], (zeros, zeros[:4])
    )
    coupled, carried, block, value = eliminate(levels - 1, (coupled, carried))
    for k in range(10):
        message[k] = coupled[k]
        ends[k] = block[k]
    for c in range(4):
        message[10 + c] = carried[c]
        ends[10 + c] = value[c]
    for at, n in ((14, levels - 1), (34, levels - 2)):
        for k in range(16):
            message[at + k] = gains[n, k]
        for c in range(4):
            message[at + 16 + c] = rests[n, c]


def back_kernel(levels, gains, rests, ends, got, codes_s, tables, xs, kx, x3, y3, d3):
    lane = lane_index()

    def carry_on(gain, rest, x):
        out = []
        for i in range(4):
            out.append(
                rest[i] + ((gain[4 * i] * x[0] + gain[4 * i + 1] * x[1])
                           + (gain[4 * i + 2] * x[2] + gain[4 * i + 3] * x[3]))
            )
        return out

    block = [ends[k] - got[k] for k in range(10)]
    value = [ends[10 + c] + got[10 + c] for c in range(4)]
    x = apply_sym(invert(block), value)
    x_met = carry_on([got[14 + k] for k in range(16)], [got[30 + c] for c in range(4)], x)
    x_far = carry_on([got[34 + k] for k in range(16)], [got[50 + c] for c in range(4)], x_met)
    for c in range(4):
        xs[levels - 1, c] = x[c]
        xs[levels, c] = x_met[c]
        xs[levels + 1, c] = x_far[c]

    def retreat(step, x):
        n = levels - 2 - step
        x = carry_on([gains[n, k] for k in range(16)], [rests[n, c] for c in range(4)], x)
        for c in range(4):
            xs[n, c] = x[c]
        return x

    lax.fori_loop(0, levels - 1, retreat, x)

    x3[...] = jnp.zeros(x3.shape, F32)
    acc = [jnp.zeros((ROWS, LANES), F32) for _ in range(8)]
    for n in range(levels + 2):
        field = [xs[n, c] for c in range(4)]
        act = activity(codes_s[n])
        flow = apply_sym(lookup(tables, 0, codes_s[n], act), field)
        for c in range(4):
            kx[n, c] = flow[c]
        for k, value in enumerate(field + flow):
            x3[2 * k, n : n + 1, :] = value[6:7]
            x3[2 * k + 1, n : n + 1, :] = value[7:8]
            acc[k] = jnp.where(lane // 2 == n, roll_lanes(value, 2 * n + 2), acc[k])
    for k in range(8):
        y3[k] = acc[k]
        d3[k] = acc[k][6:8]


def finish_kernel(
    levels, xs, kx, x3, y3, d3, iterate, codes, tables, updated, coarse, xw, yv, ys, sm
):
    side = lax.axis_index("depth")
    first_x = lax.axis_index("lx") == 0
    first_y = lax.axis_index("ly") == 0
    last_x = lax.axis_index("lx") == lax.axis_size("lx") - 1
    last_y = lax.axis_index("ly") == lax.axis_size("ly") - 1
    row, lane = row_index(), lane_index()
    wl = jnp.where(first_x & (row == 0), 0.0, 0.5).astype(F32)
    wu = jnp.where(last_x & (row == 7), 0.0, 0.5).astype(F32)
    vu = jnp.where(last_y & (lane == 127), 0.0, 0.5).astype(F32)
    vl = jnp.where(first_y, 0.0, 0.5).astype(F32)
    end = lane == 127
    start = lane == 0

    for k in range(8):
        for r in range(2):
            at = (2 * k + r) * LINE
            xw[at : at + LINE, :] = line_sum(x3[2 * k + r])
        corner = widen(d3[k])
        w2 = lane_sum(y3[k])
        wd = lane_sum(corner)
        w0 = jnp.where(row < 2, wd, roll_rows(w2, 2))
        w1 = jnp.where(row < 1, roll_rows(wd, -1), roll_rows(w2, 1))
        g = wl * w0 + wu * w2
        b = w1 + g
        h = g + vl * roll_lanes(b, 1)
        yv[k] = jnp.where(lane % 2 == 1, b, roll_lanes(h, 1))
        if k < 4:
            ys[k] = jnp.where(row < 1, roll_rows(corner, -1), roll_rows(y3[k], 1))

    def lateral(n, k, w):
        beyond = xw[pl.ds(2 * k * LINE + n, ROWS, stride=LINE), :]
        w0 = jnp.where(row < 2, beyond, roll_rows(w, 2))
        w1 = jnp.where(row < 1, roll_rows(beyond, -1), roll_rows(w, 1))
        g = wl * w0 + wu * w
        b = w1 + g
        v = roll_lanes(yv[k], -2 * n - 2)
        h = g + 0.5 * roll_lanes(jnp.where(end, v, b), 1)
        return jnp.where(start, v, roll_lanes(h, 1)) + vu * b

    def smooth(n, first):
        sums = []
        for k in range(8):
            ref, c = (xs, k) if k < 4 else (kx, k - 4)
            outer = ref[n + 1, c] if first else ref[n - 1, c] + ref[n + 1, c]
            sums.append(lateral(n, k, ref[n, c] + 0.5 * outer))
        act = activity(codes[n])
        half = 0.5 * act
        flow = apply_sym(lookup(tables, 0, codes[n], half), sums[:4])
        for c in range(4):
            sm[n + 1, c] = flow[c] + half * sums[4 + c]

    def place(n):
        z = level_of(side, n, levels)
        for c in range(4):
            low = jnp.where(row < 1, x3[2 * c + 1, pl.ds(n, 1), :], roll_rows(xs[n, c], 1))
            x = jnp.where(start, roll_lanes(ys[c], -2 * n - 1), roll_lanes(low, 1))
            updated[z, c] = iterate[z, c] + x

    for c in range(4):
        sm[0, c] = jnp.zeros((ROWS, LANES), F32)
    smooth(0, True)
    place(0)

    def level(n, carry):
        smooth(n, False)
        place(n)
        return carry

    lax.fori_loop(1, levels, level, 0)
    smooth(levels, False)

    def restrict(k, carry):
        at = side * (levels + 1) + (1 - 2 * side) * 2 * k
        step = 1 - 2 * side
        for c in range(4):
            coarse[k, c] = sm[at + step, c] + 0.5 * (sm[at, c] + sm[at + 2 * step, c])
        return carry

    lax.fori_loop(0, levels // 2, restrict, 0)


def call(kernel, outs, *args, scratch=()):
    whole = pl.BlockSpec(memory_space=pltpu.VMEM)
    return pl.pallas_call(
        kernel,
        out_shape=[jax.ShapeDtypeStruct(s, t) for s, t in outs],
        in_specs=[whole] * len(args),
        out_specs=[whole] * len(outs),
        scratch_shapes=[pltpu.VMEM(s, F32) for s in scratch],
        compiler_params=pltpu.CompilerParams(vmem_limit_bytes=VMEM_LIMIT),
    )(*args)


def around(x, dx, dy):
    nx, ny = lax.axis_size("lx"), lax.axis_size("ly")
    pairs = [
        (i * ny + j, ((i + dx) % nx) * ny + (j + dy) % ny) for i in range(nx) for j in range(ny)
    ]
    return lax.ppermute(x, ("lx", "ly"), pairs)


def swap(x):
    return lax.ppermute(x, "depth", [(0, 1), (1, 0)])


def local(iterate, right_side, storage, zones, counts, materials):
    levels = zones.shape[0]
    tile = (ROWS, LANES)
    tables = jnp.broadcast_to(
        materials.transpose(0, 2, 3, 1).reshape(32, ROWS, 1), (32, ROWS, LANES)
    )
    side = lax.axis_index("depth")
    near = (levels - 1) * (1 - side)
    next_near = near + 2 * side - 1
    near_codes = [
        jnp.where(
            z + side * levels < counts, lax.dynamic_index_in_dim(zones, z, 0, False) + 1, 0
        ).astype(F32)[None]
        for z in (near, next_near)
    ]
    plane = lax.dynamic_index_in_dim(iterate, near, 0, False)
    met = swap(jnp.concatenate([plane] + near_codes, axis=0))

    xm, ym, dm, codes = call(
        functools.partial(pack_kernel, levels),
        [((15, LINE, LANES), F32), ((10,) + tile, F32), ((10, 2, LANES), F32),
         ((levels + 2,) + tile, jnp.int32)],
        iterate, right_side, storage, zones, counts, met,
    )
    xm_in, ym_in, dm_in = around(xm, -1, 0), around(ym, 0, -1), around(dm, -1, -1)
    own, = call(
        functools.partial(own_kernel, levels),
        [((levels, SUMMED) + tile, F32)],
        iterate, codes, met, tables,
        scratch=[(levels + 2, SUMMED) + tile],
    )
    gains, rests, message, ends, codes_s = call(
        functools.partial(sweep_kernel, levels),
        [((levels, 16) + tile, F32), ((levels, 4) + tile, F32), ((54,) + tile, F32),
         ((14,) + tile, F32), ((levels + 2,) + tile, jnp.int32)],
        own, xm_in, ym_in, dm_in, iterate, right_side, storage, codes, met, tables,
        scratch=[
            (2 * SUMMED * LINE + 6 * LINE, LANES), (SUMMED,) + tile, (10,) + tile,
            (levels + 2, 4) + tile, (levels, 4) + tile, (levels,) + tile,
            (levels, 10) + tile, (levels + 1, 10) + tile, (levels, 4) + tile,
        ],
    )
    got = swap(message)
    xs, kx, x3, y3, d3 = call(
        functools.partial(back_kernel, levels),
        [((levels + 2, 4) + tile, F32), ((levels + 2, 4) + tile, F32),
         ((16, LINE, LANES), F32), ((8,) + tile, F32), ((8, 2, LANES), F32)],
        gains, rests, ends, got, codes_s, tables,
    )
    x3_in, y3_in, d3_in = around(x3, 1, 0), around(y3, 0, 1), around(d3, 1, 1)
    updated, coarse = call(
        functools.partial(finish_kernel, levels),
        [((levels, 4) + tile, F32), ((levels // 2, 4) + tile, F32)],
        xs, kx, x3_in, y3_in, d3_in, iterate, codes, tables,
        scratch=[
            (16 * LINE + 6 * LINE, LANES), (8,) + tile, (4,) + tile, (levels + 2, 4) + tile,
        ],
    )
    return updated, coarse


def solution(mesh):
    placed = (
        P("depth", None, "lx", "ly"),
        P("depth", None, "lx", "ly"),
        P("depth", "lx", "ly"),
        P("depth", "lx", "ly"),
        P("lx", "ly"),
        P(),
    )
    return jax.shard_map(
        local,
        mesh=mesh,
        in_specs=placed,
        out_specs=(P("depth", None, "lx", "ly"), P("depth", None, "lx", "ly")),
        check_vma=False,
    )
```

```python
import functools

import jax
import jax.numpy as jnp
from jax import lax
from jax.experimental import pallas as pl
from jax.experimental.pallas import tpu as pltpu
from jax.sharding import PartitionSpec as P

PAIRS = [(i, j) for i in range(4) for j in range(i, 4)]
AT = {}
for _k, (_i, _j) in enumerate(PAIRS):
    AT[_i, _j] = AT[_j, _i] = _k

ROWS, LANES = 8, 128
SUMMED = 19
PAD = 8
MESSAGE = 60
F32 = jnp.float32
VMEM_LIMIT = 48 * 1024 * 1024


def row_index():
    return lax.broadcasted_iota(jnp.int32, (ROWS, LANES), 0)


def lane_index():
    return lax.broadcasted_iota(jnp.int32, (ROWS, LANES), 1)


def roll_rows(x, by):
    return pltpu.roll(x, by % x.shape[0], 0)


def roll_lanes(x, by):
    return pltpu.roll(x, by % LANES if isinstance(by, int) else lax.rem(by + LANES, LANES), 1)


def activity(codes):
    return jnp.where(codes > 0, 1.0, 0.0).astype(F32)


def lookup(tables, kind, codes, act):
    rows = jnp.maximum(codes - 1, 0)
    found = []
    for i, j in PAIRS:
        table = tables[kind * 16 + 4 * i + j]
        parts = [
            jnp.take_along_axis(table, rows[at : at + ROWS], axis=0, mode="promise_in_bounds")
            for at in range(0, rows.shape[0], ROWS)
        ]
        value = parts[0] if len(parts) == 1 else jnp.concatenate(parts, axis=0)
        found.append(value * act)
    return found


def apply_sym(matrix, vector):
    out = []
    for i in range(4):
        total = matrix[AT[i, 0]] * vector[0]
        for j in range(1, 4):
            total = total + matrix[AT[i, j]] * vector[j]
        out.append(total)
    return out


def summed_fields(tables, codes, field):
    act = activity(codes)
    lateral = lookup(tables, 0, codes, act)
    return [act] + lateral + [act * v for v in field] + apply_sym(lateral, field)


def level_of(side, n, levels):
    return side * (levels - 1) + (1 - 2 * side) * n


def steps(first, last, body, width=1):
    passes = (last - first) // width

    def one(i, carry):
        for j in range(width):
            body(first + i * width + j)
        return carry

    lax.fori_loop(0, passes, one, 0)
    for n in range(first + passes * width, last):
        body(n)


def zero():
    return jnp.zeros((ROWS, LANES), F32)


def pack_kernel(
    levels, iterate, right, storage, zones, counts,
    it, rt, st, codes_out, xm, ym, dm, zones_v, counts_v, sems,
):
    side = lax.axis_index("depth")
    lane = lane_index()
    copies = [
        pltpu.make_async_copy(source, target, sems.at[k])
        for k, (source, target) in enumerate(
            [(zones, zones_v), (counts, counts_v), (iterate, it), (right, rt), (storage, st)]
        )
    ]
    for copy in copies:
        copy.start()
    for copy in copies:
        copy.wait()
    limit = counts_v[...] - side * levels
    acc = [zero() for _ in range(10)]
    for n in range(levels):
        z = level_of(side, n, levels)
        code = jnp.where(z < limit, zones_v[z] + 1, 0)
        codes_out[n] = code
        fields = [code.astype(F32)] + [it[z, c] for c in range(4)]
        fields += [rt[z, c] for c in range(4)] + [st[z]]
        for k, value in enumerate(fields):
            xm[k, n : n + 1, :] = value[0:1]
            if k < 5:
                xm[10 + k, n : n + 1, :] = value[1:2]
            acc[k] = jnp.where(lane // 2 == n, roll_lanes(value, 2 * n), acc[k])
    for k in range(10):
        ym[k] = acc[k]
        dm[k] = acc[k][0:2]


def own_kernel(levels, it, rt, st, codes, tables, sown, pre, u):
    side = lax.axis_index("depth")
    last_x = lax.axis_index("lx") == lax.axis_size("lx") - 1
    last_y = lax.axis_index("ly") == lax.axis_size("ly") - 1
    row, lane = row_index(), lane_index()
    wl = jnp.where(last_x & (row == 7), 0.0, 0.5).astype(F32)
    wu = jnp.where(row < 6, 0.5, 0.0).astype(F32)
    vl = jnp.where(last_y & (lane == 127), 0.0, 0.5).astype(F32)
    vu = jnp.where(lane < 127, 0.5, 0.0).astype(F32)
    for k in range(SUMMED):
        u[0, k] = zero()
        u[levels + 1, k] = zero()
        u[levels + 2, k] = zero()

    def fill(n):
        z = level_of(side, n, levels)
        field = [it[z, c] for c in range(4)]
        for k, value in enumerate(summed_fields(tables, codes[n], field)):
            u[n + 1, k] = value

    steps(0, levels, fill)

    def shift(n):
        z = level_of(side, n, levels)
        fields = [codes[n].astype(F32)] + [it[z, c] for c in range(4)]
        fields += [rt[z, c] for c in range(4)] + [st[z]]
        for k, value in enumerate(fields):
            pre[n, k] = roll_lanes(roll_rows(value, -1), -1)

    steps(0, levels, shift, 2)

    def gather(n):
        for k in range(SUMMED):
            w = u[n + 1, k] + 0.5 * (u[n, k] + u[n + 2, k])
            g = wl * w + wu * roll_rows(w, -2)
            b = jnp.where(row < 7, roll_rows(w, -1), 0.0) + g
            h = g + vu * roll_lanes(b, -1)
            sown[n, k] = jnp.where(lane < 127, roll_lanes(h, -1), 0.0) + vl * b

    steps(0, levels + 1, gather, 2)


def invert(m):
    d = lambda i, j: m[AT[i, j]]

    def small(a, b, c):
        ia = 1.0 / a
        l = b * ia
        ic = 1.0 / (c - l * b)
        lc = l * ic
        return ia + l * lc, -lc, ic

    a00, a01, a11 = small(d(0, 0), d(0, 1), d(1, 1))
    t00 = d(2, 0) * a00 + d(2, 1) * a01
    t01 = d(2, 0) * a01 + d(2, 1) * a11
    t10 = d(3, 0) * a00 + d(3, 1) * a01
    t11 = d(3, 0) * a01 + d(3, 1) * a11
    s00 = d(2, 2) - (t00 * d(2, 0) + t01 * d(2, 1))
    s01 = d(3, 2) - (t10 * d(2, 0) + t11 * d(2, 1))
    s11 = d(3, 3) - (t10 * d(3, 0) + t11 * d(3, 1))
    i22, i32, i33 = small(s00, s01, s11)
    u00 = i22 * t00 + i32 * t10
    u01 = i22 * t01 + i32 * t11
    u10 = i32 * t00 + i33 * t10
    u11 = i32 * t01 + i33 * t11
    i00 = a00 + (t00 * u00 + t10 * u10)
    i01 = a01 + (t00 * u01 + t10 * u11)
    i11 = a11 + (t01 * u01 + t11 * u11)
    return [i00, i01, -u00, -u10, i11, -u01, -u11, i22, i32, i33]


def sym_product(left, right):
    return [
        [
            (left[AT[i, 0]] * right[AT[0, j]] + left[AT[i, 1]] * right[AT[1, j]])
            + (left[AT[i, 2]] * right[AT[2, j]] + left[AT[i, 3]] * right[AT[3, j]])
            for j in range(4)
        ]
        for i in range(4)
    ]


def back_product(link, gain):
    return [
        (link[AT[i, 0]] * gain[0][j] + link[AT[i, 1]] * gain[1][j])
        + (link[AT[i, 2]] * gain[2][j] + link[AT[i, 3]] * gain[3][j])
        for i, j in PAIRS
    ]


def line_sum(values):
    return values + 0.5 * (roll_rows(values, 1) + roll_rows(values, -1))


def lane_sum(values):
    return values + 0.5 * (roll_lanes(values, 2) + roll_lanes(values, -2))


def lengthen(values, rows):
    return jnp.concatenate([values, jnp.zeros((rows - values.shape[0], LANES), F32)], axis=0)


def sweep_kernel(
    levels, sown, pre, xm, ym, dm, codes, tables,
    gains, rests, message, codes_s,
    xw, xl, yv, ys, fs, rs, ss, ps, ms, qs,
):
    line = levels + PAD
    last_x = lax.axis_index("lx") == lax.axis_size("lx") - 1
    last_y = lax.axis_index("ly") == lax.axis_size("ly") - 1
    row, lane = row_index(), lane_index()
    wl = jnp.where(last_x & (row == 7), 0.0, 0.5).astype(F32)
    wu = jnp.where(last_x & (row == 6), 0.0, 0.5).astype(F32)
    wu6 = jnp.where(last_x, 0.0, 0.5).astype(F32)
    vu127 = jnp.where(last_y, 0.0, 0.5).astype(F32)
    top = row == 7
    end = lane == 127

    line_lane = lax.broadcasted_iota(jnp.int32, (line, LANES), 1)
    line_vl = jnp.where(last_y & (line_lane == 127), 0.0, 0.5).astype(F32)
    line_vu = jnp.where(line_lane < 127, 0.5, 0.0).astype(F32)
    lines = []
    for r in range(2):
        line_codes = lengthen(xm[10 * r], line).astype(jnp.int32)
        line_field = [lengthen(xm[10 * r + 1 + c], line) for c in range(4)]
        lines.append(summed_fields(tables, line_codes, line_field))
    for k in range(SUMMED):
        x8, x9 = line_sum(lines[0][k]), line_sum(lines[1][k])
        g6, g7 = wu6 * x8, 0.5 * x9
        for r, (g, b) in enumerate(((g6, g6), (g7, x8 + g7))):
            h = g + line_vu * roll_lanes(b, -1)
            at = (2 * k + r + 6) * line
            xw[at : at + line, :] = jnp.where(line_lane < 127, roll_lanes(h, -1), 0.0) + line_vl * b
    for k in range(10):
        xl[k] = roll_lanes(xm[k], -1)

    corner = [lengthen(dm[k], ROWS) for k in range(10)]
    side_u = summed_fields(tables, ym[0].astype(jnp.int32), [ym[1 + c] for c in range(4)])
    corner_u = summed_fields(tables, corner[0].astype(jnp.int32), corner[1:5])
    for k in range(SUMMED):
        w0 = lane_sum(side_u[k])
        wd = lane_sum(corner_u[k])
        w1 = roll_rows(jnp.where(row < 1, wd, w0), -1)
        w2 = roll_rows(jnp.where(row < 2, wd, w0), -2)
        g = wl * w0 + wu * w2
        b = w1 + g
        h = g + 0.5 * roll_lanes(b, -1)
        yv[k] = jnp.where(lane % 2 == 0, vu127 * b, roll_lanes(h, 1))
    for k in range(10):
        ys[k] = roll_rows(jnp.where(row < 1, corner[k], ym[k]), -1)

    def shift_level(n):
        moved = []
        for k in range(10):
            value = jnp.where(top, xl[k, pl.ds(n, 1), :], pre[n, k])
            moved.append(jnp.where(end, roll_lanes(ys[k], 127 - 2 * n), value))
        codes_s[n] = moved[0].astype(jnp.int32)
        for c in range(4):
            fs[n + 1, c] = moved[1 + c]
            rs[n, c] = moved[5 + c]
        ss[n] = moved[9]

    steps(0, levels, shift_level, 2)
    for c in range(4):
        fs[0, c] = zero()
        fs[levels + 1, c] = zero()
    for k in range(10):
        ms[0, k] = zero()

    def lateral_sums(n):
        sums = []
        for k in range(SUMMED):
            beyond = xw[pl.ds(2 * k * line + n, ROWS, stride=line), :]
            value = sown[n, k] + jnp.where(row >= 6, beyond, 0.0)
            sums.append(value + jnp.where(lane >= 126, roll_lanes(yv[k], 126 - 2 * n), 0.0))
        return sums

    def assemble(n, last=False):
        sums = lateral_sums(n)
        act = activity(codes_s[n])
        half = 0.5 * act
        lateral = lookup(tables, 0, codes_s[n], half)
        below = [ms[n, k] for k in range(10)]
        if last:
            above = [zero() for _ in range(10)]
        else:
            both = half * activity(codes_s[n + 1])
            here = lookup(tables, 1, codes_s[n], both)
            there = lookup(tables, 1, codes_s[n + 1], both)
            above = [here[k] + there[k] for k in range(10)]
        block = []
        for k, (i, j) in enumerate(PAIRS):
            value = (lateral[k] * sums[0] + half * sums[1 + k]) + (below[k] + above[k])
            block.append(value + ss[n] if i == j else value)
        for k in range(10):
            ms[n + 1, k] = above[k]
            ps[n, k] = block[k]
        field = [fs[n + 1, c] for c in range(4)]
        before = apply_sym(below, [fs[n, c] for c in range(4)])
        after = apply_sym(above, [fs[n + 2, c] for c in range(4)])
        diagonal = apply_sym(block, field)
        flow = apply_sym(lateral, sums[11:15])
        for c in range(4):
            near = (before[c] + after[c]) + (flow[c] + half * sums[15 + c])
            qs[n, c] = act * (rs[n, c] - (diagonal[c] - near))

    steps(0, levels - 1, assemble, 2)
    assemble(levels - 1, True)

    def eliminate(n, carry):
        coupled, carried = carry
        inverse = invert([ps[n, k] - coupled[k] for k in range(10)])
        value = [qs[n, c] + carried[c] for c in range(4)]
        link = [ms[n + 1, k] for k in range(10)]
        gain = sym_product(inverse, link)
        rest = apply_sym(inverse, value)
        for i in range(4):
            rests[n, i] = rest[i]
            for j in range(4):
                gains[n, 4 * i + j] = gain[i][j]
        return back_product(link, gain), apply_sym(link, rest)

    zeros = [zero() for _ in range(10)]
    coupled, carried = lax.fori_loop(0, levels - 1, eliminate, (zeros, zeros[:4]))
    end_n = levels - 1
    for k in range(10):
        message[k] = ps[end_n, k] - coupled[k]
    for c in range(4):
        message[10 + c] = qs[end_n, c] + carried[c]
        message[33 + c] = fs[levels, c]
        message[56 + c] = rests[end_n - 1, c]
    for k, value in enumerate(lateral_sums(levels)):
        message[14 + k] = value
    message[37] = codes_s[end_n].astype(F32)
    message[38] = codes_s[end_n - 1].astype(F32)
    message[39] = codes[end_n].astype(F32)
    for k in range(16):
        message[40 + k] = gains[end_n - 1, k]


def back_kernel(levels, gains, rests, message, got, codes_s, tables, xs, kx, x3, y3, d3):
    lane = lane_index()
    planes = levels + 2

    def carry_on(gain, rest, x):
        out = []
        for i in range(4):
            out.append(
                rest[i] + ((gain[4 * i] * x[0] + gain[4 * i + 1] * x[1])
                           + (gain[4 * i + 2] * x[2] + gain[4 * i + 3] * x[3]))
            )
        return out

    def end_of(ref):
        code = ref[37].astype(jnp.int32)
        act = activity(code)
        part = lambda at, count: [ref[at + k] for k in range(count)]
        return code, act, part(0, 10), part(10, 4), part(14, SUMMED), part(33, 4)

    here, there = end_of(message), end_of(got)
    both = 0.5 * here[1] * there[1]
    link_here = lookup(tables, 1, here[0], both)
    link_there = lookup(tables, 1, there[0], both)
    link = [link_here[k] + link_there[k] for k in range(10)]

    def complete(one, other):
        code, act, block, value, _, field = one
        _, _, _, _, sums, field_there = other
        half = 0.5 * act
        lateral = lookup(tables, 0, code, half)
        added = [lateral[k] * sums[0] + half * sums[1 + k] + link[k] for k in range(10)]
        across = apply_sym(link, field_there)
        flow = apply_sym(lateral, sums[11:15])
        diagonal = apply_sym(added, field)
        full = [
            value[c] + act * ((across[c] + flow[c] + half * sums[15 + c]) - diagonal[c])
            for c in range(4)
        ]
        return [block[k] + added[k] for k in range(10)], full

    block, value = complete(here, there)
    block_there, value_there = complete(there, here)
    inverse = invert(block_there)
    gain = sym_product(inverse, link)
    rest = apply_sym(inverse, value_there)
    coupled, carried = back_product(link, gain), apply_sym(link, rest)
    x = apply_sym(
        invert([block[k] - coupled[k] for k in range(10)]),
        [value[c] + carried[c] for c in range(4)],
    )
    x_met = carry_on([gain[i][j] for i in range(4) for j in range(4)], rest, x)
    x_far = carry_on([got[40 + k] for k in range(16)], [got[56 + c] for c in range(4)], x_met)
    for c in range(4):
        xs[levels - 1, c] = x[c]
        xs[levels, c] = x_met[c]
        xs[levels + 1, c] = x_far[c]

    def retreat(step, x):
        n = levels - 2 - step
        x = carry_on([gains[n, k] for k in range(16)], [rests[n, c] for c in range(4)], x)
        for c in range(4):
            xs[n, c] = x[c]
        return x

    lax.fori_loop(0, levels - 1, retreat, x)

    acc = [zero() for _ in range(8)]
    for n in range(planes):
        field = [xs[n, c] for c in range(4)]
        code = codes_s[n] if n < levels else got[37 + n - levels].astype(jnp.int32)
        flow = apply_sym(lookup(tables, 0, code, activity(code)), field)
        for c in range(4):
            kx[n, c] = flow[c]
        for k, value in enumerate(field + flow):
            for r in range(2):
                at = (2 * k + r) * planes + n
                x3[at : at + 1, :] = value[6 + r : 7 + r]
            acc[k] = jnp.where(lane // 2 == n, roll_lanes(value, 2 * n + 2), acc[k])
    for k in range(8):
        y3[k] = acc[k]
        d3[k] = acc[k][6:8]


def own_back_kernel(levels, xs, kx, sown, pre):
    last_x = lax.axis_index("lx") == lax.axis_size("lx") - 1
    last_y = lax.axis_index("ly") == lax.axis_size("ly") - 1
    row, lane = row_index(), lane_index()
    wl = jnp.where(row >= 2, 0.5, 0.0).astype(F32)
    wu = jnp.where(last_x & (row == 7), 0.0, 0.5).astype(F32)
    vl = jnp.where(lane >= 1, 0.5, 0.0).astype(F32)
    vu = jnp.where(last_y & (lane == 127), 0.0, 0.5).astype(F32)

    def gather(n, first=False):
        for k in range(8):
            ref, c = (xs, k) if k < 4 else (kx, k - 4)
            outer = ref[n + 1, c] if first else ref[n - 1, c] + ref[n + 1, c]
            w = ref[n, c] + 0.5 * outer
            g = wl * roll_rows(w, 2) + wu * w
            b = jnp.where(row >= 1, roll_rows(w, 1), 0.0) + g
            h = g + vl * roll_lanes(b, 1)
            sown[n, k] = jnp.where(lane >= 1, roll_lanes(h, 1), 0.0) + vu * b

    gather(0, True)
    steps(1, levels + 1, gather, 2)

    def shift(n):
        for c in range(4):
            pre[n, c] = roll_lanes(roll_rows(xs[n, c], 1), 1)

    steps(0, levels, shift, 4)


def finish_kernel(
    levels, sown, pre, x3, y3, d3, it, codes, got, tables,
    updated, coarse, xw, xl, yv, ys, sm, up, co, sems,
):
    line = levels + PAD
    planes = levels + 2
    side = lax.axis_index("depth")
    first_x = lax.axis_index("lx") == 0
    first_y = lax.axis_index("ly") == 0
    last_x = lax.axis_index("lx") == lax.axis_size("lx") - 1
    last_y = lax.axis_index("ly") == lax.axis_size("ly") - 1
    row, lane = row_index(), lane_index()
    wl = jnp.where(first_x & (row == 0), 0.0, 0.5).astype(F32)
    wu = jnp.where(last_x & (row == 7), 0.0, 0.5).astype(F32)
    wl0 = jnp.where(first_x, 0.0, 0.5).astype(F32)
    vl0 = jnp.where(first_y, 0.0, 0.5).astype(F32)
    line_lane = lax.broadcasted_iota(jnp.int32, (line, LANES), 1)
    line_vu = jnp.where(last_y & (line_lane == 127), 0.0, 0.5).astype(F32)
    line_vl = jnp.where(line_lane >= 1, 0.5, 0.0).astype(F32)

    corner = [lengthen(d3[k], ROWS) for k in range(8)]
    for c in range(4):
        last_row = lengthen(x3[(2 * c + 1) * planes : (2 * c + 2) * planes, :], line)
        xl[c] = roll_lanes(last_row, 1)
        ys[c] = jnp.where(row < 1, roll_rows(corner[c], -1), roll_rows(y3[c], 1))

    def place(n):
        z = level_of(side, n, levels)
        for c in range(4):
            x = jnp.where(row < 1, xl[c, pl.ds(n, 1), :], pre[n, c])
            x = jnp.where(lane < 1, roll_lanes(ys[c], -2 * n - 1), x)
            up[z, c] = it[z, c] + x

    steps(0, levels, place, 4)
    send_updated = pltpu.make_async_copy(up, updated, sems.at[0])
    send_updated.start()

    for k in range(8):
        far, near = [
            line_sum(lengthen(x3[(2 * k + r) * planes : (2 * k + r + 1) * planes, :], line))
            for r in range(2)
        ]
        g0, g1 = wl0 * far, 0.5 * near
        for r, (g, b) in enumerate(((g0, near + g0), (g1, g1))):
            h = g + line_vl * roll_lanes(b, 1)
            at = (2 * k + r) * line
            xw[at : at + line, :] = jnp.where(line_lane >= 1, roll_lanes(h, 1), 0.0) + line_vu * b
        w2 = lane_sum(y3[k])
        wd = lane_sum(corner[k])
        w0 = jnp.where(row < 2, wd, roll_rows(w2, 2))
        w1 = jnp.where(row < 1, roll_rows(wd, -1), roll_rows(w2, 1))
        g = wl * w0 + wu * w2
        b = w1 + g
        h = g + vl0 * roll_lanes(b, 1)
        yv[k] = jnp.where(lane % 2 == 0, roll_lanes(h, -1), 0.5 * b)

    def smooth(n, code):
        sums = []
        for k in range(8):
            beyond = xw[pl.ds(2 * k * line + n, ROWS, stride=line), :]
            value = sown[n, k] + jnp.where(row < 2, beyond, 0.0)
            sums.append(value + jnp.where(lane < 2, roll_lanes(yv[k], -2 * n), 0.0))
        half = 0.5 * activity(code)
        flow = apply_sym(lookup(tables, 0, code, half), sums[:4])
        for c in range(4):
            sm[n + 1, c] = flow[c] + half * sums[4 + c]

    for c in range(4):
        sm[0, c] = zero()
    steps(0, levels, lambda n: smooth(n, codes[n]), 4)
    smooth(levels, got[39].astype(jnp.int32))

    step = 1 - 2 * side
    for k in range(levels // 2):
        at = side * (levels + 1) + step * 2 * k
        for c in range(4):
            co[k, c] = sm[at + step, c] + 0.5 * (sm[at, c] + sm[at + 2 * step, c])
    send_coarse = pltpu.make_async_copy(co, coarse, sems.at[1])
    send_coarse.start()
    send_updated.wait()
    send_coarse.wait()


def call(kernel, outs, *args, scratch=(), far_in=False, far_out=False):
    vmem = pl.BlockSpec(memory_space=pltpu.VMEM)
    if far_in:
        args = [pltpu.with_memory_space_constraint(x, pltpu.HBM) for x in args]
    far = pl.BlockSpec(memory_space=pltpu.HBM)
    return pl.pallas_call(
        kernel,
        out_shape=[jax.ShapeDtypeStruct(s, t) for s, t in outs],
        in_specs=[far if far_in else vmem] * len(args),
        out_specs=[far if far_out else vmem] * len(outs),
        scratch_shapes=list(scratch),
        compiler_params=pltpu.CompilerParams(vmem_limit_bytes=VMEM_LIMIT),
    )(*args)


def around(x, dx, dy):
    nx, ny = lax.axis_size("lx"), lax.axis_size("ly")
    pairs = [
        (i * ny + j, ((i + dx) % nx) * ny + (j + dy) % ny) for i in range(nx) for j in range(ny)
    ]
    return lax.ppermute(x, ("lx", "ly"), pairs)


def swap(x):
    return lax.ppermute(x, "depth", [(0, 1), (1, 0)])


def local(iterate, right_side, storage, zones, counts, materials):
    levels = zones.shape[0]
    line, planes = levels + PAD, levels + 2
    tile = (ROWS, LANES)
    vmem = lambda *shape: pltpu.VMEM(shape, F32)
    tables = jnp.broadcast_to(
        materials.transpose(0, 2, 3, 1).reshape(32, ROWS, 1), (32, ROWS, LANES)
    )
    it, rt, st, codes, xm, ym, dm = call(
        functools.partial(pack_kernel, levels),
        [((levels, 4) + tile, F32), ((levels, 4) + tile, F32), ((levels,) + tile, F32),
         ((levels,) + tile, jnp.int32),
         ((15, levels, LANES), F32), ((10,) + tile, F32), ((10, 2, LANES), F32)],
        iterate, right_side, storage, zones, counts,
        scratch=[
            pltpu.VMEM((levels,) + tile, jnp.int32), pltpu.VMEM(tile, jnp.int32),
            pltpu.SemaphoreType.DMA((5,)),
        ],
        far_in=True,
    )
    xm_in, ym_in, dm_in = around(xm, -1, 0), around(ym, 0, -1), around(dm, -1, -1)
    sown, pre = call(
        functools.partial(own_kernel, levels),
        [((levels + 1, SUMMED) + tile, F32), ((levels, 10) + tile, F32)],
        it, rt, st, codes, tables,
        scratch=[vmem(levels + 3, SUMMED, *tile)],
    )
    gains, rests, message, codes_s = call(
        functools.partial(sweep_kernel, levels),
        [((levels - 1, 16) + tile, F32), ((levels - 1, 4) + tile, F32), ((MESSAGE,) + tile, F32),
         ((levels,) + tile, jnp.int32)],
        sown, pre, xm_in, ym_in, dm_in, codes, tables,
        scratch=[
            vmem((2 * SUMMED + 12) * line, LANES), vmem(10, levels, LANES),
            vmem(SUMMED, *tile), vmem(10, *tile),
            vmem(planes, 4, *tile), vmem(levels, 4, *tile), vmem(levels, *tile),
            vmem(levels, 10, *tile), vmem(levels + 1, 10, *tile), vmem(levels, 4, *tile),
        ],
    )
    got = swap(message)
    xs, kx, x3, y3, d3 = call(
        functools.partial(back_kernel, levels),
        [((planes, 4) + tile, F32), ((planes, 4) + tile, F32),
         ((16 * planes, LANES), F32), ((8,) + tile, F32), ((8, 2, LANES), F32)],
        gains, rests, message, got, codes_s, tables,
    )
    x3_in, y3_in, d3_in = around(x3, 1, 0), around(y3, 0, 1), around(d3, 1, 1)
    sown3, pre3 = call(
        functools.partial(own_back_kernel, levels),
        [((levels + 1, 8) + tile, F32), ((levels, 4) + tile, F32)],
        xs, kx,
    )
    updated, coarse = call(
        functools.partial(finish_kernel, levels),
        [((levels, 4) + tile, F32), ((levels // 2, 4) + tile, F32)],
        sown3, pre3, x3_in, y3_in, d3_in, it, codes, got, tables,
        scratch=[
            vmem((16 + 6) * line, LANES), vmem(4, line, LANES), vmem(8, *tile), vmem(4, *tile),
            vmem(levels + 2, 4, *tile), vmem(levels, 4, *tile), vmem(levels // 2, 4, *tile),
            pltpu.SemaphoreType.DMA((2,)),
        ],
        far_out=True,
    )
    return updated, coarse


def solution(mesh):
    placed = (
        P("depth", None, "lx", "ly"),
        P("depth", None, "lx", "ly"),
        P("depth", "lx", "ly"),
        P("depth", "lx", "ly"),
        P("lx", "ly"),
        P(),
    )
    return jax.shard_map(
        local,
        mesh=mesh,
        in_specs=placed,
        out_specs=(P("depth", None, "lx", "ly"), P("depth", None, "lx", "ly")),
        check_vma=False,
    )
```

```python
import functools

import jax
import jax.numpy as jnp
from jax import lax
from jax.experimental import pallas as pl
from jax.experimental.pallas import tpu as pltpu
from jax.sharding import PartitionSpec as P

PAIRS = [(i, j) for i in range(4) for j in range(i, 4)]
AT = {}
for _k, (_i, _j) in enumerate(PAIRS):
    AT[_i, _j] = AT[_j, _i] = _k

ROWS, LANES = 8, 128
SUMMED = 19
PAD = 8
MESSAGE = 60
F32 = jnp.float32
VMEM_LIMIT = 48 * 1024 * 1024


def row_index():
    return lax.broadcasted_iota(jnp.int32, (ROWS, LANES), 0)


def lane_index():
    return lax.broadcasted_iota(jnp.int32, (ROWS, LANES), 1)


def roll_rows(x, by):
    return pltpu.roll(x, by % x.shape[0], 0)


def roll_lanes(x, by):
    return pltpu.roll(x, by % LANES if isinstance(by, int) else lax.rem(by + LANES, LANES), 1)


def activity(codes):
    return jnp.where(codes > 0, 1.0, 0.0).astype(F32)


def lookup(tables, kind, codes):
    rows = jnp.maximum(codes - 1, 0)
    found = []
    for i, j in PAIRS:
        table = tables[kind * 16 + 4 * i + j]
        parts = [
            jnp.take_along_axis(table, rows[at : at + ROWS], axis=0, mode="promise_in_bounds")
            for at in range(0, rows.shape[0], ROWS)
        ]
        found.append(parts[0] if len(parts) == 1 else jnp.concatenate(parts, axis=0))
    return found


def apply_sym(matrix, vector):
    out = []
    for i in range(4):
        total = matrix[AT[i, 0]] * vector[0]
        for j in range(1, 4):
            total = total + matrix[AT[i, j]] * vector[j]
        out.append(total)
    return out


def summed_fields(tables, codes, field):
    act = activity(codes)
    lateral = [act * value for value in lookup(tables, 0, codes)]
    return [act] + lateral + [act * v for v in field] + apply_sym(lateral, field)


def level_of(side, n, levels):
    return side * (levels - 1) + (1 - 2 * side) * n


def steps(first, last, body, width=1):
    passes = (last - first) // width

    def one(i, carry):
        for j in range(width):
            body(first + i * width + j)
        return carry

    lax.fori_loop(0, passes, one, 0)
    for n in range(first + passes * width, last):
        body(n)


def zero():
    return jnp.zeros((ROWS, LANES), F32)


def pack_kernel(
    levels, iterate, right, storage, zones, counts,
    it, rt, st, codes_out, xm, ym, dm, zones_v, counts_v, sems,
):
    side = lax.axis_index("depth")
    lane = lane_index()
    copies = [
        pltpu.make_async_copy(source, target, sems.at[k])
        for k, (source, target) in enumerate(
            [(zones, zones_v), (counts, counts_v), (iterate, it), (right, rt), (storage, st)]
        )
    ]
    for copy in copies:
        copy.start()
    for copy in copies:
        copy.wait()
    limit = counts_v[...] - side * levels
    acc = [zero() for _ in range(10)]
    for n in range(levels):
        z = level_of(side, n, levels)
        code = jnp.where(z < limit, zones_v[z] + 1, 0)
        codes_out[n] = code
        fields = [code.astype(F32)] + [it[z, c] for c in range(4)]
        fields += [rt[z, c] for c in range(4)] + [st[z]]
        for k, value in enumerate(fields):
            xm[k, n : n + 1, :] = value[0:1]
            if k < 5:
                xm[10 + k, n : n + 1, :] = value[1:2]
            acc[k] = jnp.where(lane // 2 == n, roll_lanes(value, 2 * n), acc[k])
    for k in range(10):
        ym[k] = acc[k]
        dm[k] = acc[k][0:2]


def own_kernel(levels, it, rt, st, codes, tables, sown, pre, u):
    side = lax.axis_index("depth")
    last_x = lax.axis_index("lx") == lax.axis_size("lx") - 1
    last_y = lax.axis_index("ly") == lax.axis_size("ly") - 1
    row, lane = row_index(), lane_index()
    wl = jnp.where(last_x & (row == 7), 0.0, 0.5).astype(F32)
    wu = jnp.where(row < 6, 0.5, 0.0).astype(F32)
    vl = jnp.where(last_y & (lane == 127), 0.0, 0.5).astype(F32)
    vu = jnp.where(lane < 126, 0.5, 0.0).astype(F32)
    for k in range(SUMMED):
        u[0, k] = zero()
        u[levels + 1, k] = zero()
        u[levels + 2, k] = zero()

    def fill(n):
        z = level_of(side, n, levels)
        field = [it[z, c] for c in range(4)]
        for k, value in enumerate(summed_fields(tables, codes[n], field)):
            u[n + 1, k] = value

    steps(0, levels, fill)

    def shift(n):
        z = level_of(side, n, levels)
        fields = [codes[n].astype(F32)] + [it[z, c] for c in range(4)]
        fields += [rt[z, c] for c in range(4)] + [st[z]]
        for k, value in enumerate(fields):
            pre[n, k] = roll_lanes(roll_rows(value, -1), -1)

    steps(0, levels, shift, 2)

    def gather(n):
        for k in range(SUMMED):
            w = u[n + 1, k] + 0.5 * (u[n, k] + u[n + 2, k])
            g = wl * w + wu * roll_rows(w, -2)
            b = jnp.where(row < 7, roll_rows(w, -1), 0.0) + g
            sown[n, k] = jnp.where(lane < 127, roll_lanes(g, -1), 0.0) + (vu * roll_lanes(b, -2) + vl * b)

    steps(0, levels + 1, gather, 2)


def invert(m):
    d = lambda i, j: m[AT[i, j]]

    def small(a, b, c):
        ia = 1.0 / a
        l = b * ia
        ic = 1.0 / (c - l * b)
        lc = l * ic
        return ia + l * lc, -lc, ic

    a00, a01, a11 = small(d(0, 0), d(0, 1), d(1, 1))
    t00 = d(2, 0) * a00 + d(2, 1) * a01
    t01 = d(2, 0) * a01 + d(2, 1) * a11
    t10 = d(3, 0) * a00 + d(3, 1) * a01
    t11 = d(3, 0) * a01 + d(3, 1) * a11
    s00 = d(2, 2) - (t00 * d(2, 0) + t01 * d(2, 1))
    s01 = d(3, 2) - (t10 * d(2, 0) + t11 * d(2, 1))
    s11 = d(3, 3) - (t10 * d(3, 0) + t11 * d(3, 1))
    i22, i32, i33 = small(s00, s01, s11)
    u00 = i22 * t00 + i32 * t10
    u01 = i22 * t01 + i32 * t11
    u10 = i32 * t00 + i33 * t10
    u11 = i32 * t01 + i33 * t11
    i00 = a00 + (t00 * u00 + t10 * u10)
    i01 = a01 + (t00 * u01 + t10 * u11)
    i11 = a11 + (t01 * u01 + t11 * u11)
    return [i00, i01, -u00, -u10, i11, -u01, -u11, i22, i32, i33]


def sym_product(left, right):
    return [
        [
            (left[AT[i, 0]] * right[AT[0, j]] + left[AT[i, 1]] * right[AT[1, j]])
            + (left[AT[i, 2]] * right[AT[2, j]] + left[AT[i, 3]] * right[AT[3, j]])
            for j in range(4)
        ]
        for i in range(4)
    ]


def back_product(link, gain):
    return [
        (link[AT[i, 0]] * gain[0][j] + link[AT[i, 1]] * gain[1][j])
        + (link[AT[i, 2]] * gain[2][j] + link[AT[i, 3]] * gain[3][j])
        for i, j in PAIRS
    ]


def line_sum(values):
    return values + 0.5 * (roll_rows(values, 1) + roll_rows(values, -1))


def lane_sum(values):
    return values + 0.5 * (roll_lanes(values, 2) + roll_lanes(values, -2))


def lengthen(values, rows):
    return jnp.concatenate([values, jnp.zeros((rows - values.shape[0], LANES), F32)], axis=0)


def line_kernel(levels, sown, pre, xm, tables, sums, moved, xw, xl):
    line = levels + PAD
    last_x = lax.axis_index("lx") == lax.axis_size("lx") - 1
    last_y = lax.axis_index("ly") == lax.axis_size("ly") - 1
    row = row_index()
    wu6 = jnp.where(last_x, 0.0, 0.5).astype(F32)
    lane = lax.broadcasted_iota(jnp.int32, (line, LANES), 1)
    vl = jnp.where(last_y & (lane == 127), 0.0, 0.5).astype(F32)
    vu = jnp.where(lane < 126, 0.5, 0.0).astype(F32)
    lines = []
    for r in range(2):
        codes = lengthen(xm[10 * r], line).astype(jnp.int32)
        lines.append(summed_fields(tables, codes, [lengthen(xm[10 * r + 1 + c], line) for c in range(4)]))
    for k in range(SUMMED):
        x8, x9 = line_sum(lines[0][k]), line_sum(lines[1][k])
        g6, g7 = wu6 * x8, 0.5 * x9
        for r, (g, b) in enumerate(((g6, g6), (g7, x8 + g7))):
            at = (2 * k + r + 6) * line
            xw[at : at + line, :] = jnp.where(lane < 127, roll_lanes(g, -1), 0.0) + (
                vu * roll_lanes(b, -2) + vl * b
            )
    for k in range(10):
        xl[k] = roll_lanes(xm[k], -1)

    def add(n):
        for k in range(SUMMED):
            beyond = xw[pl.ds(2 * k * line + n, ROWS, stride=line), :]
            sums[n, k] = sown[n, k] + jnp.where(row >= 6, beyond, 0.0)

    def fill(n):
        for k in range(10):
            moved[n, k] = jnp.where(row == 7, xl[k, pl.ds(n, 1), :], pre[n, k])

    steps(0, levels + 1, add, 2)
    steps(0, levels, fill, 2)


def sweep_kernel(
    levels, sown, pre, ym, dm, codes, tables,
    gains, rests, message, codes_s,
    yv, ys, fs, rs, ss, ps, ms, qs,
):
    last_x = lax.axis_index("lx") == lax.axis_size("lx") - 1
    last_y = lax.axis_index("ly") == lax.axis_size("ly") - 1
    row, lane = row_index(), lane_index()
    wl = jnp.where(last_x & (row == 7), 0.0, 0.5).astype(F32)
    wu = jnp.where(last_x & (row == 6), 0.0, 0.5).astype(F32)
    vu127 = jnp.where(last_y, 0.0, 0.5).astype(F32)
    even = lane % 2 == 0
    end = lane == 127

    corner = [lengthen(dm[k], ROWS) for k in range(10)]
    for k in range(10):
        ys[k] = roll_rows(jnp.where(row < 1, corner[k], ym[k]), -1)
    side_u = summed_fields(tables, ym[0].astype(jnp.int32), [ym[1 + c] for c in range(4)])
    corner_u = summed_fields(tables, corner[0].astype(jnp.int32), corner[1:5])
    for k in range(SUMMED):
        one = roll_rows(jnp.where(row < 1, corner_u[k], side_u[k]), -1)
        two = roll_rows(jnp.where(row < 2, corner_u[k], side_u[k]), -2)
        g = wl * side_u[k] + wu * two
        b = one + g
        yv[k] = lane_sum(jnp.where(even, vu127 * b, roll_lanes(g, 1) + 0.5 * b))

    def shift(n):
        moved = [jnp.where(end, roll_lanes(ys[k], 127 - 2 * n), pre[n, k]) for k in range(10)]
        codes_s[n] = moved[0].astype(jnp.int32)
        for c in range(4):
            fs[n + 1, c] = moved[1 + c]
            rs[n, c] = moved[5 + c]
        ss[n] = moved[9]

    for c in range(4):
        fs[0, c] = zero()
        fs[levels + 1, c] = zero()
    for k in range(10):
        ms[0, k] = zero()

    def lateral_sums(n):
        return [
            sown[n, k] + jnp.where(lane >= 126, roll_lanes(yv[k], 126 - 2 * n), 0.0)
            for k in range(SUMMED)
        ]

    def assemble(n, last=False):
        sums = lateral_sums(n)
        act = activity(codes_s[n])
        half = 0.5 * act
        lateral = lookup(tables, 0, codes_s[n])
        below = [ms[n, k] for k in range(10)]
        if last:
            above = [zero() for _ in range(10)]
        else:
            both = half * activity(codes_s[n + 1])
            here = lookup(tables, 1, codes_s[n])
            there = lookup(tables, 1, codes_s[n + 1])
            above = [both * (here[k] + there[k]) for k in range(10)]
        block = []
        for k, (i, j) in enumerate(PAIRS):
            value = half * (lateral[k] * sums[0] + sums[1 + k]) + (below[k] + above[k])
            block.append(value + ss[n] if i == j else value)
        field = [fs[n + 1, c] for c in range(4)]
        before = apply_sym(below, [fs[n, c] for c in range(4)])
        after = apply_sym(above, [fs[n + 2, c] for c in range(4)])
        diagonal = apply_sym(block, field)
        flow = apply_sym(lateral, sums[11:15])
        for k in range(10):
            ms[n + 1, k] = above[k]
            ps[n, k] = block[k]
        for c in range(4):
            near = (before[c] + after[c]) + half * (flow[c] + sums[15 + c])
            qs[n, c] = act * (rs[n, c] - (diagonal[c] - near))

    def eliminate(n, carry):
        coupled, carried = carry
        block = [ps[n, k] for k in range(10)]
        link = [ms[n + 1, k] for k in range(10)]
        value = [qs[n, c] + carried[c] for c in range(4)]
        inverse = invert([block[k] - coupled[k] for k in range(10)])
        gain = sym_product(inverse, link)
        rest = apply_sym(inverse, value)
        for i in range(4):
            rests[n, i] = rest[i]
            for j in range(4):
                gains[n, 4 * i + j] = gain[i][j]
        return back_product(link, gain), apply_sym(link, rest)

    shift(0)
    shift(1)
    shift(2)
    assemble(0)

    def advance(n, carry):
        carry = eliminate(n, carry)
        assemble(n + 1)
        shift(n + 3)
        return carry

    zeros = [zero() for _ in range(10)]
    carry = lax.fori_loop(0, levels - 3, advance, (zeros, zeros[:4]))
    carry = eliminate(levels - 3, carry)
    assemble(levels - 2)
    carry = eliminate(levels - 2, carry)
    assemble(levels - 1, True)
    coupled, carried = carry
    end_n = levels - 1
    for k in range(10):
        message[k] = ps[end_n, k] - coupled[k]
    for c in range(4):
        message[10 + c] = qs[end_n, c] + carried[c]
        message[33 + c] = fs[levels, c]
        message[56 + c] = rests[end_n - 1, c]
    for k, value in enumerate(lateral_sums(levels)):
        message[14 + k] = value
    message[37] = codes_s[end_n].astype(F32)
    message[38] = codes_s[end_n - 1].astype(F32)
    message[39] = codes[end_n].astype(F32)
    for k in range(16):
        message[40 + k] = gains[end_n - 1, k]


def back_kernel(levels, gains, rests, message, got, codes_s, tables, xs, kx, x3, y3, d3):
    lane = lane_index()
    planes = levels + 2

    def carry_on(gain, rest, x):
        out = []
        for i in range(4):
            out.append(
                rest[i] + ((gain[4 * i] * x[0] + gain[4 * i + 1] * x[1])
                           + (gain[4 * i + 2] * x[2] + gain[4 * i + 3] * x[3]))
            )
        return out

    def end_of(ref):
        code = ref[37].astype(jnp.int32)
        act = activity(code)
        part = lambda at, count: [ref[at + k] for k in range(count)]
        return code, act, part(0, 10), part(10, 4), part(14, SUMMED), part(33, 4)

    here, there = end_of(message), end_of(got)
    both = 0.5 * here[1] * there[1]
    link_here = lookup(tables, 1, here[0])
    link_there = lookup(tables, 1, there[0])
    link = [both * (link_here[k] + link_there[k]) for k in range(10)]

    def complete(one, other):
        code, act, block, value, _, field = one
        _, _, _, _, sums, field_there = other
        half = 0.5 * act
        lateral = lookup(tables, 0, code)
        added = [half * (lateral[k] * sums[0] + sums[1 + k]) + link[k] for k in range(10)]
        across = apply_sym(link, field_there)
        flow = apply_sym(lateral, sums[11:15])
        diagonal = apply_sym(added, field)
        full = [
            value[c] + act * ((across[c] + half * (flow[c] + sums[15 + c])) - diagonal[c])
            for c in range(4)
        ]
        return [block[k] + added[k] for k in range(10)], full

    block, value = complete(here, there)
    block_there, value_there = complete(there, here)
    inverse = invert(block_there)
    gain = sym_product(inverse, link)
    rest = apply_sym(inverse, value_there)
    coupled, carried = back_product(link, gain), apply_sym(link, rest)
    x = apply_sym(
        invert([block[k] - coupled[k] for k in range(10)]),
        [value[c] + carried[c] for c in range(4)],
    )
    x_met = carry_on([gain[i][j] for i in range(4) for j in range(4)], rest, x)
    x_far = carry_on([got[40 + k] for k in range(16)], [got[56 + c] for c in range(4)], x_met)
    for c in range(4):
        xs[levels - 1, c] = x[c]
        xs[levels, c] = x_met[c]
        xs[levels + 1, c] = x_far[c]

    def retreat(step, x):
        n = levels - 2 - step
        x = carry_on([gains[n, k] for k in range(16)], [rests[n, c] for c in range(4)], x)
        for c in range(4):
            xs[n, c] = x[c]
        return x

    lax.fori_loop(0, levels - 1, retreat, x)

    acc = [zero() for _ in range(8)]
    for n in range(planes):
        field = [xs[n, c] for c in range(4)]
        code = codes_s[n] if n < levels else got[37 + n - levels].astype(jnp.int32)
        act = activity(code)
        flow = [act * value for value in apply_sym(lookup(tables, 0, code), field)]
        for c in range(4):
            kx[n, c] = flow[c]
        for k, value in enumerate(field + flow):
            for r in range(2):
                at = (2 * k + r) * planes + n
                x3[at : at + 1, :] = value[6 + r : 7 + r]
            acc[k] = jnp.where(lane // 2 == n, roll_lanes(value, 2 * n + 2), acc[k])
    for k in range(8):
        y3[k] = acc[k]
        d3[k] = acc[k][6:8]


def own_back_kernel(levels, xs, kx, sown, pre):
    last_x = lax.axis_index("lx") == lax.axis_size("lx") - 1
    last_y = lax.axis_index("ly") == lax.axis_size("ly") - 1
    row, lane = row_index(), lane_index()
    wl = jnp.where(row >= 2, 0.5, 0.0).astype(F32)
    wu = jnp.where(last_x & (row == 7), 0.0, 0.5).astype(F32)
    vl = jnp.where(lane >= 2, 0.5, 0.0).astype(F32)
    vu = jnp.where(last_y & (lane == 127), 0.0, 0.5).astype(F32)

    def gather(n, first=False):
        for k in range(8):
            ref, c = (xs, k) if k < 4 else (kx, k - 4)
            outer = ref[n + 1, c] if first else ref[n - 1, c] + ref[n + 1, c]
            w = ref[n, c] + 0.5 * outer
            g = wl * roll_rows(w, 2) + wu * w
            b = jnp.where(row >= 1, roll_rows(w, 1), 0.0) + g
            sown[n, k] = jnp.where(lane >= 1, roll_lanes(g, 1), 0.0) + (vl * roll_lanes(b, 2) + vu * b)

    gather(0, True)
    steps(1, levels + 1, gather, 2)

    def shift(n):
        for c in range(4):
            pre[n, c] = roll_lanes(roll_rows(xs[n, c], 1), 1)

    steps(0, levels, shift, 4)


def line_back_kernel(levels, sown, pre, x3, sums, moved, xw, xl):
    line = levels + PAD
    planes = levels + 2
    first_x = lax.axis_index("lx") == 0
    last_y = lax.axis_index("ly") == lax.axis_size("ly") - 1
    row = row_index()
    wl0 = jnp.where(first_x, 0.0, 0.5).astype(F32)
    lane = lax.broadcasted_iota(jnp.int32, (line, LANES), 1)
    vu = jnp.where(last_y & (lane == 127), 0.0, 0.5).astype(F32)
    vl = jnp.where(lane >= 2, 0.5, 0.0).astype(F32)
    for k in range(8):
        far, near = [
            lengthen(x3[(2 * k + r) * planes : (2 * k + r + 1) * planes, :], line) for r in range(2)
        ]
        if k < 4:
            xl[k] = roll_lanes(near, 1)
        far, near = line_sum(far), line_sum(near)
        g0, g1 = wl0 * far, 0.5 * near
        for r, (g, b) in enumerate(((g0, near + g0), (g1, g1))):
            at = (2 * k + r) * line
            xw[at : at + line, :] = jnp.where(lane >= 1, roll_lanes(g, 1), 0.0) + (
                vl * roll_lanes(b, 2) + vu * b
            )

    def add(n):
        for k in range(8):
            beyond = xw[pl.ds(2 * k * line + n, ROWS, stride=line), :]
            sums[n, k] = sown[n, k] + jnp.where(row < 2, beyond, 0.0)

    def fill(n):
        for c in range(4):
            moved[n, c] = jnp.where(row < 1, xl[c, pl.ds(n, 1), :], pre[n, c])

    steps(0, levels + 1, add, 4)
    steps(0, levels, fill, 4)


def finish_kernel(
    levels, sown, pre, y3, d3, it, codes, got, tables,
    updated, coarse, yv, ys, sm, up, co, sems,
):
    side = lax.axis_index("depth")
    first_x = lax.axis_index("lx") == 0
    first_y = lax.axis_index("ly") == 0
    last_x = lax.axis_index("lx") == lax.axis_size("lx") - 1
    row, lane = row_index(), lane_index()
    wl = jnp.where(first_x & (row == 0), 0.0, 0.5).astype(F32)
    wu = jnp.where(last_x & (row == 7), 0.0, 0.5).astype(F32)
    vl0 = jnp.where(first_y, 0.0, 0.5).astype(F32)
    even = lane % 2 == 0

    corner = [lengthen(d3[k], ROWS) for k in range(8)]
    for c in range(4):
        ys[c] = jnp.where(row < 1, roll_rows(corner[c], -1), roll_rows(y3[c], 1))

    def place(n):
        z = level_of(side, n, levels)
        for c in range(4):
            x = jnp.where(lane < 1, roll_lanes(ys[c], -2 * n - 1), pre[n, c])
            up[z, c] = it[z, c] + x

    steps(0, levels, place, 4)
    send_updated = pltpu.make_async_copy(up, updated, sems.at[0])
    send_updated.start()

    for k in range(8):
        two = jnp.where(row < 2, corner[k], roll_rows(y3[k], 2))
        one = jnp.where(row < 1, roll_rows(corner[k], -1), roll_rows(y3[k], 1))
        g = wl * two + wu * y3[k]
        b = one + g
        yv[k] = lane_sum(jnp.where(even, roll_lanes(g, -1) + vl0 * b, 0.5 * b))

    def smooth(n, code):
        sums = [
            sown[n, k] + jnp.where(lane < 2, roll_lanes(yv[k], -2 * n), 0.0) for k in range(8)
        ]
        half = 0.5 * activity(code)
        flow = apply_sym(lookup(tables, 0, code), sums[:4])
        for c in range(4):
            sm[n + 1, c] = half * (flow[c] + sums[4 + c])

    for c in range(4):
        sm[0, c] = zero()
    steps(0, levels, lambda n: smooth(n, codes[n]), 4)
    smooth(levels, got[39].astype(jnp.int32))

    step = 1 - 2 * side
    for k in range(levels // 2):
        at = side * (levels + 1) + step * 2 * k
        for c in range(4):
            co[k, c] = sm[at + step, c] + 0.5 * (sm[at, c] + sm[at + 2 * step, c])
    send_coarse = pltpu.make_async_copy(co, coarse, sems.at[1])
    send_coarse.start()
    send_updated.wait()
    send_coarse.wait()


def call(kernel, outs, *args, scratch=(), far_in=False, far_out=False):
    vmem = pl.BlockSpec(memory_space=pltpu.VMEM)
    if far_in:
        args = [pltpu.with_memory_space_constraint(x, pltpu.HBM) for x in args]
    far = pl.BlockSpec(memory_space=pltpu.HBM)
    return pl.pallas_call(
        kernel,
        out_shape=[jax.ShapeDtypeStruct(s, t) for s, t in outs],
        in_specs=[far if far_in else vmem] * len(args),
        out_specs=[far if far_out else vmem] * len(outs),
        scratch_shapes=list(scratch),
        compiler_params=pltpu.CompilerParams(vmem_limit_bytes=VMEM_LIMIT),
    )(*args)


def around(x, dx, dy):
    nx, ny = lax.axis_size("lx"), lax.axis_size("ly")
    pairs = [
        (i * ny + j, ((i + dx) % nx) * ny + (j + dy) % ny) for i in range(nx) for j in range(ny)
    ]
    return lax.ppermute(x, ("lx", "ly"), pairs)


def swap(x):
    return lax.ppermute(x, "depth", [(0, 1), (1, 0)])


def local(iterate, right_side, storage, zones, counts, materials):
    levels = zones.shape[0]
    line, planes = levels + PAD, levels + 2
    tile = (ROWS, LANES)
    vmem = lambda *shape: pltpu.VMEM(shape, F32)
    tables = jnp.broadcast_to(
        materials.transpose(0, 2, 3, 1).reshape(32, ROWS, 1), (32, ROWS, LANES)
    )
    it, rt, st, codes, xm, ym, dm = call(
        functools.partial(pack_kernel, levels),
        [((levels, 4) + tile, F32), ((levels, 4) + tile, F32), ((levels,) + tile, F32),
         ((levels,) + tile, jnp.int32),
         ((15, levels, LANES), F32), ((10,) + tile, F32), ((10, 2, LANES), F32)],
        iterate, right_side, storage, zones, counts,
        scratch=[
            pltpu.VMEM((levels,) + tile, jnp.int32), pltpu.VMEM(tile, jnp.int32),
            pltpu.SemaphoreType.DMA((5,)),
        ],
        far_in=True,
    )
    xm_in, ym_in, dm_in = around(xm, -1, 0), around(ym, 0, -1), around(dm, -1, -1)
    sown, pre = call(
        functools.partial(own_kernel, levels),
        [((levels + 1, SUMMED) + tile, F32), ((levels, 10) + tile, F32)],
        it, rt, st, codes, tables,
        scratch=[vmem(levels + 3, SUMMED, *tile)],
    )
    sums, moved = call(
        functools.partial(line_kernel, levels),
        [((levels + 1, SUMMED) + tile, F32), ((levels, 10) + tile, F32)],
        sown, pre, xm_in, tables,
        scratch=[vmem((2 * SUMMED + 12) * line, LANES), vmem(10, levels, LANES)],
    )
    gains, rests, message, codes_s = call(
        functools.partial(sweep_kernel, levels),
        [((levels - 1, 16) + tile, F32), ((levels - 1, 4) + tile, F32), ((MESSAGE,) + tile, F32),
         ((levels,) + tile, jnp.int32)],
        sums, moved, ym_in, dm_in, codes, tables,
        scratch=[
            vmem(SUMMED, *tile), vmem(10, *tile),
            vmem(planes, 4, *tile), vmem(levels, 4, *tile), vmem(levels, *tile),
            vmem(levels, 10, *tile), vmem(levels + 1, 10, *tile), vmem(levels, 4, *tile),
        ],
    )
    got = swap(message)
    xs, kx, x3, y3, d3 = call(
        functools.partial(back_kernel, levels),
        [((planes, 4) + tile, F32), ((planes, 4) + tile, F32),
         ((16 * planes, LANES), F32), ((8,) + tile, F32), ((8, 2, LANES), F32)],
        gains, rests, message, got, codes_s, tables,
    )
    x3_in, y3_in, d3_in = around(x3, 1, 0), around(y3, 0, 1), around(d3, 1, 1)
    sown3, pre3 = call(
        functools.partial(own_back_kernel, levels),
        [((levels + 1, 8) + tile, F32), ((levels, 4) + tile, F32)],
        xs, kx,
    )
    sums3, moved3 = call(
        functools.partial(line_back_kernel, levels),
        [((levels + 1, 8) + tile, F32), ((levels, 4) + tile, F32)],
        sown3, pre3, x3_in,
        scratch=[vmem((16 + 6) * line, LANES), vmem(4, line, LANES)],
    )
    updated, coarse = call(
        functools.partial(finish_kernel, levels),
        [((levels, 4) + tile, F32), ((levels // 2, 4) + tile, F32)],
        sums3, moved3, y3_in, d3_in, it, codes, got, tables,
        scratch=[
            vmem(8, *tile), vmem(4, *tile),
            vmem(levels + 2, 4, *tile), vmem(levels, 4, *tile), vmem(levels // 2, 4, *tile),
            pltpu.SemaphoreType.DMA((2,)),
        ],
        far_out=True,
    )
    return updated, coarse


def solution(mesh):
    placed = (
        P("depth", None, "lx", "ly"),
        P("depth", None, "lx", "ly"),
        P("depth", "lx", "ly"),
        P("depth", "lx", "ly"),
        P("lx", "ly"),
        P(),
    )
    return jax.shard_map(
        local,
        mesh=mesh,
        in_specs=placed,
        out_specs=(P("depth", None, "lx", "ly"), P("depth", None, "lx", "ly")),
        check_vma=False,
    )
```

```python
import functools

import jax
import jax.numpy as jnp
from jax import lax
from jax.experimental import pallas as pl
from jax.experimental.pallas import tpu as pltpu
from jax.sharding import PartitionSpec as P

PAIRS = [(i, j) for i in range(4) for j in range(i, 4)]
AT = {}
for _k, (_i, _j) in enumerate(PAIRS):
    AT[_i, _j] = AT[_j, _i] = _k

ROWS, LANES = 8, 128
SUMMED = 19
PAD = 8
MESSAGE = 60
F32 = jnp.float32
VMEM_LIMIT = 48 * 1024 * 1024


def row_index():
    return lax.broadcasted_iota(jnp.int32, (ROWS, LANES), 0)


def lane_index():
    return lax.broadcasted_iota(jnp.int32, (ROWS, LANES), 1)


def roll_rows(x, by):
    return pltpu.roll(x, by % x.shape[0], 0)


def roll_lanes(x, by):
    return pltpu.roll(x, by % LANES if isinstance(by, int) else lax.rem(by + LANES, LANES), 1)


def activity(codes):
    return jnp.where(codes > 0, 1.0, 0.0).astype(F32)


def lookup(tables, kind, codes):
    rows = jnp.maximum(codes - 1, 0)
    found = []
    for i, j in PAIRS:
        table = tables[kind * 16 + 4 * i + j]
        parts = [
            jnp.take_along_axis(table, rows[at : at + ROWS], axis=0, mode="promise_in_bounds")
            for at in range(0, rows.shape[0], ROWS)
        ]
        found.append(parts[0] if len(parts) == 1 else jnp.concatenate(parts, axis=0))
    return found


def apply_sym(matrix, vector):
    out = []
    for i in range(4):
        total = matrix[AT[i, 0]] * vector[0]
        for j in range(1, 4):
            total = total + matrix[AT[i, j]] * vector[j]
        out.append(total)
    return out


def summed_fields(tables, codes, field):
    act = activity(codes)
    lateral = [act * value for value in lookup(tables, 0, codes)]
    return [act] + lateral + [act * v for v in field] + apply_sym(lateral, field)


def level_of(side, n, levels):
    return side * (levels - 1) + (1 - 2 * side) * n


def steps(first, last, body, width=1):
    passes = (last - first) // width

    def one(i, carry):
        for j in range(width):
            body(first + i * width + j)
        return carry

    lax.fori_loop(0, passes, one, 0)
    for n in range(first + passes * width, last):
        body(n)


def zero():
    return jnp.zeros((ROWS, LANES), F32)


def pack_kernel(
    levels, iterate, right, storage, zones, counts,
    it, rt, st, codes_out, ym, dm, zones_v, counts_v, sems,
):
    side = lax.axis_index("depth")
    lane = lane_index()
    copies = [
        pltpu.make_async_copy(source, target, sems.at[k])
        for k, (source, target) in enumerate(
            [(zones, zones_v), (counts, counts_v), (iterate, it), (right, rt), (storage, st)]
        )
    ]
    for copy in copies:
        copy.start()
    for copy in copies:
        copy.wait()
    limit = counts_v[...] - side * levels
    acc = [zero() for _ in range(10)]
    for n in range(levels):
        z = level_of(side, n, levels)
        code = jnp.where(z < limit, zones_v[z] + 1, 0)
        codes_out[n] = code
        fields = [code.astype(F32)] + [it[z, c] for c in range(4)]
        fields += [rt[z, c] for c in range(4)] + [st[z]]
        for k, value in enumerate(fields):
            acc[k] = jnp.where(lane // 2 == n, roll_lanes(value, 2 * n), acc[k])
    for k in range(10):
        ym[k] = acc[k]
        dm[k] = acc[k][0:2]


def pack_rows_kernel(levels, it, rt, st, codes, xm):
    side = lax.axis_index("depth")
    for n in range(levels):
        z = level_of(side, n, levels)
        fields = [codes[n].astype(F32)] + [it[z, c] for c in range(4)]
        fields += [rt[z, c] for c in range(4)] + [st[z]]
        for k, value in enumerate(fields):
            xm[k, n : n + 1, :] = value[0:1]
            if k < 5:
                xm[10 + k, n : n + 1, :] = value[1:2]


def own_kernel(levels, it, rt, st, codes, tables, sown, pre, u):
    side = lax.axis_index("depth")
    last_x = lax.axis_index("lx") == lax.axis_size("lx") - 1
    last_y = lax.axis_index("ly") == lax.axis_size("ly") - 1
    row, lane = row_index(), lane_index()
    wl = jnp.where(last_x & (row == 7), 0.0, 0.5).astype(F32)
    wu = jnp.where(row < 6, 0.5, 0.0).astype(F32)
    vl = jnp.where(last_y & (lane == 127), 0.0, 0.5).astype(F32)
    vu = jnp.where(lane < 126, 0.5, 0.0).astype(F32)
    for k in range(SUMMED):
        u[0, k] = zero()
        u[levels + 1, k] = zero()
        u[levels + 2, k] = zero()

    def fill(n):
        z = level_of(side, n, levels)
        field = [it[z, c] for c in range(4)]
        for k, value in enumerate(summed_fields(tables, codes[n], field)):
            u[n + 1, k] = value

    steps(0, levels, fill)

    def shift(n):
        z = level_of(side, n, levels)
        fields = [codes[n].astype(F32)] + [it[z, c] for c in range(4)]
        fields += [rt[z, c] for c in range(4)] + [st[z]]
        for k, value in enumerate(fields):
            pre[n, k] = roll_lanes(roll_rows(value, -1), -1)

    steps(0, levels, shift, 2)

    def gather(n):
        for k in range(SUMMED):
            w = u[n + 1, k] + 0.5 * (u[n, k] + u[n + 2, k])
            g = wl * w + wu * roll_rows(w, -2)
            b = jnp.where(row < 7, roll_rows(w, -1), 0.0) + g
            sown[n, k] = jnp.where(lane < 127, roll_lanes(g, -1), 0.0) + (vu * roll_lanes(b, -2) + vl * b)

    steps(0, levels + 1, gather, 2)


def invert(m):
    d = lambda i, j: m[AT[i, j]]

    def small(a, b, c):
        ia = 1.0 / a
        l = b * ia
        ic = 1.0 / (c - l * b)
        lc = l * ic
        return ia + l * lc, -lc, ic

    a00, a01, a11 = small(d(0, 0), d(0, 1), d(1, 1))
    t00 = d(2, 0) * a00 + d(2, 1) * a01
    t01 = d(2, 0) * a01 + d(2, 1) * a11
    t10 = d(3, 0) * a00 + d(3, 1) * a01
    t11 = d(3, 0) * a01 + d(3, 1) * a11
    s00 = d(2, 2) - (t00 * d(2, 0) + t01 * d(2, 1))
    s01 = d(3, 2) - (t10 * d(2, 0) + t11 * d(2, 1))
    s11 = d(3, 3) - (t10 * d(3, 0) + t11 * d(3, 1))
    i22, i32, i33 = small(s00, s01, s11)
    u00 = i22 * t00 + i32 * t10
    u01 = i22 * t01 + i32 * t11
    u10 = i32 * t00 + i33 * t10
    u11 = i32 * t01 + i33 * t11
    i00 = a00 + (t00 * u00 + t10 * u10)
    i01 = a01 + (t00 * u01 + t10 * u11)
    i11 = a11 + (t01 * u01 + t11 * u11)
    return [i00, i01, -u00, -u10, i11, -u01, -u11, i22, i32, i33]


def sym_product(left, right):
    return [
        [
            (left[AT[i, 0]] * right[AT[0, j]] + left[AT[i, 1]] * right[AT[1, j]])
            + (left[AT[i, 2]] * right[AT[2, j]] + left[AT[i, 3]] * right[AT[3, j]])
            for j in range(4)
        ]
        for i in range(4)
    ]


def back_product(link, gain):
    return [
        (link[AT[i, 0]] * gain[0][j] + link[AT[i, 1]] * gain[1][j])
        + (link[AT[i, 2]] * gain[2][j] + link[AT[i, 3]] * gain[3][j])
        for i, j in PAIRS
    ]


def line_sum(values):
    return values + 0.5 * (roll_rows(values, 1) + roll_rows(values, -1))


def lane_sum(values):
    return values + 0.5 * (roll_lanes(values, 2) + roll_lanes(values, -2))


def lengthen(values, rows):
    return jnp.concatenate([values, jnp.zeros((rows - values.shape[0], LANES), F32)], axis=0)


def line_kernel(levels, sown, pre, xm, tables, sums, moved, xw, xl):
    line = levels + PAD
    last_x = lax.axis_index("lx") == lax.axis_size("lx") - 1
    last_y = lax.axis_index("ly") == lax.axis_size("ly") - 1
    row = row_index()
    wu6 = jnp.where(last_x, 0.0, 0.5).astype(F32)
    lane = lax.broadcasted_iota(jnp.int32, (line, LANES), 1)
    vl = jnp.where(last_y & (lane == 127), 0.0, 0.5).astype(F32)
    vu = jnp.where(lane < 126, 0.5, 0.0).astype(F32)
    lines = []
    for r in range(2):
        codes = lengthen(xm[10 * r], line).astype(jnp.int32)
        lines.append(summed_fields(tables, codes, [lengthen(xm[10 * r + 1 + c], line) for c in range(4)]))
    for k in range(SUMMED):
        x8, x9 = line_sum(lines[0][k]), line_sum(lines[1][k])
        g6, g7 = wu6 * x8, 0.5 * x9
        for r, (g, b) in enumerate(((g6, g6), (g7, x8 + g7))):
            at = (2 * k + r + 6) * line
            xw[at : at + line, :] = jnp.where(lane < 127, roll_lanes(g, -1), 0.0) + (
                vu * roll_lanes(b, -2) + vl * b
            )
    for k in range(10):
        xl[k] = roll_lanes(xm[k], -1)

    def add(n):
        for k in range(SUMMED):
            beyond = xw[pl.ds(2 * k * line + n, ROWS, stride=line), :]
            sums[n, k] = sown[n, k] + jnp.where(row >= 6, beyond, 0.0)

    def fill(n):
        for k in range(10):
            moved[n, k] = jnp.where(row == 7, xl[k, pl.ds(n, 1), :], pre[n, k])

    steps(0, levels + 1, add, 2)
    steps(0, levels, fill, 2)


def sweep_kernel(
    levels, sown, pre, ym, dm, codes, tables,
    gains, rests, message, codes_s,
    yv, ys, fs, rs, ss, ps, ms, qs,
):
    last_x = lax.axis_index("lx") == lax.axis_size("lx") - 1
    last_y = lax.axis_index("ly") == lax.axis_size("ly") - 1
    row, lane = row_index(), lane_index()
    wl = jnp.where(last_x & (row == 7), 0.0, 0.5).astype(F32)
    wu = jnp.where(last_x & (row == 6), 0.0, 0.5).astype(F32)
    vu127 = jnp.where(last_y, 0.0, 0.5).astype(F32)
    even = lane % 2 == 0
    end = lane == 127

    corner = [lengthen(dm[k], ROWS) for k in range(10)]
    for k in range(10):
        ys[k] = roll_rows(jnp.where(row < 1, corner[k], ym[k]), -1)
    side_u = summed_fields(tables, ym[0].astype(jnp.int32), [ym[1 + c] for c in range(4)])
    corner_u = summed_fields(tables, corner[0].astype(jnp.int32), corner[1:5])
    for k in range(SUMMED):
        one = roll_rows(jnp.where(row < 1, corner_u[k], side_u[k]), -1)
        two = roll_rows(jnp.where(row < 2, corner_u[k], side_u[k]), -2)
        g = wl * side_u[k] + wu * two
        b = one + g
        yv[k] = lane_sum(jnp.where(even, vu127 * b, roll_lanes(g, 1) + 0.5 * b))

    def shift(n):
        moved = [jnp.where(end, roll_lanes(ys[k], 127 - 2 * n), pre[n, k]) for k in range(10)]
        codes_s[n] = moved[0].astype(jnp.int32)
        for c in range(4):
            fs[n + 1, c] = moved[1 + c]
            rs[n, c] = moved[5 + c]
        ss[n] = moved[9]

    for c in range(4):
        fs[0, c] = zero()
        fs[levels + 1, c] = zero()
    for k in range(10):
        ms[0, k] = zero()

    def lateral_sums(n):
        return [
            sown[n, k] + jnp.where(lane >= 126, roll_lanes(yv[k], 126 - 2 * n), 0.0)
            for k in range(SUMMED)
        ]

    def assemble(n, last=False):
        sums = lateral_sums(n)
        act = activity(codes_s[n])
        half = 0.5 * act
        lateral = lookup(tables, 0, codes_s[n])
        below = [ms[n, k] for k in range(10)]
        if last:
            above = [zero() for _ in range(10)]
        else:
            both = half * activity(codes_s[n + 1])
            here = lookup(tables, 1, codes_s[n])
            there = lookup(tables, 1, codes_s[n + 1])
            above = [both * (here[k] + there[k]) for k in range(10)]
        block = []
        for k, (i, j) in enumerate(PAIRS):
            value = half * (lateral[k] * sums[0] + sums[1 + k]) + (below[k] + above[k])
            block.append(value + ss[n] if i == j else value)
        field = [fs[n + 1, c] for c in range(4)]
        before = apply_sym(below, [fs[n, c] for c in range(4)])
        after = apply_sym(above, [fs[n + 2, c] for c in range(4)])
        diagonal = apply_sym(block, field)
        flow = apply_sym(lateral, sums[11:15])
        for k in range(10):
            ms[n + 1, k] = above[k]
            ps[n, k] = block[k]
        for c in range(4):
            near = (before[c] + after[c]) + half * (flow[c] + sums[15 + c])
            qs[n, c] = act * (rs[n, c] - (diagonal[c] - near))

    def eliminate(n, carry):
        coupled, carried = carry
        block = [ps[n, k] for k in range(10)]
        link = [ms[n + 1, k] for k in range(10)]
        value = [qs[n, c] + carried[c] for c in range(4)]
        inverse = invert([block[k] - coupled[k] for k in range(10)])
        gain = sym_product(inverse, link)
        rest = apply_sym(inverse, value)
        for i in range(4):
            rests[n, i] = rest[i]
            for j in range(4):
                gains[n, 4 * i + j] = gain[i][j]
        return back_product(link, gain), apply_sym(link, rest)

    shift(0)
    shift(1)
    shift(2)
    assemble(0)

    def advance(n, carry):
        carry = eliminate(n, carry)
        assemble(n + 1)
        shift(n + 3)
        return carry

    zeros = [zero() for _ in range(10)]
    carry = lax.fori_loop(0, levels - 3, advance, (zeros, zeros[:4]))
    carry = eliminate(levels - 3, carry)
    assemble(levels - 2)
    carry = eliminate(levels - 2, carry)
    assemble(levels - 1, True)
    coupled, carried = carry
    end_n = levels - 1
    for k in range(10):
        message[k] = ps[end_n, k] - coupled[k]
    for c in range(4):
        message[10 + c] = qs[end_n, c] + carried[c]
        message[33 + c] = fs[levels, c]
        message[56 + c] = rests[end_n - 1, c]
    for k, value in enumerate(lateral_sums(levels)):
        message[14 + k] = value
    message[37] = codes_s[end_n].astype(F32)
    message[38] = codes_s[end_n - 1].astype(F32)
    message[39] = codes[end_n].astype(F32)
    for k in range(16):
        message[40 + k] = gains[end_n - 1, k]


def back_kernel(levels, gains, rests, message, got, codes_s, tables, xs, kx, x3, y3, d3):
    lane = lane_index()
    planes = levels + 2

    def carry_on(gain, rest, x):
        out = []
        for i in range(4):
            out.append(
                rest[i] + ((gain[4 * i] * x[0] + gain[4 * i + 1] * x[1])
                           + (gain[4 * i + 2] * x[2] + gain[4 * i + 3] * x[3]))
            )
        return out

    def end_of(ref):
        code = ref[37].astype(jnp.int32)
        act = activity(code)
        part = lambda at, count: [ref[at + k] for k in range(count)]
        return code, act, part(0, 10), part(10, 4), part(14, SUMMED), part(33, 4)

    here, there = end_of(message), end_of(got)
    both = 0.5 * here[1] * there[1]
    link_here = lookup(tables, 1, here[0])
    link_there = lookup(tables, 1, there[0])
    link = [both * (link_here[k] + link_there[k]) for k in range(10)]

    def complete(one, other):
        code, act, block, value, _, field = one
        _, _, _, _, sums, field_there = other
        half = 0.5 * act
        lateral = lookup(tables, 0, code)
        added = [half * (lateral[k] * sums[0] + sums[1 + k]) + link[k] for k in range(10)]
        across = apply_sym(link, field_there)
        flow = apply_sym(lateral, sums[11:15])
        diagonal = apply_sym(added, field)
        full = [
            value[c] + act * ((across[c] + half * (flow[c] + sums[15 + c])) - diagonal[c])
            for c in range(4)
        ]
        return [block[k] + added[k] for k in range(10)], full

    block, value = complete(here, there)
    block_there, value_there = complete(there, here)
    inverse = invert(block_there)
    gain = sym_product(inverse, link)
    rest = apply_sym(inverse, value_there)
    coupled, carried = back_product(link, gain), apply_sym(link, rest)
    x = apply_sym(
        invert([block[k] - coupled[k] for k in range(10)]),
        [value[c] + carried[c] for c in range(4)],
    )
    x_met = carry_on([gain[i][j] for i in range(4) for j in range(4)], rest, x)
    x_far = carry_on([got[40 + k] for k in range(16)], [got[56 + c] for c in range(4)], x_met)
    for c in range(4):
        xs[levels - 1, c] = x[c]
        xs[levels, c] = x_met[c]
        xs[levels + 1, c] = x_far[c]

    def retreat(step, x):
        n = levels - 2 - step
        x = carry_on([gains[n, k] for k in range(16)], [rests[n, c] for c in range(4)], x)
        for c in range(4):
            xs[n, c] = x[c]
        return x

    lax.fori_loop(0, levels - 1, retreat, x)

    acc = [zero() for _ in range(8)]
    for n in range(planes):
        field = [xs[n, c] for c in range(4)]
        code = codes_s[n] if n < levels else got[37 + n - levels].astype(jnp.int32)
        act = activity(code)
        flow = [act * value for value in apply_sym(lookup(tables, 0, code), field)]
        for c in range(4):
            kx[n, c] = flow[c]
        for k, value in enumerate(field + [code.astype(F32)]):
            for r in range(2):
                at = (2 * k + r) * planes + n
                x3[at : at + 1, :] = value[6 + r : 7 + r]
        for k, value in enumerate(field + flow):
            acc[k] = jnp.where(lane // 2 == n, roll_lanes(value, 2 * n + 2), acc[k])
    for k in range(8):
        y3[k] = acc[k]
        d3[k] = acc[k][6:8]


def own_back_kernel(levels, xs, kx, sown, pre):
    last_x = lax.axis_index("lx") == lax.axis_size("lx") - 1
    last_y = lax.axis_index("ly") == lax.axis_size("ly") - 1
    row, lane = row_index(), lane_index()
    wl = jnp.where(row >= 2, 0.5, 0.0).astype(F32)
    wu = jnp.where(last_x & (row == 7), 0.0, 0.5).astype(F32)
    vl = jnp.where(lane >= 2, 0.5, 0.0).astype(F32)
    vu = jnp.where(last_y & (lane == 127), 0.0, 0.5).astype(F32)

    def gather(n, first=False):
        for k in range(8):
            ref, c = (xs, k) if k < 4 else (kx, k - 4)
            outer = ref[n + 1, c] if first else ref[n - 1, c] + ref[n + 1, c]
            w = ref[n, c] + 0.5 * outer
            g = wl * roll_rows(w, 2) + wu * w
            b = jnp.where(row >= 1, roll_rows(w, 1), 0.0) + g
            sown[n, k] = jnp.where(lane >= 1, roll_lanes(g, 1), 0.0) + (vl * roll_lanes(b, 2) + vu * b)

    gather(0, True)
    steps(1, levels + 1, gather, 2)

    def shift(n):
        for c in range(4):
            pre[n, c] = roll_lanes(roll_rows(xs[n, c], 1), 1)

    steps(0, levels, shift, 4)


def line_back_kernel(levels, sown, pre, x3, tables, sums, moved, xw, xl):
    line = levels + PAD
    planes = levels + 2
    first_x = lax.axis_index("lx") == 0
    last_y = lax.axis_index("ly") == lax.axis_size("ly") - 1
    row = row_index()
    wl0 = jnp.where(first_x, 0.0, 0.5).astype(F32)
    lane = lax.broadcasted_iota(jnp.int32, (line, LANES), 1)
    vu = jnp.where(last_y & (lane == 127), 0.0, 0.5).astype(F32)
    vl = jnp.where(lane >= 2, 0.5, 0.0).astype(F32)
    lines = []
    for r in range(2):
        parts = [
            lengthen(x3[(2 * k + r) * planes : (2 * k + r + 1) * planes, :], line) for k in range(5)
        ]
        codes = parts[4].astype(jnp.int32)
        act = activity(codes)
        flow = apply_sym(lookup(tables, 0, codes), parts[:4])
        lines.append(parts[:4] + [act * value for value in flow])
    for k in range(8):
        far, near = lines[0][k], lines[1][k]
        if k < 4:
            xl[k] = roll_lanes(near, 1)
        far, near = line_sum(far), line_sum(near)
        g0, g1 = wl0 * far, 0.5 * near
        for r, (g, b) in enumerate(((g0, near + g0), (g1, g1))):
            at = (2 * k + r) * line
            xw[at : at + line, :] = jnp.where(lane >= 1, roll_lanes(g, 1), 0.0) + (
                vl * roll_lanes(b, 2) + vu * b
            )

    def add(n):
        for k in range(8):
            beyond = xw[pl.ds(2 * k * line + n, ROWS, stride=line), :]
            sums[n, k] = sown[n, k] + jnp.where(row < 2, beyond, 0.0)

    def fill(n):
        for c in range(4):
            moved[n, c] = jnp.where(row < 1, xl[c, pl.ds(n, 1), :], pre[n, c])

    steps(0, levels + 1, add, 4)
    steps(0, levels, fill, 4)


def finish_kernel(
    levels, sown, pre, y3, d3, it, codes, got, tables,
    updated, coarse, yv, ys, sm, up, co, sems,
):
    side = lax.axis_index("depth")
    first_x = lax.axis_index("lx") == 0
    first_y = lax.axis_index("ly") == 0
    last_x = lax.axis_index("lx") == lax.axis_size("lx") - 1
    row, lane = row_index(), lane_index()
    wl = jnp.where(first_x & (row == 0), 0.0, 0.5).astype(F32)
    wu = jnp.where(last_x & (row == 7), 0.0, 0.5).astype(F32)
    vl0 = jnp.where(first_y, 0.0, 0.5).astype(F32)
    even = lane % 2 == 0

    corner = [lengthen(d3[k], ROWS) for k in range(8)]
    for c in range(4):
        ys[c] = jnp.where(row < 1, roll_rows(corner[c], -1), roll_rows(y3[c], 1))

    def place(n):
        z = level_of(side, n, levels)
        for c in range(4):
            x = jnp.where(lane < 1, roll_lanes(ys[c], -2 * n - 1), pre[n, c])
            up[z, c] = it[z, c] + x

    steps(0, levels, place, 4)
    send_updated = pltpu.make_async_copy(up, updated, sems.at[0])
    send_updated.start()

    for k in range(8):
        two = jnp.where(row < 2, corner[k], roll_rows(y3[k], 2))
        one = jnp.where(row < 1, roll_rows(corner[k], -1), roll_rows(y3[k], 1))
        g = wl * two + wu * y3[k]
        b = one + g
        yv[k] = lane_sum(jnp.where(even, roll_lanes(g, -1) + vl0 * b, 0.5 * b))

    def smooth(n, code):
        sums = [
            sown[n, k] + jnp.where(lane < 2, roll_lanes(yv[k], -2 * n), 0.0) for k in range(8)
        ]
        half = 0.5 * activity(code)
        flow = apply_sym(lookup(tables, 0, code), sums[:4])
        for c in range(4):
            sm[n + 1, c] = half * (flow[c] + sums[4 + c])

    for c in range(4):
        sm[0, c] = zero()
    steps(0, levels, lambda n: smooth(n, codes[n]), 4)
    smooth(levels, got[39].astype(jnp.int32))

    step = 1 - 2 * side
    for k in range(levels // 2):
        at = side * (levels + 1) + step * 2 * k
        for c in range(4):
            co[k, c] = sm[at + step, c] + 0.5 * (sm[at, c] + sm[at + 2 * step, c])
    send_coarse = pltpu.make_async_copy(co, coarse, sems.at[1])
    send_coarse.start()
    send_updated.wait()
    send_coarse.wait()


def call(kernel, outs, *args, scratch=(), far_in=False, far_out=False):
    vmem = pl.BlockSpec(memory_space=pltpu.VMEM)
    if far_in:
        args = [pltpu.with_memory_space_constraint(x, pltpu.HBM) for x in args]
    far = pl.BlockSpec(memory_space=pltpu.HBM)
    return pl.pallas_call(
        kernel,
        out_shape=[jax.ShapeDtypeStruct(s, t) for s, t in outs],
        in_specs=[far if far_in else vmem] * len(args),
        out_specs=[far if far_out else vmem] * len(outs),
        scratch_shapes=list(scratch),
        compiler_params=pltpu.CompilerParams(vmem_limit_bytes=VMEM_LIMIT),
    )(*args)


def around(x, dx, dy):
    nx, ny = lax.axis_size("lx"), lax.axis_size("ly")
    pairs = [
        (i * ny + j, ((i + dx) % nx) * ny + (j + dy) % ny) for i in range(nx) for j in range(ny)
    ]
    return lax.ppermute(x, ("lx", "ly"), pairs)


def swap(x):
    return lax.ppermute(x, "depth", [(0, 1), (1, 0)])


def local(iterate, right_side, storage, zones, counts, materials):
    levels = zones.shape[0]
    line, planes = levels + PAD, levels + 2
    tile = (ROWS, LANES)
    vmem = lambda *shape: pltpu.VMEM(shape, F32)
    tables = jnp.broadcast_to(
        materials.transpose(0, 2, 3, 1).reshape(32, ROWS, 1), (32, ROWS, LANES)
    )
    it, rt, st, codes, ym, dm = call(
        functools.partial(pack_kernel, levels),
        [((levels, 4) + tile, F32), ((levels, 4) + tile, F32), ((levels,) + tile, F32),
         ((levels,) + tile, jnp.int32),
         ((10,) + tile, F32), ((10, 2, LANES), F32)],
        iterate, right_side, storage, zones, counts,
        scratch=[
            pltpu.VMEM((levels,) + tile, jnp.int32), pltpu.VMEM(tile, jnp.int32),
            pltpu.SemaphoreType.DMA((5,)),
        ],
        far_in=True,
    )
    xm, = call(
        functools.partial(pack_rows_kernel, levels), [((15, levels, LANES), F32)], it, rt, st, codes
    )
    xm_in, ym_in, dm_in = around(xm, -1, 0), around(ym, 0, -1), around(dm, -1, -1)
    sown, pre = call(
        functools.partial(own_kernel, levels),
        [((levels + 1, SUMMED) + tile, F32), ((levels, 10) + tile, F32)],
        it, rt, st, codes, tables,
        scratch=[vmem(levels + 3, SUMMED, *tile)],
    )
    sums, moved = call(
        functools.partial(line_kernel, levels),
        [((levels + 1, SUMMED) + tile, F32), ((levels, 10) + tile, F32)],
        sown, pre, xm_in, tables,
        scratch=[vmem((2 * SUMMED + 12) * line, LANES), vmem(10, levels, LANES)],
    )
    gains, rests, message, codes_s = call(
        functools.partial(sweep_kernel, levels),
        [((levels - 1, 16) + tile, F32), ((levels - 1, 4) + tile, F32), ((MESSAGE,) + tile, F32),
         ((levels,) + tile, jnp.int32)],
        sums, moved, ym_in, dm_in, codes, tables,
        scratch=[
            vmem(SUMMED, *tile), vmem(10, *tile),
            vmem(planes, 4, *tile), vmem(levels, 4, *tile), vmem(levels, *tile),
            vmem(levels, 10, *tile), vmem(levels + 1, 10, *tile), vmem(levels, 4, *tile),
        ],
    )
    got = swap(message)
    xs, kx, x3, y3, d3 = call(
        functools.partial(back_kernel, levels),
        [((planes, 4) + tile, F32), ((planes, 4) + tile, F32),
         ((10 * planes, LANES), F32), ((8,) + tile, F32), ((8, 2, LANES), F32)],
        gains, rests, message, got, codes_s, tables,
    )
    x3_in, y3_in, d3_in = around(x3, 1, 0), around(y3, 0, 1), around(d3, 1, 1)
    sown3, pre3 = call(
        functools.partial(own_back_kernel, levels),
        [((levels + 1, 8) + tile, F32), ((levels, 4) + tile, F32)],
        xs, kx,
    )
    sums3, moved3 = call(
        functools.partial(line_back_kernel, levels),
        [((levels + 1, 8) + tile, F32), ((levels, 4) + tile, F32)],
        sown3, pre3, x3_in, tables,
        scratch=[vmem((16 + 6) * line, LANES), vmem(4, line, LANES)],
    )
    updated, coarse = call(
        functools.partial(finish_kernel, levels),
        [((levels, 4) + tile, F32), ((levels // 2, 4) + tile, F32)],
        sums3, moved3, y3_in, d3_in, it, codes, got, tables,
        scratch=[
            vmem(8, *tile), vmem(4, *tile),
            vmem(levels + 2, 4, *tile), vmem(levels, 4, *tile), vmem(levels // 2, 4, *tile),
            pltpu.SemaphoreType.DMA((2,)),
        ],
        far_out=True,
    )
    return updated, coarse


def solution(mesh):
    placed = (
        P("depth", None, "lx", "ly"),
        P("depth", None, "lx", "ly"),
        P("depth", "lx", "ly"),
        P("depth", "lx", "ly"),
        P("lx", "ly"),
        P(),
    )
    return jax.shard_map(
        local,
        mesh=mesh,
        in_specs=placed,
        out_specs=(P("depth", None, "lx", "ly"), P("depth", None, "lx", "ly")),
        check_vma=False,
    )
```

```python
import functools

import jax
import jax.numpy as jnp
from jax import lax
from jax.experimental import pallas as pl
from jax.experimental.pallas import tpu as pltpu
from jax.sharding import PartitionSpec as P

PAIRS = [(i, j) for i in range(4) for j in range(i, 4)]
AT = {}
for _k, (_i, _j) in enumerate(PAIRS):
    AT[_i, _j] = AT[_j, _i] = _k

ROWS, LANES = 8, 128
SUMMED = 19
PAD = 8
MESSAGE = 60
F32 = jnp.float32
VMEM_LIMIT = 48 * 1024 * 1024


def row_index():
    return lax.broadcasted_iota(jnp.int32, (ROWS, LANES), 0)


def lane_index():
    return lax.broadcasted_iota(jnp.int32, (ROWS, LANES), 1)


def roll_rows(x, by):
    return pltpu.roll(x, by % x.shape[0], 0)


def roll_lanes(x, by):
    return pltpu.roll(x, by % LANES if isinstance(by, int) else lax.rem(by + LANES, LANES), 1)


def activity(codes):
    return jnp.where(codes > 0, 1.0, 0.0).astype(F32)


def lookup(tables, kind, codes):
    rows = jnp.maximum(codes - 1, 0)
    found = []
    for i, j in PAIRS:
        table = tables[kind * 16 + 4 * i + j]
        parts = [
            jnp.take_along_axis(table, rows[at : at + ROWS], axis=0, mode="promise_in_bounds")
            for at in range(0, rows.shape[0], ROWS)
        ]
        found.append(parts[0] if len(parts) == 1 else jnp.concatenate(parts, axis=0))
    return found


def apply_sym(matrix, vector):
    out = []
    for i in range(4):
        total = matrix[AT[i, 0]] * vector[0]
        for j in range(1, 4):
            total = total + matrix[AT[i, j]] * vector[j]
        out.append(total)
    return out


def summed_fields(tables, codes, field):
    act = activity(codes)
    lateral = [act * value for value in lookup(tables, 0, codes)]
    return [act] + lateral + [act * v for v in field] + apply_sym(lateral, field)


def level_of(side, n, levels):
    return side * (levels - 1) + (1 - 2 * side) * n


def steps(first, last, body, width=1):
    passes = (last - first) // width

    def one(i, carry):
        for j in range(width):
            body(first + i * width + j)
        return carry

    lax.fori_loop(0, passes, one, 0)
    for n in range(first + passes * width, last):
        body(n)


def zero():
    return jnp.zeros((ROWS, LANES), F32)


def pack_kernel(
    levels, iterate, right, storage, zones, counts,
    it, rt, st, codes_out, ym, dm, zones_v, counts_v, sems,
):
    side = lax.axis_index("depth")
    lane = lane_index()
    copies = [
        pltpu.make_async_copy(source, target, sems.at[k])
        for k, (source, target) in enumerate(
            [(zones, zones_v), (counts, counts_v), (iterate, it), (right, rt), (storage, st)]
        )
    ]
    for copy in copies:
        copy.start()
    for copy in copies:
        copy.wait()
    limit = counts_v[...] - side * levels
    acc = [zero() for _ in range(10)]
    for n in range(levels):
        z = level_of(side, n, levels)
        code = jnp.where(z < limit, zones_v[z] + 1, 0)
        codes_out[n] = code
        fields = [code.astype(F32)] + [it[z, c] for c in range(4)]
        fields += [rt[z, c] for c in range(4)] + [st[z]]
        for k, value in enumerate(fields):
            acc[k] = jnp.where(lane // 2 == n, roll_lanes(value, 2 * n + 2), acc[k])
    for k in range(10):
        ym[k] = acc[k]
        dm[k] = acc[k][6:8]


def pack_rows_kernel(levels, it, rt, st, codes, xm):
    side = lax.axis_index("depth")
    for n in range(levels):
        z = level_of(side, n, levels)
        fields = [codes[n].astype(F32)] + [it[z, c] for c in range(4)]
        fields += [rt[z, c] for c in range(4)] + [st[z]]
        for k, value in enumerate(fields):
            xm[k, n : n + 1, :] = value[7:8]
            if k < 5:
                xm[10 + k, n : n + 1, :] = value[6:7]


def own_kernel(levels, it, rt, st, codes, tables, sown, pre, u):
    side = lax.axis_index("depth")
    first_x = lax.axis_index("lx") == 0
    first_y = lax.axis_index("ly") == 0
    row, lane = row_index(), lane_index()
    wl = jnp.where(row >= 2, 0.5, 0.0).astype(F32)
    wu = jnp.where(first_x & (row == 0), 0.0, 0.5).astype(F32)
    vl = jnp.where(lane >= 2, 0.5, 0.0).astype(F32)
    vu = jnp.where(first_y & (lane == 0), 0.0, 0.5).astype(F32)
    for k in range(SUMMED):
        u[0, k] = zero()
        u[levels + 1, k] = zero()
        u[levels + 2, k] = zero()

    def fill(n):
        z = level_of(side, n, levels)
        field = [it[z, c] for c in range(4)]
        for k, value in enumerate(summed_fields(tables, codes[n], field)):
            u[n + 1, k] = value

    steps(0, levels, fill)

    def shift(n):
        z = level_of(side, n, levels)
        fields = [codes[n].astype(F32)] + [it[z, c] for c in range(4)]
        fields += [rt[z, c] for c in range(4)] + [st[z]]
        for k, value in enumerate(fields):
            pre[n, k] = roll_lanes(roll_rows(value, 1), 1)

    steps(0, levels, shift, 2)

    def gather(n):
        for k in range(SUMMED):
            w = u[n + 1, k] + 0.5 * (u[n, k] + u[n + 2, k])
            g = wl * roll_rows(w, 2) + wu * w
            b = jnp.where(row >= 1, roll_rows(w, 1), 0.0) + g
            sown[n, k] = jnp.where(lane >= 1, roll_lanes(g, 1), 0.0) + (vl * roll_lanes(b, 2) + vu * b)

    steps(0, levels + 1, gather, 2)


def invert(m):
    d = lambda i, j: m[AT[i, j]]

    def small(a, b, c):
        ia = 1.0 / a
        l = b * ia
        ic = 1.0 / (c - l * b)
        lc = l * ic
        return ia + l * lc, -lc, ic

    a00, a01, a11 = small(d(0, 0), d(0, 1), d(1, 1))
    t00 = d(2, 0) * a00 + d(2, 1) * a01
    t01 = d(2, 0) * a01 + d(2, 1) * a11
    t10 = d(3, 0) * a00 + d(3, 1) * a01
    t11 = d(3, 0) * a01 + d(3, 1) * a11
    s00 = d(2, 2) - (t00 * d(2, 0) + t01 * d(2, 1))
    s01 = d(3, 2) - (t10 * d(2, 0) + t11 * d(2, 1))
    s11 = d(3, 3) - (t10 * d(3, 0) + t11 * d(3, 1))
    i22, i32, i33 = small(s00, s01, s11)
    u00 = i22 * t00 + i32 * t10
    u01 = i22 * t01 + i32 * t11
    u10 = i32 * t00 + i33 * t10
    u11 = i32 * t01 + i33 * t11
    i00 = a00 + (t00 * u00 + t10 * u10)
    i01 = a01 + (t00 * u01 + t10 * u11)
    i11 = a11 + (t01 * u01 + t11 * u11)
    return [i00, i01, -u00, -u10, i11, -u01, -u11, i22, i32, i33]


def sym_product(left, right):
    return [
        [
            (left[AT[i, 0]] * right[AT[0, j]] + left[AT[i, 1]] * right[AT[1, j]])
            + (left[AT[i, 2]] * right[AT[2, j]] + left[AT[i, 3]] * right[AT[3, j]])
            for j in range(4)
        ]
        for i in range(4)
    ]


def back_product(link, gain):
    return [
        (link[AT[i, 0]] * gain[0][j] + link[AT[i, 1]] * gain[1][j])
        + (link[AT[i, 2]] * gain[2][j] + link[AT[i, 3]] * gain[3][j])
        for i, j in PAIRS
    ]


def line_sum(values):
    return values + 0.5 * (roll_rows(values, 1) + roll_rows(values, -1))


def lane_sum(values):
    return values + 0.5 * (roll_lanes(values, 2) + roll_lanes(values, -2))


def lengthen(values, rows):
    return jnp.concatenate([values, jnp.zeros((rows - values.shape[0], LANES), F32)], axis=0)


def line_kernel(levels, sown, pre, xm, tables, sums, moved, xw, xl):
    line = levels + PAD
    first_x = lax.axis_index("lx") == 0
    first_y = lax.axis_index("ly") == 0
    row = row_index()
    wl1 = jnp.where(first_x, 0.0, 0.5).astype(F32)
    lane = lax.broadcasted_iota(jnp.int32, (line, LANES), 1)
    vl = jnp.where(lane >= 2, 0.5, 0.0).astype(F32)
    vu = jnp.where(first_y & (lane == 0), 0.0, 0.5).astype(F32)
    lines = []
    for r in range(2):
        codes = lengthen(xm[10 * r], line).astype(jnp.int32)
        lines.append(summed_fields(tables, codes, [lengthen(xm[10 * r + 1 + c], line) for c in range(4)]))
    for k in range(SUMMED):
        near, far = line_sum(lines[0][k]), line_sum(lines[1][k])
        g0, g1 = 0.5 * far, wl1 * near
        for r, (g, b) in enumerate(((g0, near + g0), (g1, g1))):
            at = (2 * k + r) * line
            xw[at : at + line, :] = jnp.where(lane >= 1, roll_lanes(g, 1), 0.0) + (
                vl * roll_lanes(b, 2) + vu * b
            )
    for k in range(10):
        xl[k] = roll_lanes(xm[k], 1)

    def add(n):
        for k in range(SUMMED):
            beyond = xw[pl.ds(2 * k * line + n, ROWS, stride=line), :]
            sums[n, k] = sown[n, k] + jnp.where(row < 2, beyond, 0.0)

    def fill(n):
        for k in range(10):
            moved[n, k] = jnp.where(row < 1, xl[k, pl.ds(n, 1), :], pre[n, k])

    steps(0, levels + 1, add, 2)
    steps(0, levels, fill, 2)


def sweep_kernel(
    levels, sown, pre, ym, dm, codes, tables,
    gains, rests, message, codes_s,
    yv, ys, fs, rs, ss, ps, ms, qs,
):
    first_x = lax.axis_index("lx") == 0
    first_y = lax.axis_index("ly") == 0
    row, lane = row_index(), lane_index()
    wl = jnp.where(first_x & (row == 1), 0.0, 0.5).astype(F32)
    wu = jnp.where(first_x & (row == 0), 0.0, 0.5).astype(F32)
    vl1 = jnp.where(first_y, 0.0, 0.5).astype(F32)
    even = lane % 2 == 0

    corner = [lengthen(dm[k], ROWS) for k in range(10)]
    for k in range(10):
        ys[k] = jnp.where(row < 1, roll_rows(corner[k], -1), roll_rows(ym[k], 1))
    side_u = summed_fields(tables, ym[0].astype(jnp.int32), [ym[1 + c] for c in range(4)])
    corner_u = summed_fields(tables, corner[0].astype(jnp.int32), corner[1:5])
    for k in range(SUMMED):
        one = jnp.where(row < 1, roll_rows(corner_u[k], -1), roll_rows(side_u[k], 1))
        two = jnp.where(row < 2, corner_u[k], roll_rows(side_u[k], 2))
        g = wl * two + wu * side_u[k]
        b = one + g
        yv[k] = lane_sum(jnp.where(even, roll_lanes(g, -1) + 0.5 * b, vl1 * b))

    def shift(n):
        moved = [jnp.where(lane < 1, roll_lanes(ys[k], -2 * n - 1), pre[n, k]) for k in range(10)]
        codes_s[n] = moved[0].astype(jnp.int32)
        for c in range(4):
            fs[n + 1, c] = moved[1 + c]
            rs[n, c] = moved[5 + c]
        ss[n] = moved[9]

    for c in range(4):
        fs[0, c] = zero()
        fs[levels + 1, c] = zero()
    for k in range(10):
        ms[0, k] = zero()

    def lateral_sums(n):
        return [
            sown[n, k] + jnp.where(lane < 2, roll_lanes(yv[k], -2 * n), 0.0)
            for k in range(SUMMED)
        ]

    def assemble(n, last=False):
        sums = lateral_sums(n)
        act = activity(codes_s[n])
        half = 0.5 * act
        lateral = lookup(tables, 0, codes_s[n])
        below = [ms[n, k] for k in range(10)]
        if last:
            above = [zero() for _ in range(10)]
        else:
            both = half * activity(codes_s[n + 1])
            here = lookup(tables, 1, codes_s[n])
            there = lookup(tables, 1, codes_s[n + 1])
            above = [both * (here[k] + there[k]) for k in range(10)]
        block = []
        for k, (i, j) in enumerate(PAIRS):
            value = half * (lateral[k] * sums[0] + sums[1 + k]) + (below[k] + above[k])
            block.append(value + ss[n] if i == j else value)
        field = [fs[n + 1, c] for c in range(4)]
        before = apply_sym(below, [fs[n, c] for c in range(4)])
        after = apply_sym(above, [fs[n + 2, c] for c in range(4)])
        diagonal = apply_sym(block, field)
        flow = apply_sym(lateral, sums[11:15])
        for k in range(10):
            ms[n + 1, k] = above[k]
            ps[n, k] = block[k]
        for c in range(4):
            near = (before[c] + after[c]) + half * (flow[c] + sums[15 + c])
            qs[n, c] = act * (rs[n, c] - (diagonal[c] - near))

    def eliminate(n, carry):
        coupled, carried = carry
        block = [ps[n, k] for k in range(10)]
        link = [ms[n + 1, k] for k in range(10)]
        value = [qs[n, c] + carried[c] for c in range(4)]
        inverse = invert([block[k] - coupled[k] for k in range(10)])
        gain = sym_product(inverse, link)
        rest = apply_sym(inverse, value)
        for i in range(4):
            rests[n, i] = rest[i]
            for j in range(4):
                gains[n, 4 * i + j] = gain[i][j]
        return back_product(link, gain), apply_sym(link, rest)

    shift(0)
    shift(1)
    shift(2)
    assemble(0)

    def advance(n, carry):
        carry = eliminate(n, carry)
        assemble(n + 1)
        shift(n + 3)
        return carry

    zeros = [zero() for _ in range(10)]
    carry = lax.fori_loop(0, levels - 3, advance, (zeros, zeros[:4]))
    carry = eliminate(levels - 3, carry)
    assemble(levels - 2)
    carry = eliminate(levels - 2, carry)
    assemble(levels - 1, True)
    coupled, carried = carry
    end_n = levels - 1
    for k in range(10):
        message[k] = ps[end_n, k] - coupled[k]
    for c in range(4):
        message[10 + c] = qs[end_n, c] + carried[c]
        message[33 + c] = fs[levels, c]
        message[56 + c] = rests[end_n - 1, c]
    for k, value in enumerate(lateral_sums(levels)):
        message[14 + k] = value
    message[37] = codes_s[end_n].astype(F32)
    message[38] = codes_s[end_n - 1].astype(F32)
    message[39] = codes[end_n].astype(F32)
    for k in range(16):
        message[40 + k] = gains[end_n - 1, k]


def back_kernel(levels, gains, rests, message, got, codes_s, tables, xs, kx, x3, y3, d3):
    lane = lane_index()
    planes = levels + 2

    def carry_on(gain, rest, x):
        out = []
        for i in range(4):
            out.append(
                rest[i] + ((gain[4 * i] * x[0] + gain[4 * i + 1] * x[1])
                           + (gain[4 * i + 2] * x[2] + gain[4 * i + 3] * x[3]))
            )
        return out

    def end_of(ref):
        code = ref[37].astype(jnp.int32)
        act = activity(code)
        part = lambda at, count: [ref[at + k] for k in range(count)]
        return code, act, part(0, 10), part(10, 4), part(14, SUMMED), part(33, 4)

    here, there = end_of(message), end_of(got)
    both = 0.5 * here[1] * there[1]
    link_here = lookup(tables, 1, here[0])
    link_there = lookup(tables, 1, there[0])
    link = [both * (link_here[k] + link_there[k]) for k in range(10)]

    def complete(one, other):
        code, act, block, value, _, field = one
        _, _, _, _, sums, field_there = other
        half = 0.5 * act
        lateral = lookup(tables, 0, code)
        added = [half * (lateral[k] * sums[0] + sums[1 + k]) + link[k] for k in range(10)]
        across = apply_sym(link, field_there)
        flow = apply_sym(lateral, sums[11:15])
        diagonal = apply_sym(added, field)
        full = [
            value[c] + act * ((across[c] + half * (flow[c] + sums[15 + c])) - diagonal[c])
            for c in range(4)
        ]
        return [block[k] + added[k] for k in range(10)], full

    block, value = complete(here, there)
    block_there, value_there = complete(there, here)
    inverse = invert(block_there)
    gain = sym_product(inverse, link)
    rest = apply_sym(inverse, value_there)
    coupled, carried = back_product(link, gain), apply_sym(link, rest)
    x = apply_sym(
        invert([block[k] - coupled[k] for k in range(10)]),
        [value[c] + carried[c] for c in range(4)],
    )
    x_met = carry_on([gain[i][j] for i in range(4) for j in range(4)], rest, x)
    x_far = carry_on([got[40 + k] for k in range(16)], [got[56 + c] for c in range(4)], x_met)
    for c in range(4):
        xs[levels - 1, c] = x[c]
        xs[levels, c] = x_met[c]
        xs[levels + 1, c] = x_far[c]

    def retreat(step, x):
        n = levels - 2 - step
        x = carry_on([gains[n, k] for k in range(16)], [rests[n, c] for c in range(4)], x)
        for c in range(4):
            xs[n, c] = x[c]
        return x

    lax.fori_loop(0, levels - 1, retreat, x)

    acc = [zero() for _ in range(8)]
    for n in range(planes):
        field = [xs[n, c] for c in range(4)]
        code = codes_s[n] if n < levels else got[37 + n - levels].astype(jnp.int32)
        act = activity(code)
        flow = [act * value for value in apply_sym(lookup(tables, 0, code), field)]
        for c in range(4):
            kx[n, c] = flow[c]
        for k, value in enumerate(field + [code.astype(F32)]):
            for r in range(2):
                at = (2 * k + r) * planes + n
                x3[at : at + 1, :] = value[r : r + 1]
        for k, value in enumerate(field + flow):
            acc[k] = jnp.where(lane // 2 == n, roll_lanes(value, 2 * n), acc[k])
    for k in range(8):
        y3[k] = acc[k]
        d3[k] = acc[k][0:2]


def own_back_kernel(levels, xs, kx, sown, pre):
    first_x = lax.axis_index("lx") == 0
    first_y = lax.axis_index("ly") == 0
    row, lane = row_index(), lane_index()
    wl = jnp.where(first_x & (row == 0), 0.0, 0.5).astype(F32)
    wu = jnp.where(row < 6, 0.5, 0.0).astype(F32)
    vl = jnp.where(first_y & (lane == 0), 0.0, 0.5).astype(F32)
    vu = jnp.where(lane < 126, 0.5, 0.0).astype(F32)

    def gather(n, first=False):
        for k in range(8):
            ref, c = (xs, k) if k < 4 else (kx, k - 4)
            outer = ref[n + 1, c] if first else ref[n - 1, c] + ref[n + 1, c]
            w = ref[n, c] + 0.5 * outer
            g = wl * w + wu * roll_rows(w, -2)
            b = jnp.where(row < 7, roll_rows(w, -1), 0.0) + g
            sown[n, k] = jnp.where(lane < 127, roll_lanes(g, -1), 0.0) + (vu * roll_lanes(b, -2) + vl * b)

    gather(0, True)
    steps(1, levels + 1, gather, 2)

    def shift(n):
        for c in range(4):
            pre[n, c] = roll_lanes(roll_rows(xs[n, c], -1), -1)

    steps(0, levels, shift, 4)


def line_back_kernel(levels, sown, pre, x3, tables, sums, moved, xw, xl):
    line = levels + PAD
    planes = levels + 2
    last_x = lax.axis_index("lx") == lax.axis_size("lx") - 1
    first_y = lax.axis_index("ly") == 0
    row = row_index()
    wu7 = jnp.where(last_x, 0.0, 0.5).astype(F32)
    lane = lax.broadcasted_iota(jnp.int32, (line, LANES), 1)
    vl = jnp.where(first_y & (lane == 0), 0.0, 0.5).astype(F32)
    vu = jnp.where(lane < 126, 0.5, 0.0).astype(F32)
    lines = []
    for r in range(2):
        parts = [
            lengthen(x3[(2 * k + r) * planes : (2 * k + r + 1) * planes, :], line) for k in range(5)
        ]
        codes = parts[4].astype(jnp.int32)
        act = activity(codes)
        flow = apply_sym(lookup(tables, 0, codes), parts[:4])
        lines.append(parts[:4] + [act * value for value in flow])
    for k in range(8):
        near, far = lines[0][k], lines[1][k]
        if k < 4:
            xl[k] = roll_lanes(near, -1)
        near, far = line_sum(near), line_sum(far)
        g6, g7 = 0.5 * near, wu7 * far
        for r, (g, b) in enumerate(((g6, g6), (g7, near + g7))):
            at = (2 * k + r + 6) * line
            xw[at : at + line, :] = jnp.where(lane < 127, roll_lanes(g, -1), 0.0) + (
                vu * roll_lanes(b, -2) + vl * b
            )

    def add(n):
        for k in range(8):
            beyond = xw[pl.ds(2 * k * line + n, ROWS, stride=line), :]
            sums[n, k] = sown[n, k] + jnp.where(row >= 6, beyond, 0.0)

    def fill(n):
        for c in range(4):
            moved[n, c] = jnp.where(row == 7, xl[c, pl.ds(n, 1), :], pre[n, c])

    steps(0, levels + 1, add, 4)
    steps(0, levels, fill, 4)


def finish_kernel(
    levels, sown, pre, y3, d3, it, codes, got, tables,
    updated, coarse, yv, ys, sm, up, co, sems,
):
    side = lax.axis_index("depth")
    first_x = lax.axis_index("lx") == 0
    last_y = lax.axis_index("ly") == lax.axis_size("ly") - 1
    last_x = lax.axis_index("lx") == lax.axis_size("lx") - 1
    row, lane = row_index(), lane_index()
    wl = jnp.where(first_x & (row == 0), 0.0, 0.5).astype(F32)
    wu = jnp.where(last_x & (row == 7), 0.0, 0.5).astype(F32)
    vu127 = jnp.where(last_y, 0.0, 0.5).astype(F32)
    even = lane % 2 == 0

    corner = [lengthen(d3[k], ROWS) for k in range(8)]
    for c in range(4):
        ys[c] = roll_rows(jnp.where(row < 1, corner[c], y3[c]), -1)

    def place(n):
        z = level_of(side, n, levels)
        for c in range(4):
            x = jnp.where(lane == 127, roll_lanes(ys[c], 127 - 2 * n), pre[n, c])
            up[z, c] = it[z, c] + x

    steps(0, levels, place, 4)
    send_updated = pltpu.make_async_copy(up, updated, sems.at[0])
    send_updated.start()

    for k in range(8):
        two = roll_rows(jnp.where(row < 2, corner[k], y3[k]), -2)
        one = roll_rows(jnp.where(row < 1, corner[k], y3[k]), -1)
        g = wl * y3[k] + wu * two
        b = one + g
        yv[k] = lane_sum(jnp.where(even, 0.5 * b, roll_lanes(g, 1) + vu127 * b))

    def smooth(n, code):
        sums = [
            sown[n, k] + jnp.where(lane >= 126, roll_lanes(yv[k], 126 - 2 * n), 0.0) for k in range(8)
        ]
        half = 0.5 * activity(code)
        flow = apply_sym(lookup(tables, 0, code), sums[:4])
        for c in range(4):
            sm[n + 1, c] = half * (flow[c] + sums[4 + c])

    for c in range(4):
        sm[0, c] = zero()
    steps(0, levels, lambda n: smooth(n, codes[n]), 4)
    smooth(levels, got[39].astype(jnp.int32))

    step = 1 - 2 * side
    for k in range(levels // 2):
        at = side * (levels + 1) + step * 2 * k
        for c in range(4):
            co[k, c] = sm[at + step, c] + 0.5 * (sm[at, c] + sm[at + 2 * step, c])
    send_coarse = pltpu.make_async_copy(co, coarse, sems.at[1])
    send_coarse.start()
    send_updated.wait()
    send_coarse.wait()


def call(kernel, outs, *args, scratch=(), far_in=False, far_out=False):
    vmem = pl.BlockSpec(memory_space=pltpu.VMEM)
    if far_in:
        args = [pltpu.with_memory_space_constraint(x, pltpu.HBM) for x in args]
    far = pl.BlockSpec(memory_space=pltpu.HBM)
    return pl.pallas_call(
        kernel,
        out_shape=[jax.ShapeDtypeStruct(s, t) for s, t in outs],
        in_specs=[far if far_in else vmem] * len(args),
        out_specs=[far if far_out else vmem] * len(outs),
        scratch_shapes=list(scratch),
        compiler_params=pltpu.CompilerParams(vmem_limit_bytes=VMEM_LIMIT),
    )(*args)


def around(x, dx, dy):
    nx, ny = lax.axis_size("lx"), lax.axis_size("ly")
    pairs = [
        (i * ny + j, ((i + dx) % nx) * ny + (j + dy) % ny) for i in range(nx) for j in range(ny)
    ]
    return lax.ppermute(x, ("lx", "ly"), pairs)


def swap(x):
    return lax.ppermute(x, "depth", [(0, 1), (1, 0)])


def local(iterate, right_side, storage, zones, counts, materials):
    levels = zones.shape[0]
    line, planes = levels + PAD, levels + 2
    tile = (ROWS, LANES)
    vmem = lambda *shape: pltpu.VMEM(shape, F32)
    tables = jnp.broadcast_to(
        materials.transpose(0, 2, 3, 1).reshape(32, ROWS, 1), (32, ROWS, LANES)
    )
    it, rt, st, codes, ym, dm = call(
        functools.partial(pack_kernel, levels),
        [((levels, 4) + tile, F32), ((levels, 4) + tile, F32), ((levels,) + tile, F32),
         ((levels,) + tile, jnp.int32),
         ((10,) + tile, F32), ((10, 2, LANES), F32)],
        iterate, right_side, storage, zones, counts,
        scratch=[
            pltpu.VMEM((levels,) + tile, jnp.int32), pltpu.VMEM(tile, jnp.int32),
            pltpu.SemaphoreType.DMA((5,)),
        ],
        far_in=True,
    )
    xm, = call(
        functools.partial(pack_rows_kernel, levels), [((15, levels, LANES), F32)], it, rt, st, codes
    )
    xm_in, ym_in, dm_in = around(xm, 1, 0), around(ym, 0, 1), around(dm, 1, 1)
    sown, pre = call(
        functools.partial(own_kernel, levels),
        [((levels + 1, SUMMED) + tile, F32), ((levels, 10) + tile, F32)],
        it, rt, st, codes, tables,
        scratch=[vmem(levels + 3, SUMMED, *tile)],
    )
    sums, moved = call(
        functools.partial(line_kernel, levels),
        [((levels + 1, SUMMED) + tile, F32), ((levels, 10) + tile, F32)],
        sown, pre, xm_in, tables,
        scratch=[vmem((2 * SUMMED + 12) * line, LANES), vmem(10, levels, LANES)],
    )
    gains, rests, message, codes_s = call(
        functools.partial(sweep_kernel, levels),
        [((levels - 1, 16) + tile, F32), ((levels - 1, 4) + tile, F32), ((MESSAGE,) + tile, F32),
         ((levels,) + tile, jnp.int32)],
        sums, moved, ym_in, dm_in, codes, tables,
        scratch=[
            vmem(SUMMED, *tile), vmem(10, *tile),
            vmem(planes, 4, *tile), vmem(levels, 4, *tile), vmem(levels, *tile),
            vmem(levels, 10, *tile), vmem(levels + 1, 10, *tile), vmem(levels, 4, *tile),
        ],
    )
    got = swap(message)
    xs, kx, x3, y3, d3 = call(
        functools.partial(back_kernel, levels),
        [((planes, 4) + tile, F32), ((planes, 4) + tile, F32),
         ((10 * planes, LANES), F32), ((8,) + tile, F32), ((8, 2, LANES), F32)],
        gains, rests, message, got, codes_s, tables,
    )
    x3_in, y3_in, d3_in = around(x3, -1, 0), around(y3, 0, -1), around(d3, -1, -1)
    sown3, pre3 = call(
        functools.partial(own_back_kernel, levels),
        [((levels + 1, 8) + tile, F32), ((levels, 4) + tile, F32)],
        xs, kx,
    )
    sums3, moved3 = call(
        functools.partial(line_back_kernel, levels),
        [((levels + 1, 8) + tile, F32), ((levels, 4) + tile, F32)],
        sown3, pre3, x3_in, tables,
        scratch=[vmem((16 + 6) * line, LANES), vmem(4, line, LANES)],
    )
    updated, coarse = call(
        functools.partial(finish_kernel, levels),
        [((levels, 4) + tile, F32), ((levels // 2, 4) + tile, F32)],
        sums3, moved3, y3_in, d3_in, it, codes, got, tables,
        scratch=[
            vmem(8, *tile), vmem(4, *tile),
            vmem(levels + 2, 4, *tile), vmem(levels, 4, *tile), vmem(levels // 2, 4, *tile),
            pltpu.SemaphoreType.DMA((2,)),
        ],
        far_out=True,
    )
    return updated, coarse


def solution(mesh):
    placed = (
        P("depth", None, "lx", "ly"),
        P("depth", None, "lx", "ly"),
        P("depth", "lx", "ly"),
        P("depth", "lx", "ly"),
        P("lx", "ly"),
        P(),
    )
    return jax.shard_map(
        local,
        mesh=mesh,
        in_specs=placed,
        out_specs=(P("depth", None, "lx", "ly"), P("depth", None, "lx", "ly")),
        check_vma=False,
    )
```

```python
import functools

import jax
import jax.numpy as jnp
from jax import lax
from jax.experimental import pallas as pl
from jax.experimental.pallas import tpu as pltpu
from jax.sharding import PartitionSpec as P

PAIRS = [(i, j) for i in range(4) for j in range(i, 4)]
AT = {}
for _k, (_i, _j) in enumerate(PAIRS):
    AT[_i, _j] = AT[_j, _i] = _k

ROWS, LANES = 8, 128
SUMMED = 19
PAD = 8
MESSAGE = 60
F32 = jnp.float32
VMEM_LIMIT = 48 * 1024 * 1024


def row_index():
    return lax.broadcasted_iota(jnp.int32, (ROWS, LANES), 0)


def lane_index():
    return lax.broadcasted_iota(jnp.int32, (ROWS, LANES), 1)


def roll_rows(x, by):
    return pltpu.roll(x, by % x.shape[0], 0)


def roll_lanes(x, by):
    return pltpu.roll(x, by % LANES if isinstance(by, int) else lax.rem(by + LANES, LANES), 1)


def activity(codes):
    return jnp.where(codes > 0, 1.0, 0.0).astype(F32)


def lookup(tables, kind, codes):
    rows = jnp.maximum(codes - 1, 0)
    found = []
    for i, j in PAIRS:
        table = tables[kind * 16 + 4 * i + j]
        parts = [
            jnp.take_along_axis(table, rows[at : at + ROWS], axis=0, mode="promise_in_bounds")
            for at in range(0, rows.shape[0], ROWS)
        ]
        found.append(parts[0] if len(parts) == 1 else jnp.concatenate(parts, axis=0))
    return found


def apply_sym(matrix, vector):
    out = []
    for i in range(4):
        total = matrix[AT[i, 0]] * vector[0]
        for j in range(1, 4):
            total = total + matrix[AT[i, j]] * vector[j]
        out.append(total)
    return out


def summed_fields(tables, codes, field):
    act = activity(codes)
    lateral = [act * value for value in lookup(tables, 0, codes)]
    return [act] + lateral + [act * v for v in field] + apply_sym(lateral, field)


def level_of(side, n, levels):
    return side * (levels - 1) + (1 - 2 * side) * n


def steps(first, last, body, width=1):
    passes = (last - first) // width

    def one(i, carry):
        for j in range(width):
            body(first + i * width + j)
        return carry

    lax.fori_loop(0, passes, one, 0)
    for n in range(first + passes * width, last):
        body(n)


def zero():
    return jnp.zeros((ROWS, LANES), F32)


def pack_kernel(
    levels, iterate, right, storage, zones, counts,
    it, rt, st, codes_out, ym, dm, zones_v, counts_v, sems,
):
    side = lax.axis_index("depth")
    lane = lane_index()
    copies = [
        pltpu.make_async_copy(source, target, sems.at[k])
        for k, (source, target) in enumerate(
            [(zones, zones_v), (counts, counts_v), (iterate, it), (right, rt), (storage, st)]
        )
    ]
    for copy in copies:
        copy.start()
    for copy in copies:
        copy.wait()
    limit = counts_v[...] - side * levels
    acc = [zero() for _ in range(10)]
    for n in range(levels):
        z = level_of(side, n, levels)
        code = jnp.where(z < limit, zones_v[z] + 1, 0)
        codes_out[n] = code
        fields = [code.astype(F32)] + [it[z, c] for c in range(4)]
        fields += [rt[z, c] for c in range(4)] + [st[z]]
        for k, value in enumerate(fields):
            acc[k] = jnp.where(lane // 2 == n, roll_lanes(value, 2 * n + 2), acc[k])
    for k in range(10):
        ym[k] = acc[k]
        dm[k] = acc[k][6:8]


def pack_rows_kernel(levels, it, rt, st, codes, xm):
    side = lax.axis_index("depth")
    for n in range(levels):
        z = level_of(side, n, levels)
        fields = [codes[n].astype(F32)] + [it[z, c] for c in range(4)]
        fields += [rt[z, c] for c in range(4)] + [st[z]]
        for k, value in enumerate(fields):
            xm[k, n : n + 1, :] = value[7:8]
            if k < 5:
                xm[10 + k, n : n + 1, :] = value[6:7]


def own_kernel(levels, it, rt, st, codes, tables, sown, pre, u):
    side = lax.axis_index("depth")
    first_x = lax.axis_index("lx") == 0
    first_y = lax.axis_index("ly") == 0
    row, lane = row_index(), lane_index()
    wl = jnp.where(row >= 2, 0.5, 0.0).astype(F32)
    wu = jnp.where(first_x & (row == 0), 0.0, 0.5).astype(F32)
    vl = jnp.where(lane >= 2, 0.5, 0.0).astype(F32)
    vu = jnp.where(first_y & (lane == 0), 0.0, 0.5).astype(F32)
    for k in range(SUMMED):
        u[0, k] = zero()
        u[levels + 1, k] = zero()
        u[levels + 2, k] = zero()

    def fill(n):
        z = level_of(side, n, levels)
        field = [it[z, c] for c in range(4)]
        for k, value in enumerate(summed_fields(tables, codes[n], field)):
            u[n + 1, k] = value

    steps(0, levels, fill, 2)

    def shift(n):
        z = level_of(side, n, levels)
        fields = [codes[n].astype(F32)] + [it[z, c] for c in range(4)]
        fields += [rt[z, c] for c in range(4)] + [st[z]]
        for k, value in enumerate(fields):
            pre[n, k] = roll_lanes(roll_rows(value, 1), 1)

    steps(0, levels, shift, 4)

    def gather(n):
        for k in range(SUMMED):
            w = u[n + 1, k] + 0.5 * (u[n, k] + u[n + 2, k])
            g = wl * roll_rows(w, 2) + wu * w
            b = jnp.where(row >= 1, roll_rows(w, 1), 0.0) + g
            sown[n, k] = jnp.where(lane >= 1, roll_lanes(g, 1), 0.0) + (vl * roll_lanes(b, 2) + vu * b)

    steps(0, levels + 1, gather, 4)


def invert(m):
    d = lambda i, j: m[AT[i, j]]

    def small(a, b, c):
        ia = 1.0 / a
        l = b * ia
        ic = 1.0 / (c - l * b)
        lc = l * ic
        return ia + l * lc, -lc, ic

    a00, a01, a11 = small(d(0, 0), d(0, 1), d(1, 1))
    t00 = d(2, 0) * a00 + d(2, 1) * a01
    t01 = d(2, 0) * a01 + d(2, 1) * a11
    t10 = d(3, 0) * a00 + d(3, 1) * a01
    t11 = d(3, 0) * a01 + d(3, 1) * a11
    s00 = d(2, 2) - (t00 * d(2, 0) + t01 * d(2, 1))
    s01 = d(3, 2) - (t10 * d(2, 0) + t11 * d(2, 1))
    s11 = d(3, 3) - (t10 * d(3, 0) + t11 * d(3, 1))
    i22, i32, i33 = small(s00, s01, s11)
    u00 = i22 * t00 + i32 * t10
    u01 = i22 * t01 + i32 * t11
    u10 = i32 * t00 + i33 * t10
    u11 = i32 * t01 + i33 * t11
    i00 = a00 + (t00 * u00 + t10 * u10)
    i01 = a01 + (t00 * u01 + t10 * u11)
    i11 = a11 + (t01 * u01 + t11 * u11)
    return [i00, i01, -u00, -u10, i11, -u01, -u11, i22, i32, i33]


def sym_product(left, right):
    return [
        [
            (left[AT[i, 0]] * right[AT[0, j]] + left[AT[i, 1]] * right[AT[1, j]])
            + (left[AT[i, 2]] * right[AT[2, j]] + left[AT[i, 3]] * right[AT[3, j]])
            for j in range(4)
        ]
        for i in range(4)
    ]


def back_product(link, gain):
    return [
        (link[AT[i, 0]] * gain[0][j] + link[AT[i, 1]] * gain[1][j])
        + (link[AT[i, 2]] * gain[2][j] + link[AT[i, 3]] * gain[3][j])
        for i, j in PAIRS
    ]


def line_sum(values):
    return values + 0.5 * (roll_rows(values, 1) + roll_rows(values, -1))


def lane_sum(values):
    return values + 0.5 * (roll_lanes(values, 2) + roll_lanes(values, -2))


def lengthen(values, rows):
    return jnp.concatenate([values, jnp.zeros((rows - values.shape[0], LANES), F32)], axis=0)


def line_kernel(levels, sown, pre, xm, tables, sums, moved, xw, xl):
    line = levels + PAD
    first_x = lax.axis_index("lx") == 0
    first_y = lax.axis_index("ly") == 0
    row = row_index()
    wl1 = jnp.where(first_x, 0.0, 0.5).astype(F32)
    lane = lax.broadcasted_iota(jnp.int32, (line, LANES), 1)
    vl = jnp.where(lane >= 2, 0.5, 0.0).astype(F32)
    vu = jnp.where(first_y & (lane == 0), 0.0, 0.5).astype(F32)
    lines = []
    for r in range(2):
        codes = lengthen(xm[10 * r], line).astype(jnp.int32)
        lines.append(summed_fields(tables, codes, [lengthen(xm[10 * r + 1 + c], line) for c in range(4)]))
    for k in range(SUMMED):
        near, far = line_sum(lines[0][k]), line_sum(lines[1][k])
        g0, g1 = 0.5 * far, wl1 * near
        for r, (g, b) in enumerate(((g0, near + g0), (g1, g1))):
            at = (2 * k + r) * line
            xw[at : at + line, :] = jnp.where(lane >= 1, roll_lanes(g, 1), 0.0) + (
                vl * roll_lanes(b, 2) + vu * b
            )
    for k in range(10):
        xl[k] = roll_lanes(xm[k], 1)

    def add(n):
        for k in range(SUMMED):
            beyond = xw[pl.ds(2 * k * line + n, ROWS, stride=line), :]
            sums[n, k] = sown[n, k] + jnp.where(row < 2, beyond, 0.0)

    def fill(n):
        for k in range(10):
            moved[n, k] = jnp.where(row < 1, xl[k, pl.ds(n, 1), :], pre[n, k])

    steps(0, levels + 1, add, 2)
    steps(0, levels, fill, 2)


def sweep_kernel(
    levels, sown, pre, ym, dm, codes, tables,
    gains, rests, message, codes_s,
    yv, ys, fs, rs, ss, ps, ms, qs, vs, total,
):
    first_x = lax.axis_index("lx") == 0
    first_y = lax.axis_index("ly") == 0
    row, lane = row_index(), lane_index()
    wl = jnp.where(first_x & (row == 1), 0.0, 0.5).astype(F32)
    wu = jnp.where(first_x & (row == 0), 0.0, 0.5).astype(F32)
    vl1 = jnp.where(first_y, 0.0, 0.5).astype(F32)
    even = lane % 2 == 0

    corner = [lengthen(dm[k], ROWS) for k in range(10)]
    for k in range(10):
        ys[k] = jnp.where(row < 1, roll_rows(corner[k], -1), roll_rows(ym[k], 1))
    side_u = summed_fields(tables, ym[0].astype(jnp.int32), [ym[1 + c] for c in range(4)])
    corner_u = summed_fields(tables, corner[0].astype(jnp.int32), corner[1:5])
    for k in range(SUMMED):
        one = jnp.where(row < 1, roll_rows(corner_u[k], -1), roll_rows(side_u[k], 1))
        two = jnp.where(row < 2, corner_u[k], roll_rows(side_u[k], 2))
        g = wl * two + wu * side_u[k]
        b = one + g
        yv[k] = lane_sum(jnp.where(even, roll_lanes(g, -1) + 0.5 * b, vl1 * b))

    def shift(n):
        moved = [jnp.where(lane < 1, roll_lanes(ys[k], -2 * n - 1), pre[n, k]) for k in range(10)]
        codes_s[n] = moved[0].astype(jnp.int32)
        for c in range(4):
            fs[n + 1, c] = moved[1 + c]
            rs[n, c] = moved[5 + c]
        ss[n] = moved[9]

    for c in range(4):
        vs[0, c] = zero()
    for k in range(10):
        ms[0, k] = zero()

    def gather(n):
        for k in range(SUMMED):
            total[n, k] = sown[n, k] + jnp.where(lane < 2, roll_lanes(yv[k], -2 * n), 0.0)

    def assemble(n, last=False):
        sums = [total[n, k] for k in range(SUMMED)]
        act = activity(codes_s[n])
        half = 0.5 * act
        lateral = lookup(tables, 0, codes_s[n])
        below = [ms[n, k] for k in range(10)]
        if last:
            above = [zero() for _ in range(10)]
        else:
            both = half * activity(codes_s[n + 1])
            here = lookup(tables, 1, codes_s[n])
            there = lookup(tables, 1, codes_s[n + 1])
            above = [both * (here[k] + there[k]) for k in range(10)]
        block = []
        for k, (i, j) in enumerate(PAIRS):
            value = half * (lateral[k] * sums[0] + sums[1 + k]) + (below[k] + above[k])
            block.append(value + ss[n] if i == j else value)
        field = [fs[n + 1, c] for c in range(4)]
        if last:
            flux = [zero() for _ in range(4)]
        else:
            flux = apply_sym(above, [field[c] - fs[n + 2, c] for c in range(4)])
        flow = apply_sym(lateral, [sums[0] * field[c] - sums[11 + c] for c in range(4)])
        flow_back = apply_sym(sums[1:11], field)
        stored = ss[n]
        for c in range(4):
            out = half * (flow[c] + (flow_back[c] - sums[15 + c])) + (flux[c] - vs[n, c])
            qs[n, c] = act * (rs[n, c] - (stored * field[c] + out))
        for k in range(10):
            ms[n + 1, k] = above[k]
            ps[n, k] = block[k]
        for c in range(4):
            vs[n + 1, c] = flux[c]

    def eliminate(n, carry):
        coupled, carried = carry
        block = [ps[n, k] for k in range(10)]
        link = [ms[n + 1, k] for k in range(10)]
        value = [qs[n, c] + carried[c] for c in range(4)]
        inverse = invert([block[k] - coupled[k] for k in range(10)])
        gain = sym_product(inverse, link)
        rest = apply_sym(inverse, value)
        for i in range(4):
            rests[n, i] = rest[i]
            for j in range(4):
                gains[n, 4 * i + j] = gain[i][j]
        return back_product(link, gain), apply_sym(link, rest)

    for n in range(3):
        shift(n)
    for n in range(2):
        gather(n)
    assemble(0)

    def advance(n, carry):
        carry = eliminate(n, carry)
        assemble(n + 1)
        shift(n + 3)
        gather(n + 2)
        return carry

    zeros = [zero() for _ in range(10)]
    carry = lax.fori_loop(0, levels - 3, advance, (zeros, zeros[:4]))
    gather(levels - 1)
    gather(levels)
    carry = eliminate(levels - 3, carry)
    assemble(levels - 2)
    carry = eliminate(levels - 2, carry)
    assemble(levels - 1, True)
    coupled, carried = carry
    end_n = levels - 1
    for k in range(10):
        message[k] = ps[end_n, k] - coupled[k]
    for c in range(4):
        message[10 + c] = qs[end_n, c] + carried[c]
        message[33 + c] = fs[levels, c]
        message[56 + c] = rests[end_n - 1, c]
    for k in range(SUMMED):
        message[14 + k] = total[levels, k]
    message[37] = codes_s[end_n].astype(F32)
    message[38] = codes_s[end_n - 1].astype(F32)
    message[39] = codes[end_n].astype(F32)
    for k in range(16):
        message[40 + k] = gains[end_n - 1, k]


def back_kernel(levels, gains, rests, message, got, codes_s, tables, xs, kx, x3, y3, d3):
    lane = lane_index()
    planes = levels + 2

    def carry_on(gain, rest, x):
        out = []
        for i in range(4):
            out.append(
                rest[i] + ((gain[4 * i] * x[0] + gain[4 * i + 1] * x[1])
                           + (gain[4 * i + 2] * x[2] + gain[4 * i + 3] * x[3]))
            )
        return out

    def end_of(ref):
        code = ref[37].astype(jnp.int32)
        act = activity(code)
        part = lambda at, count: [ref[at + k] for k in range(count)]
        return code, act, part(0, 10), part(10, 4), part(14, SUMMED), part(33, 4)

    here, there = end_of(message), end_of(got)
    both = 0.5 * here[1] * there[1]
    link_here = lookup(tables, 1, here[0])
    link_there = lookup(tables, 1, there[0])
    link = [both * (link_here[k] + link_there[k]) for k in range(10)]

    def complete(one, other):
        code, act, block, value, _, field = one
        _, _, _, _, sums, field_there = other
        half = 0.5 * act
        lateral = lookup(tables, 0, code)
        added = [half * (lateral[k] * sums[0] + sums[1 + k]) + link[k] for k in range(10)]
        across = apply_sym(link, field_there)
        flow = apply_sym(lateral, sums[11:15])
        diagonal = apply_sym(added, field)
        full = [
            value[c] + act * ((across[c] + half * (flow[c] + sums[15 + c])) - diagonal[c])
            for c in range(4)
        ]
        return [block[k] + added[k] for k in range(10)], full

    block, value = complete(here, there)
    block_there, value_there = complete(there, here)
    inverse = invert(block_there)
    gain = sym_product(inverse, link)
    rest = apply_sym(inverse, value_there)
    coupled, carried = back_product(link, gain), apply_sym(link, rest)
    x = apply_sym(
        invert([block[k] - coupled[k] for k in range(10)]),
        [value[c] + carried[c] for c in range(4)],
    )
    x_met = carry_on([gain[i][j] for i in range(4) for j in range(4)], rest, x)
    x_far = carry_on([got[40 + k] for k in range(16)], [got[56 + c] for c in range(4)], x_met)
    for c in range(4):
        xs[levels - 1, c] = x[c]
        xs[levels, c] = x_met[c]
        xs[levels + 1, c] = x_far[c]

    def retreat(step, x):
        n = levels - 2 - step
        x = carry_on([gains[n, k] for k in range(16)], [rests[n, c] for c in range(4)], x)
        for c in range(4):
            xs[n, c] = x[c]
        return x

    lax.fori_loop(0, levels - 1, retreat, x)

    acc = [zero() for _ in range(8)]
    for n in range(planes):
        field = [xs[n, c] for c in range(4)]
        code = codes_s[n] if n < levels else got[37 + n - levels].astype(jnp.int32)
        act = activity(code)
        flow = [act * value for value in apply_sym(lookup(tables, 0, code), field)]
        for c in range(4):
            kx[n, c] = flow[c]
        for k, value in enumerate(field + [code.astype(F32)]):
            for r in range(2):
                at = (2 * k + r) * planes + n
                x3[at : at + 1, :] = value[r : r + 1]
        for k, value in enumerate(field + flow):
            acc[k] = jnp.where(lane // 2 == n, roll_lanes(value, 2 * n), acc[k])
    for k in range(8):
        y3[k] = acc[k]
        d3[k] = acc[k][0:2]


def own_back_kernel(levels, xs, kx, sown, pre):
    first_x = lax.axis_index("lx") == 0
    first_y = lax.axis_index("ly") == 0
    row, lane = row_index(), lane_index()
    wl = jnp.where(first_x & (row == 0), 0.0, 0.5).astype(F32)
    wu = jnp.where(row < 6, 0.5, 0.0).astype(F32)
    vl = jnp.where(first_y & (lane == 0), 0.0, 0.5).astype(F32)
    vu = jnp.where(lane < 126, 0.5, 0.0).astype(F32)

    def gather(n, first=False):
        for k in range(8):
            ref, c = (xs, k) if k < 4 else (kx, k - 4)
            outer = ref[n + 1, c] if first else ref[n - 1, c] + ref[n + 1, c]
            w = ref[n, c] + 0.5 * outer
            g = wl * w + wu * roll_rows(w, -2)
            b = jnp.where(row < 7, roll_rows(w, -1), 0.0) + g
            sown[n, k] = jnp.where(lane < 127, roll_lanes(g, -1), 0.0) + (vu * roll_lanes(b, -2) + vl * b)

    gather(0, True)
    steps(1, levels + 1, gather, 2)

    def shift(n):
        for c in range(4):
            pre[n, c] = roll_lanes(roll_rows(xs[n, c], -1), -1)

    steps(0, levels, shift, 4)


def line_back_kernel(levels, sown, pre, x3, tables, sums, moved, xw, xl):
    line = levels + PAD
    planes = levels + 2
    last_x = lax.axis_index("lx") == lax.axis_size("lx") - 1
    first_y = lax.axis_index("ly") == 0
    row = row_index()
    wu7 = jnp.where(last_x, 0.0, 0.5).astype(F32)
    lane = lax.broadcasted_iota(jnp.int32, (line, LANES), 1)
    vl = jnp.where(first_y & (lane == 0), 0.0, 0.5).astype(F32)
    vu = jnp.where(lane < 126, 0.5, 0.0).astype(F32)
    lines = []
    for r in range(2):
        parts = [
            lengthen(x3[(2 * k + r) * planes : (2 * k + r + 1) * planes, :], line) for k in range(5)
        ]
        codes = parts[4].astype(jnp.int32)
        act = activity(codes)
        flow = apply_sym(lookup(tables, 0, codes), parts[:4])
        lines.append(parts[:4] + [act * value for value in flow])
    for k in range(8):
        near, far = lines[0][k], lines[1][k]
        if k < 4:
            xl[k] = roll_lanes(near, -1)
        near, far = line_sum(near), line_sum(far)
        g6, g7 = 0.5 * near, wu7 * far
        for r, (g, b) in enumerate(((g6, g6), (g7, near + g7))):
            at = (2 * k + r + 6) * line
            xw[at : at + line, :] = jnp.where(lane < 127, roll_lanes(g, -1), 0.0) + (
                vu * roll_lanes(b, -2) + vl * b
            )

    def add(n):
        for k in range(8):
            beyond = xw[pl.ds(2 * k * line + n, ROWS, stride=line), :]
            sums[n, k] = sown[n, k] + jnp.where(row >= 6, beyond, 0.0)

    def fill(n):
        for c in range(4):
            moved[n, c] = jnp.where(row == 7, xl[c, pl.ds(n, 1), :], pre[n, c])

    steps(0, levels + 1, add, 4)
    steps(0, levels, fill, 4)


def finish_kernel(
    levels, sown, pre, y3, d3, it, codes, got, tables,
    updated, coarse, yv, ys, sm, up, co, sems,
):
    side = lax.axis_index("depth")
    first_x = lax.axis_index("lx") == 0
    last_y = lax.axis_index("ly") == lax.axis_size("ly") - 1
    last_x = lax.axis_index("lx") == lax.axis_size("lx") - 1
    row, lane = row_index(), lane_index()
    wl = jnp.where(first_x & (row == 0), 0.0, 0.5).astype(F32)
    wu = jnp.where(last_x & (row == 7), 0.0, 0.5).astype(F32)
    vu127 = jnp.where(last_y, 0.0, 0.5).astype(F32)
    even = lane % 2 == 0

    corner = [lengthen(d3[k], ROWS) for k in range(8)]
    for c in range(4):
        ys[c] = roll_rows(jnp.where(row < 1, corner[c], y3[c]), -1)

    def place(n):
        z = level_of(side, n, levels)
        for c in range(4):
            x = jnp.where(lane == 127, roll_lanes(ys[c], 127 - 2 * n), pre[n, c])
            up[z, c] = it[z, c] + x

    for n in range(levels):
        place(n)
    send_updated = pltpu.make_async_copy(up, updated, sems.at[0])
    send_updated.start()

    for k in range(8):
        two = roll_rows(jnp.where(row < 2, corner[k], y3[k]), -2)
        one = roll_rows(jnp.where(row < 1, corner[k], y3[k]), -1)
        g = wl * y3[k] + wu * two
        b = one + g
        yv[k] = lane_sum(jnp.where(even, 0.5 * b, roll_lanes(g, 1) + vu127 * b))

    def smooth(n, code):
        sums = [
            sown[n, k] + jnp.where(lane >= 126, roll_lanes(yv[k], 126 - 2 * n), 0.0) for k in range(8)
        ]
        half = 0.5 * activity(code)
        flow = apply_sym(lookup(tables, 0, code), sums[:4])
        for c in range(4):
            sm[n + 1, c] = half * (flow[c] + sums[4 + c])

    for c in range(4):
        sm[0, c] = zero()
    for n in range(levels):
        smooth(n, codes[n])
    smooth(levels, got[39].astype(jnp.int32))

    step = 1 - 2 * side
    for k in range(levels // 2):
        at = side * (levels + 1) + step * 2 * k
        for c in range(4):
            co[k, c] = sm[at + step, c] + 0.5 * (sm[at, c] + sm[at + 2 * step, c])
    send_coarse = pltpu.make_async_copy(co, coarse, sems.at[1])
    send_coarse.start()
    send_updated.wait()
    send_coarse.wait()


def call(kernel, outs, *args, scratch=(), far_in=False, far_out=False):
    vmem = pl.BlockSpec(memory_space=pltpu.VMEM)
    if far_in:
        args = [pltpu.with_memory_space_constraint(x, pltpu.HBM) for x in args]
    far = pl.BlockSpec(memory_space=pltpu.HBM)
    return pl.pallas_call(
        kernel,
        out_shape=[jax.ShapeDtypeStruct(s, t) for s, t in outs],
        in_specs=[far if far_in else vmem] * len(args),
        out_specs=[far if far_out else vmem] * len(outs),
        scratch_shapes=list(scratch),
        compiler_params=pltpu.CompilerParams(vmem_limit_bytes=VMEM_LIMIT),
    )(*args)


def around(x, dx, dy):
    nx, ny = lax.axis_size("lx"), lax.axis_size("ly")
    pairs = [
        (i * ny + j, ((i + dx) % nx) * ny + (j + dy) % ny) for i in range(nx) for j in range(ny)
    ]
    return lax.ppermute(x, ("lx", "ly"), pairs)


def swap(x):
    return lax.ppermute(x, "depth", [(0, 1), (1, 0)])


def local(iterate, right_side, storage, zones, counts, materials):
    levels = zones.shape[0]
    line, planes = levels + PAD, levels + 2
    tile = (ROWS, LANES)
    vmem = lambda *shape: pltpu.VMEM(shape, F32)
    tables = jnp.broadcast_to(
        materials.transpose(0, 2, 3, 1).reshape(32, ROWS, 1), (32, ROWS, LANES)
    )
    it, rt, st, codes, ym, dm = call(
        functools.partial(pack_kernel, levels),
        [((levels, 4) + tile, F32), ((levels, 4) + tile, F32), ((levels,) + tile, F32),
         ((levels,) + tile, jnp.int32),
         ((10,) + tile, F32), ((10, 2, LANES), F32)],
        iterate, right_side, storage, zones, counts,
        scratch=[
            pltpu.VMEM((levels,) + tile, jnp.int32), pltpu.VMEM(tile, jnp.int32),
            pltpu.SemaphoreType.DMA((5,)),
        ],
        far_in=True,
    )
    xm, = call(
        functools.partial(pack_rows_kernel, levels), [((15, levels, LANES), F32)], it, rt, st, codes
    )
    xm_in, ym_in, dm_in = around(xm, 1, 0), around(ym, 0, 1), around(dm, 1, 1)
    sown, pre = call(
        functools.partial(own_kernel, levels),
        [((levels + 1, SUMMED) + tile, F32), ((levels, 10) + tile, F32)],
        it, rt, st, codes, tables,
        scratch=[vmem(levels + 3, SUMMED, *tile)],
    )
    sums, moved = call(
        functools.partial(line_kernel, levels),
        [((levels + 1, SUMMED) + tile, F32), ((levels, 10) + tile, F32)],
        sown, pre, xm_in, tables,
        scratch=[vmem((2 * SUMMED + 12) * line, LANES), vmem(10, levels, LANES)],
    )
    gains, rests, message, codes_s = call(
        functools.partial(sweep_kernel, levels),
        [((levels - 1, 16) + tile, F32), ((levels - 1, 4) + tile, F32), ((MESSAGE,) + tile, F32),
         ((levels,) + tile, jnp.int32)],
        sums, moved, ym_in, dm_in, codes, tables,
        scratch=[
            vmem(SUMMED, *tile), vmem(10, *tile),
            vmem(planes, 4, *tile), vmem(levels, 4, *tile), vmem(levels, *tile),
            vmem(levels, 10, *tile), vmem(levels + 1, 10, *tile), vmem(levels, 4, *tile),
            vmem(levels + 1, 4, *tile), vmem(levels + 1, SUMMED, *tile),
        ],
    )
    got = swap(message)
    xs, kx, x3, y3, d3 = call(
        functools.partial(back_kernel, levels),
        [((planes, 4) + tile, F32), ((planes, 4) + tile, F32),
         ((10 * planes, LANES), F32), ((8,) + tile, F32), ((8, 2, LANES), F32)],
        gains, rests, message, got, codes_s, tables,
    )
    x3_in, y3_in, d3_in = around(x3, -1, 0), around(y3, 0, -1), around(d3, -1, -1)
    sown3, pre3 = call(
        functools.partial(own_back_kernel, levels),
        [((levels + 1, 8) + tile, F32), ((levels, 4) + tile, F32)],
        xs, kx,
    )
    sums3, moved3 = call(
        functools.partial(line_back_kernel, levels),
        [((levels + 1, 8) + tile, F32), ((levels, 4) + tile, F32)],
        sown3, pre3, x3_in, tables,
        scratch=[vmem((16 + 6) * line, LANES), vmem(4, line, LANES)],
    )
    updated, coarse = call(
        functools.partial(finish_kernel, levels),
        [((levels, 4) + tile, F32), ((levels // 2, 4) + tile, F32)],
        sums3, moved3, y3_in, d3_in, it, codes, got, tables,
        scratch=[
            vmem(8, *tile), vmem(4, *tile),
            vmem(levels + 2, 4, *tile), vmem(levels, 4, *tile), vmem(levels // 2, 4, *tile),
            pltpu.SemaphoreType.DMA((2,)),
        ],
        far_out=True,
    )
    return updated, coarse


def solution(mesh):
    placed = (
        P("depth", None, "lx", "ly"),
        P("depth", None, "lx", "ly"),
        P("depth", "lx", "ly"),
        P("depth", "lx", "ly"),
        P("lx", "ly"),
        P(),
    )
    return jax.shard_map(
        local,
        mesh=mesh,
        in_specs=placed,
        out_specs=(P("depth", None, "lx", "ly"), P("depth", None, "lx", "ly")),
        check_vma=False,
    )
```

```python
import functools

import jax
import jax.numpy as jnp
from jax import lax
from jax.experimental import pallas as pl
from jax.experimental.pallas import tpu as pltpu
from jax.sharding import PartitionSpec as P

PAIRS = [(i, j) for i in range(4) for j in range(i, 4)]
AT = {}
for _k, (_i, _j) in enumerate(PAIRS):
    AT[_i, _j] = AT[_j, _i] = _k

ROWS, LANES = 8, 128
SUMMED = 19
PAD = 8
MESSAGE = 60
F32 = jnp.float32
VMEM_LIMIT = 48 * 1024 * 1024


def row_index():
    return lax.broadcasted_iota(jnp.int32, (ROWS, LANES), 0)


def lane_index():
    return lax.broadcasted_iota(jnp.int32, (ROWS, LANES), 1)


def roll_rows(x, by):
    return pltpu.roll(x, by % x.shape[0], 0)


def roll_lanes(x, by):
    return pltpu.roll(x, by % LANES if isinstance(by, int) else lax.rem(by + LANES, LANES), 1)


def activity(codes):
    return jnp.where(codes > 0, 1.0, 0.0).astype(F32)


def lookup(tables, kind, codes):
    rows = jnp.maximum(codes - 1, 0)
    found = []
    for i, j in PAIRS:
        table = tables[kind * 16 + 4 * i + j]
        parts = [
            jnp.take_along_axis(table, rows[at : at + ROWS], axis=0, mode="promise_in_bounds")
            for at in range(0, rows.shape[0], ROWS)
        ]
        found.append(parts[0] if len(parts) == 1 else jnp.concatenate(parts, axis=0))
    return found


def apply_sym(matrix, vector):
    out = []
    for i in range(4):
        total = matrix[AT[i, 0]] * vector[0]
        for j in range(1, 4):
            total = total + matrix[AT[i, j]] * vector[j]
        out.append(total)
    return out


def summed_fields(tables, codes, field):
    act = activity(codes)
    lateral = [act * value for value in lookup(tables, 0, codes)]
    return [act] + lateral + [act * v for v in field] + apply_sym(lateral, field)


def level_of(side, n, levels):
    return side * (levels - 1) + (1 - 2 * side) * n


def steps(first, last, body, width=1):
    passes = (last - first) // width

    def one(i, carry):
        for j in range(width):
            body(first + i * width + j)
        return carry

    lax.fori_loop(0, passes, one, 0)
    for n in range(first + passes * width, last):
        body(n)


def zero():
    return jnp.zeros((ROWS, LANES), F32)


def rows_kernel(
    levels, iterate, right, storage, zones, counts,
    it, rt, st, codes_out, xm, zones_v, counts_v, sems,
):
    side = lax.axis_index("depth")
    copies = [
        pltpu.make_async_copy(source, target, sems.at[k])
        for k, (source, target) in enumerate(
            [(zones, zones_v), (counts, counts_v), (iterate, it), (right, rt), (storage, st)]
        )
    ]
    for copy in copies:
        copy.start()
    for copy in copies:
        copy.wait()
    limit = counts_v[...] - side * levels
    for n in range(levels):
        z = level_of(side, n, levels)
        code = jnp.where(z < limit, zones_v[z] + 1, 0)
        codes_out[n] = code
        fields = [code.astype(F32)] + [it[z, c] for c in range(4)]
        fields += [rt[z, c] for c in range(4)] + [st[z]]
        for k, value in enumerate(fields):
            xm[k, n : n + 1, :] = value[7:8]
            if k < 5:
                xm[10 + k, n : n + 1, :] = value[6:7]


def columns_kernel(levels, it, rt, st, codes, ym, dm):
    side = lax.axis_index("depth")
    lane = lane_index()
    acc = [zero() for _ in range(10)]
    for n in range(levels):
        z = level_of(side, n, levels)
        fields = [codes[n].astype(F32)] + [it[z, c] for c in range(4)]
        fields += [rt[z, c] for c in range(4)] + [st[z]]
        for k, value in enumerate(fields):
            acc[k] = jnp.where(lane // 2 == n, roll_lanes(value, 2 * n + 2), acc[k])
    for k in range(10):
        ym[k] = acc[k]
        dm[k] = acc[k][6:8]


def own_kernel(levels, it, rt, st, codes, tables, sown, pre, u):
    side = lax.axis_index("depth")
    first_x = lax.axis_index("lx") == 0
    first_y = lax.axis_index("ly") == 0
    row, lane = row_index(), lane_index()
    wl = jnp.where(row >= 2, 0.5, 0.0).astype(F32)
    wu = jnp.where(first_x & (row == 0), 0.0, 0.5).astype(F32)
    vl = jnp.where(lane >= 2, 0.5, 0.0).astype(F32)
    vu = jnp.where(first_y & (lane == 0), 0.0, 0.5).astype(F32)
    for k in range(SUMMED):
        u[0, k] = zero()
        u[levels + 1, k] = zero()
        u[levels + 2, k] = zero()

    def fill(n):
        z = level_of(side, n, levels)
        field = [it[z, c] for c in range(4)]
        for k, value in enumerate(summed_fields(tables, codes[n], field)):
            u[n + 1, k] = value

    steps(0, levels, fill, 2)

    def shift(n):
        z = level_of(side, n, levels)
        fields = [codes[n].astype(F32)] + [it[z, c] for c in range(4)]
        fields += [rt[z, c] for c in range(4)] + [st[z]]
        for k, value in enumerate(fields):
            pre[n, k] = roll_lanes(roll_rows(value, 1), 1)

    steps(0, levels, shift, 4)

    def gather(n):
        for k in range(SUMMED):
            w = u[n + 1, k] + 0.5 * (u[n, k] + u[n + 2, k])
            g = wl * roll_rows(w, 2) + wu * w
            b = jnp.where(row >= 1, roll_rows(w, 1), 0.0) + g
            sown[n, k] = jnp.where(lane >= 1, roll_lanes(g, 1), 0.0) + (vl * roll_lanes(b, 2) + vu * b)

    steps(0, levels + 1, gather, 4)


def invert(m):
    d = lambda i, j: m[AT[i, j]]

    def small(a, b, c):
        ia = 1.0 / a
        l = b * ia
        ic = 1.0 / (c - l * b)
        lc = l * ic
        return ia + l * lc, -lc, ic

    a00, a01, a11 = small(d(0, 0), d(0, 1), d(1, 1))
    t00 = d(2, 0) * a00 + d(2, 1) * a01
    t01 = d(2, 0) * a01 + d(2, 1) * a11
    t10 = d(3, 0) * a00 + d(3, 1) * a01
    t11 = d(3, 0) * a01 + d(3, 1) * a11
    s00 = d(2, 2) - (t00 * d(2, 0) + t01 * d(2, 1))
    s01 = d(3, 2) - (t10 * d(2, 0) + t11 * d(2, 1))
    s11 = d(3, 3) - (t10 * d(3, 0) + t11 * d(3, 1))
    i22, i32, i33 = small(s00, s01, s11)
    u00 = i22 * t00 + i32 * t10
    u01 = i22 * t01 + i32 * t11
    u10 = i32 * t00 + i33 * t10
    u11 = i32 * t01 + i33 * t11
    i00 = a00 + (t00 * u00 + t10 * u10)
    i01 = a01 + (t00 * u01 + t10 * u11)
    i11 = a11 + (t01 * u01 + t11 * u11)
    return [i00, i01, -u00, -u10, i11, -u01, -u11, i22, i32, i33]


def sym_product(left, right):
    return [
        [
            (left[AT[i, 0]] * right[AT[0, j]] + left[AT[i, 1]] * right[AT[1, j]])
            + (left[AT[i, 2]] * right[AT[2, j]] + left[AT[i, 3]] * right[AT[3, j]])
            for j in range(4)
        ]
        for i in range(4)
    ]


def back_product(link, gain):
    return [
        (link[AT[i, 0]] * gain[0][j] + link[AT[i, 1]] * gain[1][j])
        + (link[AT[i, 2]] * gain[2][j] + link[AT[i, 3]] * gain[3][j])
        for i, j in PAIRS
    ]


def line_sum(values):
    return values + 0.5 * (roll_rows(values, 1) + roll_rows(values, -1))


def lane_sum(values):
    return values + 0.5 * (roll_lanes(values, 2) + roll_lanes(values, -2))


def lengthen(values, rows):
    return jnp.concatenate([values, jnp.zeros((rows - values.shape[0], LANES), F32)], axis=0)


def line_kernel(levels, sown, pre, xm, tables, sums, moved, xw, xl):
    line = levels + PAD
    first_x = lax.axis_index("lx") == 0
    first_y = lax.axis_index("ly") == 0
    row = row_index()
    wl1 = jnp.where(first_x, 0.0, 0.5).astype(F32)
    lane = lax.broadcasted_iota(jnp.int32, (line, LANES), 1)
    vl = jnp.where(lane >= 2, 0.5, 0.0).astype(F32)
    vu = jnp.where(first_y & (lane == 0), 0.0, 0.5).astype(F32)
    lines = []
    for r in range(2):
        codes = lengthen(xm[10 * r], line).astype(jnp.int32)
        lines.append(summed_fields(tables, codes, [lengthen(xm[10 * r + 1 + c], line) for c in range(4)]))
    for k in range(SUMMED):
        near, far = line_sum(lines[0][k]), line_sum(lines[1][k])
        g0, g1 = 0.5 * far, wl1 * near
        for r, (g, b) in enumerate(((g0, near + g0), (g1, g1))):
            at = (2 * k + r) * line
            xw[at : at + line, :] = jnp.where(lane >= 1, roll_lanes(g, 1), 0.0) + (
                vl * roll_lanes(b, 2) + vu * b
            )
    for k in range(10):
        xl[k] = roll_lanes(xm[k], 1)

    def add(n):
        for k in range(SUMMED):
            beyond = xw[pl.ds(2 * k * line + n, ROWS, stride=line), :]
            sums[n, k] = sown[n, k] + jnp.where(row < 2, beyond, 0.0)

    def fill(n):
        for k in range(10):
            moved[n, k] = jnp.where(row < 1, xl[k, pl.ds(n, 1), :], pre[n, k])

    steps(0, levels + 1, add, 2)
    steps(0, levels, fill, 2)


def sweep_kernel(
    levels, sown, pre, ym, dm, codes, tables,
    gains, rests, message, codes_s,
    yv, ys, fs, rs, ss, ps, ms, qs, vs, total,
):
    first_x = lax.axis_index("lx") == 0
    first_y = lax.axis_index("ly") == 0
    row, lane = row_index(), lane_index()
    wl = jnp.where(first_x & (row == 1), 0.0, 0.5).astype(F32)
    wu = jnp.where(first_x & (row == 0), 0.0, 0.5).astype(F32)
    vl1 = jnp.where(first_y, 0.0, 0.5).astype(F32)
    even = lane % 2 == 0

    corner = [lengthen(dm[k], ROWS) for k in range(10)]
    for k in range(10):
        ys[k] = jnp.where(row < 1, roll_rows(corner[k], -1), roll_rows(ym[k], 1))
    side_u = summed_fields(tables, ym[0].astype(jnp.int32), [ym[1 + c] for c in range(4)])
    corner_u = summed_fields(tables, corner[0].astype(jnp.int32), corner[1:5])
    for k in range(SUMMED):
        one = jnp.where(row < 1, roll_rows(corner_u[k], -1), roll_rows(side_u[k], 1))
        two = jnp.where(row < 2, corner_u[k], roll_rows(side_u[k], 2))
        g = wl * two + wu * side_u[k]
        b = one + g
        summed = lane_sum(b)
        across = roll_lanes(g, -1) + 0.5 * (roll_lanes(g, 1) + roll_lanes(g, -3))
        yv[k] = jnp.where(even, across + 0.5 * summed, vl1 * summed)

    def shift(n):
        moved = [jnp.where(lane < 1, roll_lanes(ys[k], -2 * n - 1), pre[n, k]) for k in range(10)]
        codes_s[n] = moved[0].astype(jnp.int32)
        for c in range(4):
            fs[n + 1, c] = moved[1 + c]
            rs[n, c] = moved[5 + c]
        ss[n] = moved[9]

    for c in range(4):
        vs[0, c] = zero()
    for k in range(10):
        ms[0, k] = zero()

    def gather(n):
        for k in range(SUMMED):
            total[n, k] = sown[n, k] + jnp.where(lane < 2, roll_lanes(yv[k], -2 * n), 0.0)

    def assemble(n, last=False):
        sums = [total[n, k] for k in range(SUMMED)]
        act = activity(codes_s[n])
        half = 0.5 * act
        lateral = lookup(tables, 0, codes_s[n])
        below = [ms[n, k] for k in range(10)]
        if last:
            above = [zero() for _ in range(10)]
        else:
            both = half * activity(codes_s[n + 1])
            here = lookup(tables, 1, codes_s[n])
            there = lookup(tables, 1, codes_s[n + 1])
            above = [both * (here[k] + there[k]) for k in range(10)]
        block = []
        for k, (i, j) in enumerate(PAIRS):
            value = half * (lateral[k] * sums[0] + sums[1 + k]) + (below[k] + above[k])
            block.append(value + ss[n] if i == j else value)
        field = [fs[n + 1, c] for c in range(4)]
        if last:
            flux = [zero() for _ in range(4)]
        else:
            flux = apply_sym(above, [field[c] - fs[n + 2, c] for c in range(4)])
        flow = apply_sym(lateral, [sums[0] * field[c] - sums[11 + c] for c in range(4)])
        flow_back = apply_sym(sums[1:11], field)
        stored = ss[n]
        for c in range(4):
            out = half * (flow[c] + (flow_back[c] - sums[15 + c])) + (flux[c] - vs[n, c])
            qs[n, c] = act * (rs[n, c] - (stored * field[c] + out))
        for k in range(10):
            ms[n + 1, k] = above[k]
            ps[n, k] = block[k]
        for c in range(4):
            vs[n + 1, c] = flux[c]

    def eliminate(n, carry):
        coupled, carried = carry
        block = [ps[n, k] for k in range(10)]
        link = [ms[n + 1, k] for k in range(10)]
        value = [qs[n, c] + carried[c] for c in range(4)]
        inverse = invert([block[k] - coupled[k] for k in range(10)])
        gain = sym_product(inverse, link)
        rest = apply_sym(inverse, value)
        for i in range(4):
            rests[n, i] = rest[i]
            for j in range(4):
                gains[n, 4 * i + j] = gain[i][j]
        return back_product(link, gain), apply_sym(link, rest)

    for n in range(3):
        shift(n)
    for n in range(2):
        gather(n)
    assemble(0)

    def advance(n, carry):
        carry = eliminate(n, carry)
        assemble(n + 1)
        shift(n + 3)
        gather(n + 2)
        return carry

    zeros = [zero() for _ in range(10)]
    carry = lax.fori_loop(0, levels - 3, advance, (zeros, zeros[:4]))
    gather(levels - 1)
    gather(levels)
    carry = eliminate(levels - 3, carry)
    assemble(levels - 2)
    carry = eliminate(levels - 2, carry)
    assemble(levels - 1, True)
    coupled, carried = carry
    end_n = levels - 1
    for k in range(10):
        message[k] = ps[end_n, k] - coupled[k]
    for c in range(4):
        message[10 + c] = qs[end_n, c] + carried[c]
        message[33 + c] = fs[levels, c]
        message[56 + c] = rests[end_n - 1, c]
    for k in range(SUMMED):
        message[14 + k] = total[levels, k]
    message[37] = codes_s[end_n].astype(F32)
    message[38] = codes_s[end_n - 1].astype(F32)
    message[39] = codes[end_n].astype(F32)
    for k in range(16):
        message[40 + k] = gains[end_n - 1, k]


def back_kernel(levels, gains, rests, message, got, codes_s, tables, xs, kx, x3, y3, d3):
    lane = lane_index()
    planes = levels + 2

    def carry_on(gain, rest, x):
        out = []
        for i in range(4):
            out.append(
                rest[i] + ((gain[4 * i] * x[0] + gain[4 * i + 1] * x[1])
                           + (gain[4 * i + 2] * x[2] + gain[4 * i + 3] * x[3]))
            )
        return out

    def end_of(ref):
        code = ref[37].astype(jnp.int32)
        act = activity(code)
        part = lambda at, count: [ref[at + k] for k in range(count)]
        return code, act, part(0, 10), part(10, 4), part(14, SUMMED), part(33, 4)

    here, there = end_of(message), end_of(got)
    both = 0.5 * here[1] * there[1]
    link_here = lookup(tables, 1, here[0])
    link_there = lookup(tables, 1, there[0])
    link = [both * (link_here[k] + link_there[k]) for k in range(10)]

    def complete(one, other):
        code, act, block, value, _, field = one
        _, _, _, _, sums, field_there = other
        half = 0.5 * act
        lateral = lookup(tables, 0, code)
        added = [half * (lateral[k] * sums[0] + sums[1 + k]) + link[k] for k in range(10)]
        across = apply_sym(link, field_there)
        flow = apply_sym(lateral, sums[11:15])
        diagonal = apply_sym(added, field)
        full = [
            value[c] + act * ((across[c] + half * (flow[c] + sums[15 + c])) - diagonal[c])
            for c in range(4)
        ]
        return [block[k] + added[k] for k in range(10)], full

    block, value = complete(here, there)
    block_there, value_there = complete(there, here)
    inverse = invert(block_there)
    gain = sym_product(inverse, link)
    rest = apply_sym(inverse, value_there)
    coupled, carried = back_product(link, gain), apply_sym(link, rest)
    x = apply_sym(
        invert([block[k] - coupled[k] for k in range(10)]),
        [value[c] + carried[c] for c in range(4)],
    )
    x_met = carry_on([gain[i][j] for i in range(4) for j in range(4)], rest, x)
    x_far = carry_on([got[40 + k] for k in range(16)], [got[56 + c] for c in range(4)], x_met)
    for c in range(4):
        xs[levels - 1, c] = x[c]
        xs[levels, c] = x_met[c]
        xs[levels + 1, c] = x_far[c]

    def retreat(step, x):
        n = levels - 2 - step
        x = carry_on([gains[n, k] for k in range(16)], [rests[n, c] for c in range(4)], x)
        for c in range(4):
            xs[n, c] = x[c]
        return x

    lax.fori_loop(0, levels - 1, retreat, x)

    acc = [zero() for _ in range(8)]
    for n in range(planes):
        field = [xs[n, c] for c in range(4)]
        code = codes_s[n] if n < levels else got[37 + n - levels].astype(jnp.int32)
        act = activity(code)
        flow = [act * value for value in apply_sym(lookup(tables, 0, code), field)]
        for c in range(4):
            kx[n, c] = flow[c]
        for k, value in enumerate(field + [code.astype(F32)]):
            for r in range(2):
                at = (2 * k + r) * planes + n
                x3[at : at + 1, :] = value[r : r + 1]
        for k, value in enumerate(field + flow):
            acc[k] = jnp.where(lane // 2 == n, roll_lanes(value, 2 * n), acc[k])
    for k in range(8):
        y3[k] = acc[k]
        d3[k] = acc[k][0:2]


def own_back_kernel(levels, xs, kx, sown, pre):
    first_x = lax.axis_index("lx") == 0
    first_y = lax.axis_index("ly") == 0
    row, lane = row_index(), lane_index()
    wl = jnp.where(first_x & (row == 0), 0.0, 0.5).astype(F32)
    wu = jnp.where(row < 6, 0.5, 0.0).astype(F32)
    vl = jnp.where(first_y & (lane == 0), 0.0, 0.5).astype(F32)
    vu = jnp.where(lane < 126, 0.5, 0.0).astype(F32)

    def gather(n, first=False):
        for k in range(8):
            ref, c = (xs, k) if k < 4 else (kx, k - 4)
            outer = ref[n + 1, c] if first else ref[n - 1, c] + ref[n + 1, c]
            w = ref[n, c] + 0.5 * outer
            g = wl * w + wu * roll_rows(w, -2)
            b = jnp.where(row < 7, roll_rows(w, -1), 0.0) + g
            sown[n, k] = jnp.where(lane < 127, roll_lanes(g, -1), 0.0) + (vu * roll_lanes(b, -2) + vl * b)

    gather(0, True)
    steps(1, levels + 1, gather, 2)

    def shift(n):
        for c in range(4):
            pre[n, c] = roll_lanes(roll_rows(xs[n, c], -1), -1)

    steps(0, levels, shift, 4)


def line_back_kernel(levels, sown, pre, x3, tables, sums, moved, xw, xl):
    line = levels + PAD
    planes = levels + 2
    last_x = lax.axis_index("lx") == lax.axis_size("lx") - 1
    first_y = lax.axis_index("ly") == 0
    row = row_index()
    wu7 = jnp.where(last_x, 0.0, 0.5).astype(F32)
    lane = lax.broadcasted_iota(jnp.int32, (line, LANES), 1)
    vl = jnp.where(first_y & (lane == 0), 0.0, 0.5).astype(F32)
    vu = jnp.where(lane < 126, 0.5, 0.0).astype(F32)
    lines = []
    for r in range(2):
        parts = [
            lengthen(x3[(2 * k + r) * planes : (2 * k + r + 1) * planes, :], line) for k in range(5)
        ]
        codes = parts[4].astype(jnp.int32)
        act = activity(codes)
        flow = apply_sym(lookup(tables, 0, codes), parts[:4])
        lines.append(parts[:4] + [act * value for value in flow])
    for k in range(8):
        near, far = lines[0][k], lines[1][k]
        if k < 4:
            xl[k] = roll_lanes(near, -1)
        near, far = line_sum(near), line_sum(far)
        g6, g7 = 0.5 * near, wu7 * far
        for r, (g, b) in enumerate(((g6, g6), (g7, near + g7))):
            at = (2 * k + r + 6) * line
            xw[at : at + line, :] = jnp.where(lane < 127, roll_lanes(g, -1), 0.0) + (
                vu * roll_lanes(b, -2) + vl * b
            )

    def add(n):
        for k in range(8):
            beyond = xw[pl.ds(2 * k * line + n, ROWS, stride=line), :]
            sums[n, k] = sown[n, k] + jnp.where(row >= 6, beyond, 0.0)

    def fill(n):
        for c in range(4):
            moved[n, c] = jnp.where(row == 7, xl[c, pl.ds(n, 1), :], pre[n, c])

    steps(0, levels + 1, add, 4)
    steps(0, levels, fill, 4)


def finish_kernel(
    levels, sown, pre, y3, d3, it, codes, got, tables,
    updated, coarse, yv, ys, sm, up, co, sems,
):
    side = lax.axis_index("depth")
    first_x = lax.axis_index("lx") == 0
    last_y = lax.axis_index("ly") == lax.axis_size("ly") - 1
    last_x = lax.axis_index("lx") == lax.axis_size("lx") - 1
    row, lane = row_index(), lane_index()
    wl = jnp.where(first_x & (row == 0), 0.0, 0.5).astype(F32)
    wu = jnp.where(last_x & (row == 7), 0.0, 0.5).astype(F32)
    vu127 = jnp.where(last_y, 0.0, 0.5).astype(F32)
    even = lane % 2 == 0

    corner = [lengthen(d3[k], ROWS) for k in range(8)]
    for c in range(4):
        ys[c] = roll_rows(jnp.where(row < 1, corner[c], y3[c]), -1)

    def place(n):
        z = level_of(side, n, levels)
        for c in range(4):
            x = jnp.where(lane == 127, roll_lanes(ys[c], 127 - 2 * n), pre[n, c])
            up[z, c] = it[z, c] + x

    for n in range(levels):
        place(n)
    send_updated = pltpu.make_async_copy(up, updated, sems.at[0])
    send_updated.start()

    for k in range(8):
        two = roll_rows(jnp.where(row < 2, corner[k], y3[k]), -2)
        one = roll_rows(jnp.where(row < 1, corner[k], y3[k]), -1)
        g = wl * y3[k] + wu * two
        b = one + g
        summed = lane_sum(b)
        across = roll_lanes(g, 1) + 0.5 * (roll_lanes(g, -1) + roll_lanes(g, 3))
        yv[k] = jnp.where(even, 0.5 * summed, across + vu127 * summed)

    def smooth(n, code):
        sums = [
            sown[n, k] + jnp.where(lane >= 126, roll_lanes(yv[k], 126 - 2 * n), 0.0) for k in range(8)
        ]
        half = 0.5 * activity(code)
        flow = apply_sym(lookup(tables, 0, code), sums[:4])
        for c in range(4):
            sm[n + 1, c] = half * (flow[c] + sums[4 + c])

    for c in range(4):
        sm[0, c] = zero()
    for n in range(levels):
        smooth(n, codes[n])
    smooth(levels, got[39].astype(jnp.int32))

    step = 1 - 2 * side
    for k in range(levels // 2):
        at = side * (levels + 1) + step * 2 * k
        for c in range(4):
            co[k, c] = sm[at + step, c] + 0.5 * (sm[at, c] + sm[at + 2 * step, c])
    send_coarse = pltpu.make_async_copy(co, coarse, sems.at[1])
    send_coarse.start()
    send_updated.wait()
    send_coarse.wait()


def call(kernel, outs, *args, scratch=(), far_in=False, far_out=False):
    vmem = pl.BlockSpec(memory_space=pltpu.VMEM)
    if far_in:
        args = [pltpu.with_memory_space_constraint(x, pltpu.HBM) for x in args]
    far = pl.BlockSpec(memory_space=pltpu.HBM)
    return pl.pallas_call(
        kernel,
        out_shape=[jax.ShapeDtypeStruct(s, t) for s, t in outs],
        in_specs=[far if far_in else vmem] * len(args),
        out_specs=[far if far_out else vmem] * len(outs),
        scratch_shapes=list(scratch),
        compiler_params=pltpu.CompilerParams(vmem_limit_bytes=VMEM_LIMIT),
    )(*args)


def around(x, dx, dy):
    nx, ny = lax.axis_size("lx"), lax.axis_size("ly")
    pairs = [
        (i * ny + j, ((i + dx) % nx) * ny + (j + dy) % ny) for i in range(nx) for j in range(ny)
    ]
    return lax.ppermute(x, ("lx", "ly"), pairs)


def swap(x):
    return lax.ppermute(x, "depth", [(0, 1), (1, 0)])


def local(iterate, right_side, storage, zones, counts, materials):
    levels = zones.shape[0]
    line, planes = levels + PAD, levels + 2
    tile = (ROWS, LANES)
    vmem = lambda *shape: pltpu.VMEM(shape, F32)
    tables = jnp.broadcast_to(
        materials.transpose(0, 2, 3, 1).reshape(32, ROWS, 1), (32, ROWS, LANES)
    )
    it, rt, st, codes, xm = call(
        functools.partial(rows_kernel, levels),
        [((levels, 4) + tile, F32), ((levels, 4) + tile, F32), ((levels,) + tile, F32),
         ((levels,) + tile, jnp.int32),
         ((15, levels, LANES), F32)],
        iterate, right_side, storage, zones, counts,
        scratch=[
            pltpu.VMEM((levels,) + tile, jnp.int32), pltpu.VMEM(tile, jnp.int32),
            pltpu.SemaphoreType.DMA((5,)),
        ],
        far_in=True,
    )
    ym, dm = call(
        functools.partial(columns_kernel, levels),
        [((10,) + tile, F32), ((10, 2, LANES), F32)],
        it, rt, st, codes,
    )
    xm_in, ym_in, dm_in = around(xm, 1, 0), around(ym, 0, 1), around(dm, 1, 1)
    sown, pre = call(
        functools.partial(own_kernel, levels),
        [((levels + 1, SUMMED) + tile, F32), ((levels, 10) + tile, F32)],
        it, rt, st, codes, tables,
        scratch=[vmem(levels + 3, SUMMED, *tile)],
    )
    sums, moved = call(
        functools.partial(line_kernel, levels),
        [((levels + 1, SUMMED) + tile, F32), ((levels, 10) + tile, F32)],
        sown, pre, xm_in, tables,
        scratch=[vmem((2 * SUMMED + 12) * line, LANES), vmem(10, levels, LANES)],
    )
    gains, rests, message, codes_s = call(
        functools.partial(sweep_kernel, levels),
        [((levels - 1, 16) + tile, F32), ((levels - 1, 4) + tile, F32), ((MESSAGE,) + tile, F32),
         ((levels,) + tile, jnp.int32)],
        sums, moved, ym_in, dm_in, codes, tables,
        scratch=[
            vmem(SUMMED, *tile), vmem(10, *tile),
            vmem(planes, 4, *tile), vmem(levels, 4, *tile), vmem(levels, *tile),
            vmem(levels, 10, *tile), vmem(levels + 1, 10, *tile), vmem(levels, 4, *tile),
            vmem(levels + 1, 4, *tile), vmem(levels + 1, SUMMED, *tile),
        ],
    )
    got = swap(message)
    xs, kx, x3, y3, d3 = call(
        functools.partial(back_kernel, levels),
        [((planes, 4) + tile, F32), ((planes, 4) + tile, F32),
         ((10 * planes, LANES), F32), ((8,) + tile, F32), ((8, 2, LANES), F32)],
        gains, rests, message, got, codes_s, tables,
    )
    x3_in, y3_in, d3_in = around(x3, -1, 0), around(y3, 0, -1), around(d3, -1, -1)
    sown3, pre3 = call(
        functools.partial(own_back_kernel, levels),
        [((levels + 1, 8) + tile, F32), ((levels, 4) + tile, F32)],
        xs, kx,
    )
    sums3, moved3 = call(
        functools.partial(line_back_kernel, levels),
        [((levels + 1, 8) + tile, F32), ((levels, 4) + tile, F32)],
        sown3, pre3, x3_in, tables,
        scratch=[vmem((16 + 6) * line, LANES), vmem(4, line, LANES)],
    )
    updated, coarse = call(
        functools.partial(finish_kernel, levels),
        [((levels, 4) + tile, F32), ((levels // 2, 4) + tile, F32)],
        sums3, moved3, y3_in, d3_in, it, codes, got, tables,
        scratch=[
            vmem(8, *tile), vmem(4, *tile),
            vmem(levels + 2, 4, *tile), vmem(levels, 4, *tile), vmem(levels // 2, 4, *tile),
            pltpu.SemaphoreType.DMA((2,)),
        ],
        far_out=True,
    )
    return updated, coarse


def solution(mesh):
    placed = (
        P("depth", None, "lx", "ly"),
        P("depth", None, "lx", "ly"),
        P("depth", "lx", "ly"),
        P("depth", "lx", "ly"),
        P("lx", "ly"),
        P(),
    )
    return jax.shard_map(
        local,
        mesh=mesh,
        in_specs=placed,
        out_specs=(P("depth", None, "lx", "ly"), P("depth", None, "lx", "ly")),
        check_vma=False,
    )
```

```python
import functools

import jax
import jax.numpy as jnp
from jax import lax
from jax.experimental import pallas as pl
from jax.experimental.pallas import tpu as pltpu
from jax.sharding import PartitionSpec as P

PAIRS = [(i, j) for i in range(4) for j in range(i, 4)]
AT = {}
for _k, (_i, _j) in enumerate(PAIRS):
    AT[_i, _j] = AT[_j, _i] = _k

ROWS, LANES = 8, 128
SUMMED = 19
PAD = 8
MESSAGE = 60
F32 = jnp.float32
VMEM_LIMIT = 48 * 1024 * 1024


def row_index():
    return lax.broadcasted_iota(jnp.int32, (ROWS, LANES), 0)


def lane_index():
    return lax.broadcasted_iota(jnp.int32, (ROWS, LANES), 1)


def roll_rows(x, by):
    return pltpu.roll(x, by % x.shape[0], 0)


def roll_lanes(x, by):
    return pltpu.roll(x, by % LANES if isinstance(by, int) else lax.rem(by + LANES, LANES), 1)


def activity(codes):
    return jnp.where(codes > 0, 1.0, 0.0).astype(F32)


def lookup(tables, kind, codes):
    rows = jnp.maximum(codes - 1, 0)
    found = []
    for i, j in PAIRS:
        table = tables[kind * 16 + 4 * i + j]
        parts = [
            jnp.take_along_axis(table, rows[at : at + ROWS], axis=0, mode="promise_in_bounds")
            for at in range(0, rows.shape[0], ROWS)
        ]
        found.append(parts[0] if len(parts) == 1 else jnp.concatenate(parts, axis=0))
    return found


def apply_sym(matrix, vector):
    out = []
    for i in range(4):
        total = matrix[AT[i, 0]] * vector[0]
        for j in range(1, 4):
            total = total + matrix[AT[i, j]] * vector[j]
        out.append(total)
    return out


def summed_fields(tables, codes, field):
    act = activity(codes)
    lateral = [act * value for value in lookup(tables, 0, codes)]
    return [act] + lateral + [act * v for v in field] + apply_sym(lateral, field)


def level_of(side, n, levels):
    return side * (levels - 1) + (1 - 2 * side) * n


def steps(first, last, body, width=1):
    passes = (last - first) // width

    def one(i, carry):
        for j in range(width):
            body(first + i * width + j)
        return carry

    lax.fori_loop(0, passes, one, 0)
    for n in range(first + passes * width, last):
        body(n)


def zero():
    return jnp.zeros((ROWS, LANES), F32)


def rows_kernel(
    levels, iterate, right, storage, zones, counts,
    it, rt, st, codes_out, xm, zones_v, counts_v, sems,
):
    side = lax.axis_index("depth")
    copies = [
        pltpu.make_async_copy(source, target, sems.at[k])
        for k, (source, target) in enumerate(
            [(zones, zones_v), (counts, counts_v), (iterate, it), (right, rt), (storage, st)]
        )
    ]
    for copy in copies:
        copy.start()
    for copy in copies:
        copy.wait()
    limit = counts_v[...] - side * levels
    for n in range(levels):
        z = level_of(side, n, levels)
        code = jnp.where(z < limit, zones_v[z] + 1, 0)
        codes_out[n] = code
        fields = [code.astype(F32)] + [it[z, c] for c in range(4)]
        fields += [rt[z, c] for c in range(4)] + [st[z]]
        for k, value in enumerate(fields):
            xm[k, n : n + 1, :] = value[7:8]
            if k < 5:
                xm[10 + k, n : n + 1, :] = value[6:7]


def columns_kernel(levels, it, rt, st, codes, ym, dm):
    side = lax.axis_index("depth")
    lane = lane_index()
    acc = [zero() for _ in range(10)]
    for n in range(levels):
        z = level_of(side, n, levels)
        fields = [codes[n].astype(F32)] + [it[z, c] for c in range(4)]
        fields += [rt[z, c] for c in range(4)] + [st[z]]
        for k, value in enumerate(fields):
            acc[k] = jnp.where(lane // 2 == n, roll_lanes(value, 2 * n + 2), acc[k])
    for k in range(10):
        ym[k] = acc[k]
        dm[k] = acc[k][6:8]


def own_kernel(levels, it, rt, st, codes, tables, sown, pre, u):
    side = lax.axis_index("depth")
    first_x = lax.axis_index("lx") == 0
    first_y = lax.axis_index("ly") == 0
    row, lane = row_index(), lane_index()
    wl = jnp.where(row >= 2, 0.5, 0.0).astype(F32)
    wu = jnp.where(first_x & (row == 0), 0.0, 0.5).astype(F32)
    vl = jnp.where(lane >= 2, 0.5, 0.0).astype(F32)
    vu = jnp.where(first_y & (lane == 0), 0.0, 0.5).astype(F32)
    for k in range(SUMMED):
        u[0, k] = zero()
        u[levels + 1, k] = zero()
        u[levels + 2, k] = zero()

    def fill(n):
        z = level_of(side, n, levels)
        field = [it[z, c] for c in range(4)]
        for k, value in enumerate(summed_fields(tables, codes[n], field)):
            u[n + 1, k] = value

    steps(0, levels, fill, 2)

    def shift(n):
        z = level_of(side, n, levels)
        fields = [codes[n].astype(F32)] + [it[z, c] for c in range(4)]
        fields += [rt[z, c] for c in range(4)] + [st[z]]
        for k, value in enumerate(fields):
            pre[n, k] = roll_lanes(roll_rows(value, 1), 1)

    steps(0, levels, shift, 4)

    def gather(n):
        for k in range(SUMMED):
            w = u[n + 1, k] + 0.5 * (u[n, k] + u[n + 2, k])
            g = wl * roll_rows(w, 2) + wu * w
            b = jnp.where(row >= 1, roll_rows(w, 1), 0.0) + g
            sown[n, k] = jnp.where(lane >= 1, roll_lanes(g, 1), 0.0) + (vl * roll_lanes(b, 2) + vu * b)

    steps(0, levels + 1, gather, 4)


def factor(m):
    rows = {(i, j): m[AT[i, j]] for i in range(4) for j in range(i + 1)}
    lower, inverse = {}, []
    for p in range(4):
        inverse.append(1.0 / rows[p, p])
        for i in range(p + 1, 4):
            lower[i, p] = rows[i, p] * inverse[p]
        for i in range(p + 1, 4):
            for j in range(p + 1, i + 1):
                rows[i, j] = rows[i, j] - lower[i, p] * rows[j, p]
    return lower, inverse


def forward(lower, column):
    out = []
    for i in range(4):
        value = column[i]
        for p in range(i):
            value = value - lower[i, p] * out[p]
        out.append(value)
    return out


def backward(lower, column):
    out = list(column)
    for i in (2, 1, 0):
        for p in range(3, i, -1):
            out[i] = out[i] - lower[p, i] * out[p]
    return out


def dot(a, b):
    return (a[0] * b[0] + a[1] * b[1]) + (a[2] * b[2] + a[3] * b[3])


def reduce_block(block, value, link):
    lower, inverse = factor(block)
    columns = [forward(lower, [link[AT[i, j]] for i in range(4)]) for j in range(4)]
    scaled = [[columns[j][i] * inverse[i] for i in range(4)] for j in range(4)]
    first = forward(lower, value)
    coupled = [dot(columns[i], scaled[j]) for i, j in PAIRS]
    carried = [dot(scaled[i], first) for i in range(4)]
    gain = [backward(lower, scaled[j]) for j in range(4)]
    rest = backward(lower, [first[i] * inverse[i] for i in range(4)])
    return [[gain[j][i] for j in range(4)] for i in range(4)], rest, coupled, carried


def solve_block(block, value):
    lower, inverse = factor(block)
    first = forward(lower, value)
    return backward(lower, [first[i] * inverse[i] for i in range(4)])


def line_sum(values):
    return values + 0.5 * (roll_rows(values, 1) + roll_rows(values, -1))


def lane_sum(values):
    return values + 0.5 * (roll_lanes(values, 2) + roll_lanes(values, -2))


def lengthen(values, rows):
    return jnp.concatenate([values, jnp.zeros((rows - values.shape[0], LANES), F32)], axis=0)


def line_kernel(levels, sown, pre, xm, tables, sums, moved, xw, xl):
    line = levels + PAD
    first_x = lax.axis_index("lx") == 0
    first_y = lax.axis_index("ly") == 0
    row = row_index()
    wl1 = jnp.where(first_x, 0.0, 0.5).astype(F32)
    lane = lax.broadcasted_iota(jnp.int32, (line, LANES), 1)
    vl = jnp.where(lane >= 2, 0.5, 0.0).astype(F32)
    vu = jnp.where(first_y & (lane == 0), 0.0, 0.5).astype(F32)
    lines = []
    for r in range(2):
        codes = lengthen(xm[10 * r], line).astype(jnp.int32)
        lines.append(summed_fields(tables, codes, [lengthen(xm[10 * r + 1 + c], line) for c in range(4)]))
    for k in range(SUMMED):
        near, far = line_sum(lines[0][k]), line_sum(lines[1][k])
        g0, g1 = 0.5 * far, wl1 * near
        for r, (g, b) in enumerate(((g0, near + g0), (g1, g1))):
            at = (2 * k + r) * line
            xw[at : at + line, :] = jnp.where(lane >= 1, roll_lanes(g, 1), 0.0) + (
                vl * roll_lanes(b, 2) + vu * b
            )
    for k in range(10):
        xl[k] = roll_lanes(xm[k], 1)

    def add(n):
        for k in range(SUMMED):
            beyond = xw[pl.ds(2 * k * line + n, ROWS, stride=line), :]
            sums[n, k] = sown[n, k] + jnp.where(row < 2, beyond, 0.0)

    def fill(n):
        for k in range(10):
            moved[n, k] = jnp.where(row < 1, xl[k, pl.ds(n, 1), :], pre[n, k])

    steps(0, levels + 1, add, 2)
    steps(0, levels, fill, 2)


def sweep_kernel(
    levels, sown, pre, ym, dm, codes, tables,
    gains, rests, message, codes_s,
    yv, ys, fs, rs, ss, ps, ms, qs, vs, total,
):
    first_x = lax.axis_index("lx") == 0
    first_y = lax.axis_index("ly") == 0
    row, lane = row_index(), lane_index()
    wl = jnp.where(first_x & (row == 1), 0.0, 0.5).astype(F32)
    wu = jnp.where(first_x & (row == 0), 0.0, 0.5).astype(F32)
    vl1 = jnp.where(first_y, 0.0, 0.5).astype(F32)
    even = lane % 2 == 0

    corner = [lengthen(dm[k], ROWS) for k in range(10)]
    for k in range(10):
        ys[k] = jnp.where(row < 1, roll_rows(corner[k], -1), roll_rows(ym[k], 1))
    side_u = summed_fields(tables, ym[0].astype(jnp.int32), [ym[1 + c] for c in range(4)])
    corner_u = summed_fields(tables, corner[0].astype(jnp.int32), corner[1:5])
    for k in range(SUMMED):
        one = jnp.where(row < 1, roll_rows(corner_u[k], -1), roll_rows(side_u[k], 1))
        two = jnp.where(row < 2, corner_u[k], roll_rows(side_u[k], 2))
        g = wl * two + wu * side_u[k]
        b = one + g
        summed = lane_sum(b)
        across = roll_lanes(g, -1) + 0.5 * (roll_lanes(g, 1) + roll_lanes(g, -3))
        yv[k] = jnp.where(even, across + 0.5 * summed, vl1 * summed)

    def shift(n):
        moved = [jnp.where(lane < 1, roll_lanes(ys[k], -2 * n - 1), pre[n, k]) for k in range(10)]
        codes_s[n] = moved[0].astype(jnp.int32)
        for c in range(4):
            fs[n + 1, c] = moved[1 + c]
            rs[n, c] = moved[5 + c]
        ss[n] = moved[9]

    for c in range(4):
        vs[0, c] = zero()
    for k in range(10):
        ms[0, k] = zero()

    def gather(n):
        for k in range(SUMMED):
            total[n, k] = sown[n, k] + jnp.where(lane < 2, roll_lanes(yv[k], -2 * n), 0.0)

    def assemble(n, last=False):
        sums = [total[n, k] for k in range(SUMMED)]
        act = activity(codes_s[n])
        half = 0.5 * act
        lateral = lookup(tables, 0, codes_s[n])
        below = [ms[n, k] for k in range(10)]
        if last:
            above = [zero() for _ in range(10)]
        else:
            both = half * activity(codes_s[n + 1])
            here = lookup(tables, 1, codes_s[n])
            there = lookup(tables, 1, codes_s[n + 1])
            above = [both * (here[k] + there[k]) for k in range(10)]
        block = []
        for k, (i, j) in enumerate(PAIRS):
            value = half * (lateral[k] * sums[0] + sums[1 + k]) + (below[k] + above[k])
            block.append(value + ss[n] if i == j else value)
        field = [fs[n + 1, c] for c in range(4)]
        if last:
            flux = [zero() for _ in range(4)]
        else:
            flux = apply_sym(above, [field[c] - fs[n + 2, c] for c in range(4)])
        flow = apply_sym(lateral, [sums[0] * field[c] - sums[11 + c] for c in range(4)])
        flow_back = apply_sym(sums[1:11], field)
        stored = ss[n]
        for c in range(4):
            out = half * (flow[c] + (flow_back[c] - sums[15 + c])) + (flux[c] - vs[n, c])
            qs[n, c] = act * (rs[n, c] - (stored * field[c] + out))
        for k in range(10):
            ms[n + 1, k] = above[k]
            ps[n, k] = block[k]
        for c in range(4):
            vs[n + 1, c] = flux[c]

    def eliminate(n, carry):
        coupled, carried = carry
        block = [ps[n, k] for k in range(10)]
        link = [ms[n + 1, k] for k in range(10)]
        value = [qs[n, c] + carried[c] for c in range(4)]
        gain, rest, coupled, carried = reduce_block(
            [block[k] - coupled[k] for k in range(10)], value, link
        )
        for i in range(4):
            rests[n, i] = rest[i]
            for j in range(4):
                gains[n, 4 * i + j] = gain[i][j]
        return coupled, carried

    for n in range(3):
        shift(n)
    for n in range(2):
        gather(n)
    assemble(0)

    def advance(n, carry):
        carry = eliminate(n, carry)
        assemble(n + 1)
        shift(n + 3)
        gather(n + 2)
        return carry

    zeros = [zero() for _ in range(10)]
    carry = lax.fori_loop(
        0, (levels - 3) // 2, lambda i, c: advance(2 * i + 1, advance(2 * i, c)), (zeros, zeros[:4])
    )
    carry = advance(levels - 4, carry)
    gather(levels - 1)
    gather(levels)
    carry = eliminate(levels - 3, carry)
    assemble(levels - 2)
    carry = eliminate(levels - 2, carry)
    assemble(levels - 1, True)
    coupled, carried = carry
    end_n = levels - 1
    for k in range(10):
        message[k] = ps[end_n, k] - coupled[k]
    for c in range(4):
        message[10 + c] = qs[end_n, c] + carried[c]
        message[33 + c] = fs[levels, c]
        message[56 + c] = rests[end_n - 1, c]
    for k in range(SUMMED):
        message[14 + k] = total[levels, k]
    message[37] = codes_s[end_n].astype(F32)
    message[38] = codes_s[end_n - 1].astype(F32)
    message[39] = codes[end_n].astype(F32)
    for k in range(16):
        message[40 + k] = gains[end_n - 1, k]


def back_kernel(levels, gains, rests, message, got, codes_s, tables, xs, kx, x3, y3, d3):
    lane = lane_index()
    planes = levels + 2

    def carry_on(gain, rest, x):
        out = []
        for i in range(4):
            out.append(
                rest[i] + ((gain[4 * i] * x[0] + gain[4 * i + 1] * x[1])
                           + (gain[4 * i + 2] * x[2] + gain[4 * i + 3] * x[3]))
            )
        return out

    def end_of(ref):
        code = ref[37].astype(jnp.int32)
        act = activity(code)
        part = lambda at, count: [ref[at + k] for k in range(count)]
        return code, act, part(0, 10), part(10, 4), part(14, SUMMED), part(33, 4)

    here, there = end_of(message), end_of(got)
    both = 0.5 * here[1] * there[1]
    link_here = lookup(tables, 1, here[0])
    link_there = lookup(tables, 1, there[0])
    link = [both * (link_here[k] + link_there[k]) for k in range(10)]

    def complete(one, other):
        code, act, block, value, _, field = one
        _, _, _, _, sums, field_there = other
        half = 0.5 * act
        lateral = lookup(tables, 0, code)
        added = [half * (lateral[k] * sums[0] + sums[1 + k]) + link[k] for k in range(10)]
        across = apply_sym(link, field_there)
        flow = apply_sym(lateral, sums[11:15])
        diagonal = apply_sym(added, field)
        full = [
            value[c] + act * ((across[c] + half * (flow[c] + sums[15 + c])) - diagonal[c])
            for c in range(4)
        ]
        return [block[k] + added[k] for k in range(10)], full

    block, value = complete(here, there)
    block_there, value_there = complete(there, here)
    gain, rest, coupled, carried = reduce_block(block_there, value_there, link)
    x = solve_block(
        [block[k] - coupled[k] for k in range(10)], [value[c] + carried[c] for c in range(4)]
    )
    x_met = carry_on([gain[i][j] for i in range(4) for j in range(4)], rest, x)
    x_far = carry_on([got[40 + k] for k in range(16)], [got[56 + c] for c in range(4)], x_met)
    for c in range(4):
        xs[levels - 1, c] = x[c]
        xs[levels, c] = x_met[c]
        xs[levels + 1, c] = x_far[c]

    def retreat(step, x):
        n = levels - 2 - step
        x = carry_on([gains[n, k] for k in range(16)], [rests[n, c] for c in range(4)], x)
        for c in range(4):
            xs[n, c] = x[c]
        return x

    lax.fori_loop(0, levels - 1, retreat, x)

    acc = [zero() for _ in range(8)]
    for n in range(planes):
        field = [xs[n, c] for c in range(4)]
        code = codes_s[n] if n < levels else got[37 + n - levels].astype(jnp.int32)
        act = activity(code)
        flow = [act * value for value in apply_sym(lookup(tables, 0, code), field)]
        for c in range(4):
            kx[n, c] = flow[c]
        for k, value in enumerate(field + [code.astype(F32)]):
            for r in range(2):
                at = (2 * k + r) * planes + n
                x3[at : at + 1, :] = value[r : r + 1]
        for k, value in enumerate(field + flow):
            acc[k] = jnp.where(lane // 2 == n, roll_lanes(value, 2 * n), acc[k])
    for k in range(8):
        y3[k] = acc[k]
        d3[k] = acc[k][0:2]


def own_back_kernel(levels, xs, kx, sown, pre):
    first_x = lax.axis_index("lx") == 0
    first_y = lax.axis_index("ly") == 0
    row, lane = row_index(), lane_index()
    wl = jnp.where(first_x & (row == 0), 0.0, 0.5).astype(F32)
    wu = jnp.where(row < 6, 0.5, 0.0).astype(F32)
    vl = jnp.where(first_y & (lane == 0), 0.0, 0.5).astype(F32)
    vu = jnp.where(lane < 126, 0.5, 0.0).astype(F32)

    def gather(n, first=False):
        for k in range(8):
            ref, c = (xs, k) if k < 4 else (kx, k - 4)
            outer = ref[n + 1, c] if first else ref[n - 1, c] + ref[n + 1, c]
            w = ref[n, c] + 0.5 * outer
            g = wl * w + wu * roll_rows(w, -2)
            b = jnp.where(row < 7, roll_rows(w, -1), 0.0) + g
            sown[n, k] = jnp.where(lane < 127, roll_lanes(g, -1), 0.0) + (vu * roll_lanes(b, -2) + vl * b)

    gather(0, True)
    steps(1, levels + 1, gather, 2)

    def shift(n):
        for c in range(4):
            pre[n, c] = roll_lanes(roll_rows(xs[n, c], -1), -1)

    steps(0, levels, shift, 4)


def line_back_kernel(levels, sown, pre, x3, tables, sums, moved, xw, xl):
    line = levels + PAD
    planes = levels + 2
    last_x = lax.axis_index("lx") == lax.axis_size("lx") - 1
    first_y = lax.axis_index("ly") == 0
    row = row_index()
    wu7 = jnp.where(last_x, 0.0, 0.5).astype(F32)
    lane = lax.broadcasted_iota(jnp.int32, (line, LANES), 1)
    vl = jnp.where(first_y & (lane == 0), 0.0, 0.5).astype(F32)
    vu = jnp.where(lane < 126, 0.5, 0.0).astype(F32)
    lines = []
    for r in range(2):
        parts = [
            lengthen(x3[(2 * k + r) * planes : (2 * k + r + 1) * planes, :], line) for k in range(5)
        ]
        codes = parts[4].astype(jnp.int32)
        act = activity(codes)
        flow = apply_sym(lookup(tables, 0, codes), parts[:4])
        lines.append(parts[:4] + [act * value for value in flow])
    for k in range(8):
        near, far = lines[0][k], lines[1][k]
        if k < 4:
            xl[k] = roll_lanes(near, -1)
        near, far = line_sum(near), line_sum(far)
        g6, g7 = 0.5 * near, wu7 * far
        for r, (g, b) in enumerate(((g6, g6), (g7, near + g7))):
            at = (2 * k + r + 6) * line
            xw[at : at + line, :] = jnp.where(lane < 127, roll_lanes(g, -1), 0.0) + (
                vu * roll_lanes(b, -2) + vl * b
            )

    def add(n):
        for k in range(8):
            beyond = xw[pl.ds(2 * k * line + n, ROWS, stride=line), :]
            sums[n, k] = sown[n, k] + jnp.where(row >= 6, beyond, 0.0)

    def fill(n):
        for c in range(4):
            moved[n, c] = jnp.where(row == 7, xl[c, pl.ds(n, 1), :], pre[n, c])

    steps(0, levels + 1, add, 4)
    steps(0, levels, fill, 4)


def finish_kernel(
    levels, sown, pre, y3, d3, it, codes, got, tables,
    updated, coarse, yv, ys, sm, up, co, sems,
):
    side = lax.axis_index("depth")
    first_x = lax.axis_index("lx") == 0
    last_y = lax.axis_index("ly") == lax.axis_size("ly") - 1
    last_x = lax.axis_index("lx") == lax.axis_size("lx") - 1
    row, lane = row_index(), lane_index()
    wl = jnp.where(first_x & (row == 0), 0.0, 0.5).astype(F32)
    wu = jnp.where(last_x & (row == 7), 0.0, 0.5).astype(F32)
    vu127 = jnp.where(last_y, 0.0, 0.5).astype(F32)
    even = lane % 2 == 0

    corner = [lengthen(d3[k], ROWS) for k in range(8)]
    for c in range(4):
        ys[c] = roll_rows(jnp.where(row < 1, corner[c], y3[c]), -1)

    def place(n):
        z = level_of(side, n, levels)
        for c in range(4):
            x = jnp.where(lane == 127, roll_lanes(ys[c], 127 - 2 * n), pre[n, c])
            up[z, c] = it[z, c] + x

    for n in range(levels):
        place(n)
    send_updated = pltpu.make_async_copy(up, updated, sems.at[0])
    send_updated.start()

    for k in range(8):
        two = roll_rows(jnp.where(row < 2, corner[k], y3[k]), -2)
        one = roll_rows(jnp.where(row < 1, corner[k], y3[k]), -1)
        g = wl * y3[k] + wu * two
        b = one + g
        summed = lane_sum(b)
        across = roll_lanes(g, 1) + 0.5 * (roll_lanes(g, -1) + roll_lanes(g, 3))
        yv[k] = jnp.where(even, 0.5 * summed, across + vu127 * summed)

    def smooth(n, code):
        sums = [
            sown[n, k] + jnp.where(lane >= 126, roll_lanes(yv[k], 126 - 2 * n), 0.0) for k in range(8)
        ]
        half = 0.5 * activity(code)
        flow = apply_sym(lookup(tables, 0, code), sums[:4])
        for c in range(4):
            sm[n + 1, c] = half * (flow[c] + sums[4 + c])

    for c in range(4):
        sm[0, c] = zero()
    for n in range(levels):
        smooth(n, codes[n])
    smooth(levels, got[39].astype(jnp.int32))

    step = 1 - 2 * side
    for k in range(levels // 2):
        at = side * (levels + 1) + step * 2 * k
        for c in range(4):
            co[k, c] = sm[at + step, c] + 0.5 * (sm[at, c] + sm[at + 2 * step, c])
    send_coarse = pltpu.make_async_copy(co, coarse, sems.at[1])
    send_coarse.start()
    send_updated.wait()
    send_coarse.wait()


def call(kernel, outs, *args, scratch=(), far_in=False, far_out=False):
    vmem = pl.BlockSpec(memory_space=pltpu.VMEM)
    if far_in:
        args = [pltpu.with_memory_space_constraint(x, pltpu.HBM) for x in args]
    far = pl.BlockSpec(memory_space=pltpu.HBM)
    return pl.pallas_call(
        kernel,
        out_shape=[jax.ShapeDtypeStruct(s, t) for s, t in outs],
        in_specs=[far if far_in else vmem] * len(args),
        out_specs=[far if far_out else vmem] * len(outs),
        scratch_shapes=list(scratch),
        compiler_params=pltpu.CompilerParams(vmem_limit_bytes=VMEM_LIMIT),
    )(*args)


def around(x, dx, dy):
    nx, ny = lax.axis_size("lx"), lax.axis_size("ly")
    pairs = [
        (i * ny + j, ((i + dx) % nx) * ny + (j + dy) % ny) for i in range(nx) for j in range(ny)
    ]
    return lax.ppermute(x, ("lx", "ly"), pairs)


def swap(x):
    return lax.ppermute(x, "depth", [(0, 1), (1, 0)])


def local(iterate, right_side, storage, zones, counts, materials):
    levels = zones.shape[0]
    line, planes = levels + PAD, levels + 2
    tile = (ROWS, LANES)
    vmem = lambda *shape: pltpu.VMEM(shape, F32)
    tables = jnp.broadcast_to(
        materials.transpose(0, 2, 3, 1).reshape(32, ROWS, 1), (32, ROWS, LANES)
    )
    it, rt, st, codes, xm = call(
        functools.partial(rows_kernel, levels),
        [((levels, 4) + tile, F32), ((levels, 4) + tile, F32), ((levels,) + tile, F32),
         ((levels,) + tile, jnp.int32),
         ((15, levels, LANES), F32)],
        iterate, right_side, storage, zones, counts,
        scratch=[
            pltpu.VMEM((levels,) + tile, jnp.int32), pltpu.VMEM(tile, jnp.int32),
            pltpu.SemaphoreType.DMA((5,)),
        ],
        far_in=True,
    )
    ym, dm = call(
        functools.partial(columns_kernel, levels),
        [((10,) + tile, F32), ((10, 2, LANES), F32)],
        it, rt, st, codes,
    )
    xm_in, ym_in, dm_in = around(xm, 1, 0), around(ym, 0, 1), around(dm, 1, 1)
    sown, pre = call(
        functools.partial(own_kernel, levels),
        [((levels + 1, SUMMED) + tile, F32), ((levels, 10) + tile, F32)],
        it, rt, st, codes, tables,
        scratch=[vmem(levels + 3, SUMMED, *tile)],
    )
    sums, moved = call(
        functools.partial(line_kernel, levels),
        [((levels + 1, SUMMED) + tile, F32), ((levels, 10) + tile, F32)],
        sown, pre, xm_in, tables,
        scratch=[vmem((2 * SUMMED + 12) * line, LANES), vmem(10, levels, LANES)],
    )
    gains, rests, message, codes_s = call(
        functools.partial(sweep_kernel, levels),
        [((levels - 1, 16) + tile, F32), ((levels - 1, 4) + tile, F32), ((MESSAGE,) + tile, F32),
         ((levels,) + tile, jnp.int32)],
        sums, moved, ym_in, dm_in, codes, tables,
        scratch=[
            vmem(SUMMED, *tile), vmem(10, *tile),
            vmem(planes, 4, *tile), vmem(levels, 4, *tile), vmem(levels, *tile),
            vmem(levels, 10, *tile), vmem(levels + 1, 10, *tile), vmem(levels, 4, *tile),
            vmem(levels + 1, 4, *tile), vmem(levels + 1, SUMMED, *tile),
        ],
    )
    got = swap(message)
    xs, kx, x3, y3, d3 = call(
        functools.partial(back_kernel, levels),
        [((planes, 4) + tile, F32), ((planes, 4) + tile, F32),
         ((10 * planes, LANES), F32), ((8,) + tile, F32), ((8, 2, LANES), F32)],
        gains, rests, message, got, codes_s, tables,
    )
    x3_in, y3_in, d3_in = around(x3, -1, 0), around(y3, 0, -1), around(d3, -1, -1)
    sown3, pre3 = call(
        functools.partial(own_back_kernel, levels),
        [((levels + 1, 8) + tile, F32), ((levels, 4) + tile, F32)],
        xs, kx,
    )
    sums3, moved3 = call(
        functools.partial(line_back_kernel, levels),
        [((levels + 1, 8) + tile, F32), ((levels, 4) + tile, F32)],
        sown3, pre3, x3_in, tables,
        scratch=[vmem((16 + 6) * line, LANES), vmem(4, line, LANES)],
    )
    updated, coarse = call(
        functools.partial(finish_kernel, levels),
        [((levels, 4) + tile, F32), ((levels // 2, 4) + tile, F32)],
        sums3, moved3, y3_in, d3_in, it, codes, got, tables,
        scratch=[
            vmem(8, *tile), vmem(4, *tile),
            vmem(levels + 2, 4, *tile), vmem(levels, 4, *tile), vmem(levels // 2, 4, *tile),
            pltpu.SemaphoreType.DMA((2,)),
        ],
        far_out=True,
    )
    return updated, coarse


def solution(mesh):
    placed = (
        P("depth", None, "lx", "ly"),
        P("depth", None, "lx", "ly"),
        P("depth", "lx", "ly"),
        P("depth", "lx", "ly"),
        P("lx", "ly"),
        P(),
    )
    return jax.shard_map(
        local,
        mesh=mesh,
        in_specs=placed,
        out_specs=(P("depth", None, "lx", "ly"), P("depth", None, "lx", "ly")),
        check_vma=False,
    )
```

```python
import functools

import jax
import jax.numpy as jnp
from jax import lax
from jax.experimental import pallas as pl
from jax.experimental.pallas import tpu as pltpu
from jax.sharding import PartitionSpec as P

PAIRS = [(i, j) for i in range(4) for j in range(i, 4)]
AT = {}
for _k, (_i, _j) in enumerate(PAIRS):
    AT[_i, _j] = AT[_j, _i] = _k

ROWS, LANES = 8, 128
SUMMED = 19
PAD = 8
MESSAGE = 60
F32 = jnp.float32
VMEM_LIMIT = 48 * 1024 * 1024


def row_index():
    return lax.broadcasted_iota(jnp.int32, (ROWS, LANES), 0)


def lane_index():
    return lax.broadcasted_iota(jnp.int32, (ROWS, LANES), 1)


def roll_rows(x, by):
    return pltpu.roll(x, by % x.shape[0], 0)


def roll_lanes(x, by):
    return pltpu.roll(x, by % LANES if isinstance(by, int) else lax.rem(by + LANES, LANES), 1)


def activity(codes):
    return jnp.where(codes > 0, 1.0, 0.0).astype(F32)


def lookup(tables, kind, codes):
    rows = jnp.maximum(codes - 1, 0)
    found = []
    for i, j in PAIRS:
        table = tables[kind * 16 + 4 * i + j]
        parts = [
            jnp.take_along_axis(table, rows[at : at + ROWS], axis=0, mode="promise_in_bounds")
            for at in range(0, rows.shape[0], ROWS)
        ]
        found.append(parts[0] if len(parts) == 1 else jnp.concatenate(parts, axis=0))
    return found


def apply_sym(matrix, vector):
    out = []
    for i in range(4):
        total = matrix[AT[i, 0]] * vector[0]
        for j in range(1, 4):
            total = total + matrix[AT[i, j]] * vector[j]
        out.append(total)
    return out


def summed_fields(tables, codes, field):
    act = activity(codes)
    lateral = [act * value for value in lookup(tables, 0, codes)]
    return [act] + lateral + [act * v for v in field] + apply_sym(lateral, field)


def level_of(side, n, levels):
    return side * (levels - 1) + (1 - 2 * side) * n


def steps(first, last, body, width=1):
    passes = (last - first) // width

    def one(i, carry):
        for j in range(width):
            body(first + i * width + j)
        return carry

    lax.fori_loop(0, passes, one, 0)
    for n in range(first + passes * width, last):
        body(n)


def zero():
    return jnp.zeros((ROWS, LANES), F32)


def rows_kernel(
    levels, iterate, right, storage, zones, counts,
    it, rt, st, codes_out, xm, zones_v, counts_v, sems,
):
    side = lax.axis_index("depth")
    copies = [
        pltpu.make_async_copy(source, target, sems.at[k])
        for k, (source, target) in enumerate(
            [(zones, zones_v), (counts, counts_v), (iterate, it), (right, rt), (storage, st)]
        )
    ]
    for copy in copies:
        copy.start()
    for copy in copies:
        copy.wait()
    limit = counts_v[...] - side * levels
    for n in range(levels):
        z = level_of(side, n, levels)
        code = jnp.where(z < limit, zones_v[z] + 1, 0)
        codes_out[n] = code
        fields = [code.astype(F32)] + [it[z, c] for c in range(4)]
        fields += [rt[z, c] for c in range(4)] + [st[z]]
        for k, value in enumerate(fields):
            xm[k, n : n + 1, :] = value[7:8]
            if k < 5:
                xm[10 + k, n : n + 1, :] = value[6:7]


def columns_kernel(levels, it, rt, st, codes, ym, dm):
    side = lax.axis_index("depth")
    lane = lane_index()
    acc = [zero() for _ in range(10)]
    for n in range(levels):
        z = level_of(side, n, levels)
        fields = [codes[n].astype(F32)] + [it[z, c] for c in range(4)]
        fields += [rt[z, c] for c in range(4)] + [st[z]]
        for k, value in enumerate(fields):
            acc[k] = jnp.where(lane // 2 == n, roll_lanes(value, 2 * n + 2), acc[k])
    for k in range(10):
        ym[k] = acc[k]
        dm[k] = acc[k][6:8]


def own_kernel(levels, it, rt, st, codes, tables, sown, pre, u):
    side = lax.axis_index("depth")
    first_x = lax.axis_index("lx") == 0
    first_y = lax.axis_index("ly") == 0
    row, lane = row_index(), lane_index()
    wl = jnp.where(row >= 2, 0.5, 0.0).astype(F32)
    wu = jnp.where(first_x & (row == 0), 0.0, 0.5).astype(F32)
    vl = jnp.where(lane >= 2, 0.5, 0.0).astype(F32)
    vu = jnp.where(first_y & (lane == 0), 0.0, 0.5).astype(F32)
    for k in range(SUMMED):
        u[0, k] = zero()
        u[levels + 1, k] = zero()
        u[levels + 2, k] = zero()

    def fill(n):
        z = level_of(side, n, levels)
        field = [it[z, c] for c in range(4)]
        for k, value in enumerate(summed_fields(tables, codes[n], field)):
            u[n + 1, k] = value

    steps(0, levels, fill, 2)

    def shift(n):
        z = level_of(side, n, levels)
        fields = [codes[n].astype(F32)] + [it[z, c] for c in range(4)]
        fields += [rt[z, c] for c in range(4)] + [st[z]]
        for k, value in enumerate(fields):
            pre[n, k] = roll_lanes(roll_rows(value, 1), 1)

    steps(0, levels, shift, 8)

    def gather(n):
        for k in range(SUMMED):
            w = u[n + 1, k] + 0.5 * (u[n, k] + u[n + 2, k])
            g = wl * roll_rows(w, 2) + wu * w
            b = jnp.where(row >= 1, roll_rows(w, 1), 0.0) + g
            sown[n, k] = jnp.where(lane >= 1, roll_lanes(g, 1), 0.0) + (vl * roll_lanes(b, 2) + vu * b)

    steps(0, levels + 1, gather, 4)


def factor(m):
    rows = {(i, j): m[AT[i, j]] for i in range(4) for j in range(i + 1)}
    lower, inverse = {}, []
    for p in range(4):
        inverse.append(1.0 / rows[p, p])
        for i in range(p + 1, 4):
            lower[i, p] = rows[i, p] * inverse[p]
        for i in range(p + 1, 4):
            for j in range(p + 1, i + 1):
                rows[i, j] = rows[i, j] - lower[i, p] * rows[j, p]
    return lower, inverse


def forward(lower, column):
    out = []
    for i in range(4):
        value = column[i]
        for p in range(i):
            value = value - lower[i, p] * out[p]
        out.append(value)
    return out


def backward(lower, column):
    out = list(column)
    for i in (2, 1, 0):
        for p in range(3, i, -1):
            out[i] = out[i] - lower[p, i] * out[p]
    return out


def dot(a, b):
    return (a[0] * b[0] + a[1] * b[1]) + (a[2] * b[2] + a[3] * b[3])


def reduce_block(block, value, link):
    lower, inverse = factor(block)
    columns = [forward(lower, [link[AT[i, j]] for i in range(4)]) for j in range(4)]
    scaled = [[columns[j][i] * inverse[i] for i in range(4)] for j in range(4)]
    first = forward(lower, value)
    coupled = [dot(columns[i], scaled[j]) for i, j in PAIRS]
    carried = [dot(scaled[i], first) for i in range(4)]
    gain = [backward(lower, scaled[j]) for j in range(4)]
    rest = backward(lower, [first[i] * inverse[i] for i in range(4)])
    return [[gain[j][i] for j in range(4)] for i in range(4)], rest, coupled, carried


def solve_block(block, value):
    lower, inverse = factor(block)
    first = forward(lower, value)
    return backward(lower, [first[i] * inverse[i] for i in range(4)])


def line_sum(values):
    return values + 0.5 * (roll_rows(values, 1) + roll_rows(values, -1))


def lane_sum(values):
    return values + 0.5 * (roll_lanes(values, 2) + roll_lanes(values, -2))


def lengthen(values, rows):
    return jnp.concatenate([values, jnp.zeros((rows - values.shape[0], LANES), F32)], axis=0)


def line_kernel(levels, sown, pre, xm, tables, sums, moved, xw, xl):
    line = levels + PAD
    first_x = lax.axis_index("lx") == 0
    first_y = lax.axis_index("ly") == 0
    row = row_index()
    wl1 = jnp.where(first_x, 0.0, 0.5).astype(F32)
    lane = lax.broadcasted_iota(jnp.int32, (line, LANES), 1)
    vl = jnp.where(lane >= 2, 0.5, 0.0).astype(F32)
    vu = jnp.where(first_y & (lane == 0), 0.0, 0.5).astype(F32)
    lines = []
    for r in range(2):
        codes = lengthen(xm[10 * r], line).astype(jnp.int32)
        lines.append(summed_fields(tables, codes, [lengthen(xm[10 * r + 1 + c], line) for c in range(4)]))
    for k in range(SUMMED):
        near, far = line_sum(lines[0][k]), line_sum(lines[1][k])
        g0, g1 = 0.5 * far, wl1 * near
        for r, (g, b) in enumerate(((g0, near + g0), (g1, g1))):
            at = (2 * k + r) * line
            xw[at : at + line, :] = jnp.where(lane >= 1, roll_lanes(g, 1), 0.0) + (
                vl * roll_lanes(b, 2) + vu * b
            )
    for k in range(10):
        xl[k] = roll_lanes(xm[k], 1)

    def add(n):
        for k in range(SUMMED):
            beyond = xw[pl.ds(2 * k * line + n, ROWS, stride=line), :]
            sums[n, k] = sown[n, k] + jnp.where(row < 2, beyond, 0.0)

    def fill(n):
        for k in range(10):
            moved[n, k] = jnp.where(row < 1, xl[k, pl.ds(n, 1), :], pre[n, k])

    steps(0, levels + 1, add, 4)
    steps(0, levels, fill, 8)


def sweep_kernel(
    levels, sown, pre, ym, dm, codes, tables,
    gains, rests, message, codes_s,
    yv, ys, fs, rs, ss, ps, ms, qs, vs, total,
):
    first_x = lax.axis_index("lx") == 0
    first_y = lax.axis_index("ly") == 0
    row, lane = row_index(), lane_index()
    wl = jnp.where(first_x & (row == 1), 0.0, 0.5).astype(F32)
    wu = jnp.where(first_x & (row == 0), 0.0, 0.5).astype(F32)
    vl1 = jnp.where(first_y, 0.0, 0.5).astype(F32)
    even = lane % 2 == 0

    corner = [lengthen(dm[k], ROWS) for k in range(10)]
    for k in range(10):
        ys[k] = jnp.where(row < 1, roll_rows(corner[k], -1), roll_rows(ym[k], 1))
    side_u = summed_fields(tables, ym[0].astype(jnp.int32), [ym[1 + c] for c in range(4)])
    corner_u = summed_fields(tables, corner[0].astype(jnp.int32), corner[1:5])
    for k in range(SUMMED):
        one = jnp.where(row < 1, roll_rows(corner_u[k], -1), roll_rows(side_u[k], 1))
        two = jnp.where(row < 2, corner_u[k], roll_rows(side_u[k], 2))
        g = wl * two + wu * side_u[k]
        b = one + g
        summed = lane_sum(b)
        across = roll_lanes(g, -1) + 0.5 * (roll_lanes(g, 1) + roll_lanes(g, -3))
        yv[k] = jnp.where(even, across + 0.5 * summed, vl1 * summed)

    def shift(n):
        moved = [jnp.where(lane < 1, roll_lanes(ys[k], -2 * n - 1), pre[n, k]) for k in range(10)]
        codes_s[n] = moved[0].astype(jnp.int32)
        for c in range(4):
            fs[n + 1, c] = moved[1 + c]
            rs[n, c] = moved[5 + c]
        ss[n] = moved[9]

    for c in range(4):
        vs[0, c] = zero()
    for k in range(10):
        ms[0, k] = zero()

    def gather(n):
        for k in range(SUMMED):
            total[n, k] = sown[n, k] + jnp.where(lane < 2, roll_lanes(yv[k], -2 * n), 0.0)

    def assemble(n, last=False):
        sums = [total[n, k] for k in range(SUMMED)]
        act = activity(codes_s[n])
        half = 0.5 * act
        lateral = lookup(tables, 0, codes_s[n])
        below = [ms[n, k] for k in range(10)]
        if last:
            above = [zero() for _ in range(10)]
        else:
            both = half * activity(codes_s[n + 1])
            here = lookup(tables, 1, codes_s[n])
            there = lookup(tables, 1, codes_s[n + 1])
            above = [both * (here[k] + there[k]) for k in range(10)]
        block = []
        for k, (i, j) in enumerate(PAIRS):
            value = half * (lateral[k] * sums[0] + sums[1 + k]) + (below[k] + above[k])
            block.append(value + ss[n] if i == j else value)
        field = [fs[n + 1, c] for c in range(4)]
        if last:
            flux = [zero() for _ in range(4)]
        else:
            flux = apply_sym(above, [field[c] - fs[n + 2, c] for c in range(4)])
        flow = apply_sym(lateral, [sums[0] * field[c] - sums[11 + c] for c in range(4)])
        flow_back = apply_sym(sums[1:11], field)
        stored = ss[n]
        for c in range(4):
            out = half * (flow[c] + (flow_back[c] - sums[15 + c])) + (flux[c] - vs[n, c])
            qs[n, c] = act * (rs[n, c] - (stored * field[c] + out))
        for k in range(10):
            ms[n + 1, k] = above[k]
            ps[n, k] = block[k]
        for c in range(4):
            vs[n + 1, c] = flux[c]

    def eliminate(n, carry):
        coupled, carried = carry
        block = [ps[n, k] for k in range(10)]
        link = [ms[n + 1, k] for k in range(10)]
        value = [qs[n, c] + carried[c] for c in range(4)]
        gain, rest, coupled, carried = reduce_block(
            [block[k] - coupled[k] for k in range(10)], value, link
        )
        for i in range(4):
            rests[n, i] = rest[i]
            for j in range(4):
                gains[n, 4 * i + j] = gain[i][j]
        return coupled, carried

    for n in range(3):
        shift(n)
    for n in range(2):
        gather(n)
    assemble(0)

    def advance(n, carry):
        carry = eliminate(n, carry)
        assemble(n + 1)
        shift(n + 3)
        gather(n + 2)
        return carry

    zeros = [zero() for _ in range(10)]
    carry = lax.fori_loop(
        0, (levels - 3) // 2, lambda i, c: advance(2 * i + 1, advance(2 * i, c)), (zeros, zeros[:4])
    )
    carry = advance(levels - 4, carry)
    gather(levels - 1)
    gather(levels)
    carry = eliminate(levels - 3, carry)
    assemble(levels - 2)
    carry = eliminate(levels - 2, carry)
    assemble(levels - 1, True)
    coupled, carried = carry
    end_n = levels - 1
    for k in range(10):
        message[k] = ps[end_n, k] - coupled[k]
    for c in range(4):
        message[10 + c] = qs[end_n, c] + carried[c]
        message[33 + c] = fs[levels, c]
        message[56 + c] = rests[end_n - 1, c]
    for k in range(SUMMED):
        message[14 + k] = total[levels, k]
    message[37] = codes_s[end_n].astype(F32)
    message[38] = codes_s[end_n - 1].astype(F32)
    message[39] = codes[end_n].astype(F32)
    for k in range(16):
        message[40 + k] = gains[end_n - 1, k]


def back_kernel(levels, gains, rests, message, got, codes_s, tables, xs, kx, x3, y3, d3):
    lane = lane_index()
    planes = levels + 2

    def carry_on(gain, rest, x):
        out = []
        for i in range(4):
            out.append(
                rest[i] + ((gain[4 * i] * x[0] + gain[4 * i + 1] * x[1])
                           + (gain[4 * i + 2] * x[2] + gain[4 * i + 3] * x[3]))
            )
        return out

    def end_of(ref):
        code = ref[37].astype(jnp.int32)
        act = activity(code)
        part = lambda at, count: [ref[at + k] for k in range(count)]
        return code, act, part(0, 10), part(10, 4), part(14, SUMMED), part(33, 4)

    here, there = end_of(message), end_of(got)
    both = 0.5 * here[1] * there[1]
    link_here = lookup(tables, 1, here[0])
    link_there = lookup(tables, 1, there[0])
    link = [both * (link_here[k] + link_there[k]) for k in range(10)]

    def complete(one, other):
        code, act, block, value, _, field = one
        _, _, _, _, sums, field_there = other
        half = 0.5 * act
        lateral = lookup(tables, 0, code)
        added = [half * (lateral[k] * sums[0] + sums[1 + k]) + link[k] for k in range(10)]
        across = apply_sym(link, field_there)
        flow = apply_sym(lateral, sums[11:15])
        diagonal = apply_sym(added, field)
        full = [
            value[c] + act * ((across[c] + half * (flow[c] + sums[15 + c])) - diagonal[c])
            for c in range(4)
        ]
        return [block[k] + added[k] for k in range(10)], full

    block, value = complete(here, there)
    block_there, value_there = complete(there, here)
    gain, rest, coupled, carried = reduce_block(block_there, value_there, link)
    x = solve_block(
        [block[k] - coupled[k] for k in range(10)], [value[c] + carried[c] for c in range(4)]
    )
    x_met = carry_on([gain[i][j] for i in range(4) for j in range(4)], rest, x)
    x_far = carry_on([got[40 + k] for k in range(16)], [got[56 + c] for c in range(4)], x_met)
    for c in range(4):
        xs[levels - 1, c] = x[c]
        xs[levels, c] = x_met[c]
        xs[levels + 1, c] = x_far[c]

    def retreat(step, x):
        n = levels - 2 - step
        x = carry_on([gains[n, k] for k in range(16)], [rests[n, c] for c in range(4)], x)
        for c in range(4):
            xs[n, c] = x[c]
        return x

    lax.fori_loop(0, levels - 1, retreat, x)

    acc = [zero() for _ in range(8)]
    for n in range(planes):
        field = [xs[n, c] for c in range(4)]
        code = codes_s[n] if n < levels else got[37 + n - levels].astype(jnp.int32)
        act = activity(code)
        flow = [act * value for value in apply_sym(lookup(tables, 0, code), field)]
        for c in range(4):
            kx[n, c] = flow[c]
        for k, value in enumerate(field + [code.astype(F32)]):
            for r in range(2):
                at = (2 * k + r) * planes + n
                x3[at : at + 1, :] = value[r : r + 1]
        for k, value in enumerate(field + flow):
            acc[k] = jnp.where(lane // 2 == n, roll_lanes(value, 2 * n), acc[k])
    for k in range(8):
        y3[k] = acc[k]
        d3[k] = acc[k][0:2]


def own_back_kernel(levels, xs, kx, sown, pre):
    first_x = lax.axis_index("lx") == 0
    first_y = lax.axis_index("ly") == 0
    row, lane = row_index(), lane_index()
    wl = jnp.where(first_x & (row == 0), 0.0, 0.5).astype(F32)
    wu = jnp.where(row < 6, 0.5, 0.0).astype(F32)
    vl = jnp.where(first_y & (lane == 0), 0.0, 0.5).astype(F32)
    vu = jnp.where(lane < 126, 0.5, 0.0).astype(F32)

    def gather(n, first=False):
        for k in range(8):
            ref, c = (xs, k) if k < 4 else (kx, k - 4)
            outer = ref[n + 1, c] if first else ref[n - 1, c] + ref[n + 1, c]
            w = ref[n, c] + 0.5 * outer
            g = wl * w + wu * roll_rows(w, -2)
            b = jnp.where(row < 7, roll_rows(w, -1), 0.0) + g
            sown[n, k] = jnp.where(lane < 127, roll_lanes(g, -1), 0.0) + (vu * roll_lanes(b, -2) + vl * b)

    gather(0, True)
    steps(1, levels + 1, gather, 4)

    def shift(n):
        for c in range(4):
            pre[n, c] = roll_lanes(roll_rows(xs[n, c], -1), -1)

    steps(0, levels, shift, 4)


def line_back_kernel(levels, sown, pre, x3, tables, sums, moved, xw, xl):
    line = levels + PAD
    planes = levels + 2
    last_x = lax.axis_index("lx") == lax.axis_size("lx") - 1
    first_y = lax.axis_index("ly") == 0
    row = row_index()
    wu7 = jnp.where(last_x, 0.0, 0.5).astype(F32)
    lane = lax.broadcasted_iota(jnp.int32, (line, LANES), 1)
    vl = jnp.where(first_y & (lane == 0), 0.0, 0.5).astype(F32)
    vu = jnp.where(lane < 126, 0.5, 0.0).astype(F32)
    lines = []
    for r in range(2):
        parts = [
            lengthen(x3[(2 * k + r) * planes : (2 * k + r + 1) * planes, :], line) for k in range(5)
        ]
        codes = parts[4].astype(jnp.int32)
        act = activity(codes)
        flow = apply_sym(lookup(tables, 0, codes), parts[:4])
        lines.append(parts[:4] + [act * value for value in flow])
    for k in range(8):
        near, far = lines[0][k], lines[1][k]
        if k < 4:
            xl[k] = roll_lanes(near, -1)
        near, far = line_sum(near), line_sum(far)
        g6, g7 = 0.5 * near, wu7 * far
        for r, (g, b) in enumerate(((g6, g6), (g7, near + g7))):
            at = (2 * k + r + 6) * line
            xw[at : at + line, :] = jnp.where(lane < 127, roll_lanes(g, -1), 0.0) + (
                vu * roll_lanes(b, -2) + vl * b
            )

    def add(n):
        for k in range(8):
            beyond = xw[pl.ds(2 * k * line + n, ROWS, stride=line), :]
            sums[n, k] = sown[n, k] + jnp.where(row >= 6, beyond, 0.0)

    def fill(n):
        for c in range(4):
            moved[n, c] = jnp.where(row == 7, xl[c, pl.ds(n, 1), :], pre[n, c])

    steps(0, levels + 1, add, 4)
    steps(0, levels, fill, 4)


def finish_kernel(
    levels, sown, pre, y3, d3, it, codes, got, tables,
    updated, coarse, yv, ys, sm, up, co, sems,
):
    side = lax.axis_index("depth")
    first_x = lax.axis_index("lx") == 0
    last_y = lax.axis_index("ly") == lax.axis_size("ly") - 1
    last_x = lax.axis_index("lx") == lax.axis_size("lx") - 1
    row, lane = row_index(), lane_index()
    wl = jnp.where(first_x & (row == 0), 0.0, 0.5).astype(F32)
    wu = jnp.where(last_x & (row == 7), 0.0, 0.5).astype(F32)
    vu127 = jnp.where(last_y, 0.0, 0.5).astype(F32)
    even = lane % 2 == 0

    corner = [lengthen(d3[k], ROWS) for k in range(8)]
    for c in range(4):
        ys[c] = roll_rows(jnp.where(row < 1, corner[c], y3[c]), -1)

    def place(n):
        z = level_of(side, n, levels)
        for c in range(4):
            x = jnp.where(lane == 127, roll_lanes(ys[c], 127 - 2 * n), pre[n, c])
            up[z, c] = it[z, c] + x

    for n in range(levels):
        place(n)
    send_updated = pltpu.make_async_copy(up, updated, sems.at[0])
    send_updated.start()

    for k in range(8):
        two = roll_rows(jnp.where(row < 2, corner[k], y3[k]), -2)
        one = roll_rows(jnp.where(row < 1, corner[k], y3[k]), -1)
        g = wl * y3[k] + wu * two
        b = one + g
        summed = lane_sum(b)
        across = roll_lanes(g, 1) + 0.5 * (roll_lanes(g, -1) + roll_lanes(g, 3))
        yv[k] = jnp.where(even, 0.5 * summed, across + vu127 * summed)

    def smooth(n, code):
        sums = [
            sown[n, k] + jnp.where(lane >= 126, roll_lanes(yv[k], 126 - 2 * n), 0.0) for k in range(8)
        ]
        half = 0.5 * activity(code)
        flow = apply_sym(lookup(tables, 0, code), sums[:4])
        for c in range(4):
            sm[n + 1, c] = half * (flow[c] + sums[4 + c])

    for c in range(4):
        sm[0, c] = zero()
    for n in range(levels):
        smooth(n, codes[n])
    smooth(levels, got[39].astype(jnp.int32))

    step = 1 - 2 * side
    for k in range(levels // 2):
        at = side * (levels + 1) + step * 2 * k
        for c in range(4):
            co[k, c] = sm[at + step, c] + 0.5 * (sm[at, c] + sm[at + 2 * step, c])
    send_coarse = pltpu.make_async_copy(co, coarse, sems.at[1])
    send_coarse.start()
    send_updated.wait()
    send_coarse.wait()


def call(kernel, outs, *args, scratch=(), far_in=False, far_out=False):
    vmem = pl.BlockSpec(memory_space=pltpu.VMEM)
    if far_in:
        args = [pltpu.with_memory_space_constraint(x, pltpu.HBM) for x in args]
    far = pl.BlockSpec(memory_space=pltpu.HBM)
    return pl.pallas_call(
        kernel,
        out_shape=[jax.ShapeDtypeStruct(s, t) for s, t in outs],
        in_specs=[far if far_in else vmem] * len(args),
        out_specs=[far if far_out else vmem] * len(outs),
        scratch_shapes=list(scratch),
        compiler_params=pltpu.CompilerParams(vmem_limit_bytes=VMEM_LIMIT),
    )(*args)


def around(x, dx, dy):
    nx, ny = lax.axis_size("lx"), lax.axis_size("ly")
    pairs = [
        (i * ny + j, ((i + dx) % nx) * ny + (j + dy) % ny) for i in range(nx) for j in range(ny)
    ]
    return lax.ppermute(x, ("lx", "ly"), pairs)


def swap(x):
    return lax.ppermute(x, "depth", [(0, 1), (1, 0)])


def local(iterate, right_side, storage, zones, counts, materials):
    levels = zones.shape[0]
    line, planes = levels + PAD, levels + 2
    tile = (ROWS, LANES)
    vmem = lambda *shape: pltpu.VMEM(shape, F32)
    tables = jnp.broadcast_to(
        materials.transpose(0, 2, 3, 1).reshape(32, ROWS, 1), (32, ROWS, LANES)
    )
    it, rt, st, codes, xm = call(
        functools.partial(rows_kernel, levels),
        [((levels, 4) + tile, F32), ((levels, 4) + tile, F32), ((levels,) + tile, F32),
         ((levels,) + tile, jnp.int32),
         ((15, levels, LANES), F32)],
        iterate, right_side, storage, zones, counts,
        scratch=[
            pltpu.VMEM((levels,) + tile, jnp.int32), pltpu.VMEM(tile, jnp.int32),
            pltpu.SemaphoreType.DMA((5,)),
        ],
        far_in=True,
    )
    ym, dm = call(
        functools.partial(columns_kernel, levels),
        [((10,) + tile, F32), ((10, 2, LANES), F32)],
        it, rt, st, codes,
    )
    xm_in, ym_in, dm_in = around(xm, 1, 0), around(ym, 0, 1), around(dm, 1, 1)
    sown, pre = call(
        functools.partial(own_kernel, levels),
        [((levels + 1, SUMMED) + tile, F32), ((levels, 10) + tile, F32)],
        it, rt, st, codes, tables,
        scratch=[vmem(levels + 3, SUMMED, *tile)],
    )
    sums, moved = call(
        functools.partial(line_kernel, levels),
        [((levels + 1, SUMMED) + tile, F32), ((levels, 10) + tile, F32)],
        sown, pre, xm_in, tables,
        scratch=[vmem((2 * SUMMED + 12) * line, LANES), vmem(10, levels, LANES)],
    )
    gains, rests, message, codes_s = call(
        functools.partial(sweep_kernel, levels),
        [((levels - 1, 16) + tile, F32), ((levels - 1, 4) + tile, F32), ((MESSAGE,) + tile, F32),
         ((levels,) + tile, jnp.int32)],
        sums, moved, ym_in, dm_in, codes, tables,
        scratch=[
            vmem(SUMMED, *tile), vmem(10, *tile),
            vmem(planes, 4, *tile), vmem(levels, 4, *tile), vmem(levels, *tile),
            vmem(levels, 10, *tile), vmem(levels + 1, 10, *tile), vmem(levels, 4, *tile),
            vmem(levels + 1, 4, *tile), vmem(levels + 1, SUMMED, *tile),
        ],
    )
    got = swap(message)
    xs, kx, x3, y3, d3 = call(
        functools.partial(back_kernel, levels),
        [((planes, 4) + tile, F32), ((planes, 4) + tile, F32),
         ((10 * planes, LANES), F32), ((8,) + tile, F32), ((8, 2, LANES), F32)],
        gains, rests, message, got, codes_s, tables,
    )
    x3_in, y3_in, d3_in = around(x3, -1, 0), around(y3, 0, -1), around(d3, -1, -1)
    sown3, pre3 = call(
        functools.partial(own_back_kernel, levels),
        [((levels + 1, 8) + tile, F32), ((levels, 4) + tile, F32)],
        xs, kx,
    )
    sums3, moved3 = call(
        functools.partial(line_back_kernel, levels),
        [((levels + 1, 8) + tile, F32), ((levels, 4) + tile, F32)],
        sown3, pre3, x3_in, tables,
        scratch=[vmem((16 + 6) * line, LANES), vmem(4, line, LANES)],
    )
    updated, coarse = call(
        functools.partial(finish_kernel, levels),
        [((levels, 4) + tile, F32), ((levels // 2, 4) + tile, F32)],
        sums3, moved3, y3_in, d3_in, it, codes, got, tables,
        scratch=[
            vmem(8, *tile), vmem(4, *tile),
            vmem(levels + 2, 4, *tile), vmem(levels, 4, *tile), vmem(levels // 2, 4, *tile),
            pltpu.SemaphoreType.DMA((2,)),
        ],
        far_out=True,
    )
    return updated, coarse


def solution(mesh):
    placed = (
        P("depth", None, "lx", "ly"),
        P("depth", None, "lx", "ly"),
        P("depth", "lx", "ly"),
        P("depth", "lx", "ly"),
        P("lx", "ly"),
        P(),
    )
    return jax.shard_map(
        local,
        mesh=mesh,
        in_specs=placed,
        out_specs=(P("depth", None, "lx", "ly"), P("depth", None, "lx", "ly")),
        check_vma=False,
    )
```

```python
import functools

import jax
import jax.numpy as jnp
from jax import lax
from jax.experimental import pallas as pl
from jax.experimental.pallas import tpu as pltpu
from jax.sharding import PartitionSpec as P

PAIRS = [(i, j) for i in range(4) for j in range(i, 4)]
AT = {}
for _k, (_i, _j) in enumerate(PAIRS):
    AT[_i, _j] = AT[_j, _i] = _k

ROWS, LANES = 8, 128
SUMMED = 19
PAD = 8
MESSAGE = 60
F32 = jnp.float32
VMEM_LIMIT = 48 * 1024 * 1024


def row_index():
    return lax.broadcasted_iota(jnp.int32, (ROWS, LANES), 0)


def lane_index():
    return lax.broadcasted_iota(jnp.int32, (ROWS, LANES), 1)


def roll_rows(x, by):
    return pltpu.roll(x, by % x.shape[0], 0)


def roll_lanes(x, by):
    return pltpu.roll(x, by % LANES if isinstance(by, int) else lax.rem(by + LANES, LANES), 1)


def activity(codes):
    return jnp.where(codes > 0, 1.0, 0.0).astype(F32)


def lookup(tables, kind, codes):
    rows = jnp.maximum(codes - 1, 0)
    found = []
    for i, j in PAIRS:
        table = tables[kind * 16 + 4 * i + j]
        parts = [
            jnp.take_along_axis(table, rows[at : at + ROWS], axis=0, mode="promise_in_bounds")
            for at in range(0, rows.shape[0], ROWS)
        ]
        found.append(parts[0] if len(parts) == 1 else jnp.concatenate(parts, axis=0))
    return found


def apply_sym(matrix, vector):
    out = []
    for i in range(4):
        total = matrix[AT[i, 0]] * vector[0]
        for j in range(1, 4):
            total = total + matrix[AT[i, j]] * vector[j]
        out.append(total)
    return out


def summed_fields(tables, codes, field):
    act = activity(codes)
    lateral = [act * value for value in lookup(tables, 0, codes)]
    return [act] + lateral + [act * v for v in field] + apply_sym(lateral, field)


def level_of(side, n, levels):
    return side * (levels - 1) + (1 - 2 * side) * n


def steps(first, last, body, width=1):
    passes = (last - first) // width

    def one(i, carry):
        for j in range(width):
            body(first + i * width + j)
        return carry

    lax.fori_loop(0, passes, one, 0)
    for n in range(first + passes * width, last):
        body(n)


def zero():
    return jnp.zeros((ROWS, LANES), F32)


def rows_kernel(
    levels, iterate, right, storage, zones, counts,
    it, rt, st, codes_out, xm, zones_v, counts_v, sems,
):
    side = lax.axis_index("depth")
    copies = [
        pltpu.make_async_copy(source, target, sems.at[k])
        for k, (source, target) in enumerate(
            [(zones, zones_v), (counts, counts_v), (iterate, it), (right, rt), (storage, st)]
        )
    ]
    for copy in copies:
        copy.start()
    for copy in copies:
        copy.wait()
    limit = counts_v[...] - side * levels
    for n in range(levels):
        z = level_of(side, n, levels)
        code = jnp.where(z < limit, zones_v[z] + 1, 0)
        codes_out[n] = code
        fields = [code.astype(F32)] + [it[z, c] for c in range(4)]
        fields += [rt[z, c] for c in range(4)] + [st[z]]
        for k, value in enumerate(fields):
            xm[k, n : n + 1, :] = value[7:8]
            if k < 5:
                xm[10 + k, n : n + 1, :] = value[6:7]


def columns_kernel(levels, it, rt, st, codes, ym, dm):
    side = lax.axis_index("depth")
    lane = lane_index()
    acc = [zero() for _ in range(10)]
    for n in range(levels):
        z = level_of(side, n, levels)
        fields = [codes[n].astype(F32)] + [it[z, c] for c in range(4)]
        fields += [rt[z, c] for c in range(4)] + [st[z]]
        for k, value in enumerate(fields):
            acc[k] = jnp.where(lane // 2 == n, roll_lanes(value, 2 * n + 2), acc[k])
    for k in range(10):
        ym[k] = acc[k]
        dm[k] = acc[k][6:8]


def own_kernel(levels, it, rt, st, codes, tables, sown, pre, u):
    side = lax.axis_index("depth")
    first_x = lax.axis_index("lx") == 0
    first_y = lax.axis_index("ly") == 0
    row, lane = row_index(), lane_index()
    wl = jnp.where(row >= 2, 0.5, 0.0).astype(F32)
    wu = jnp.where(first_x & (row == 0), 0.0, 0.5).astype(F32)
    vl = jnp.where(lane >= 2, 0.5, 0.0).astype(F32)
    vu = jnp.where(first_y & (lane == 0), 0.0, 0.5).astype(F32)
    for k in range(SUMMED):
        u[0, k] = zero()
        u[levels + 1, k] = zero()
        u[levels + 2, k] = zero()

    def fill(n):
        z = level_of(side, n, levels)
        field = [it[z, c] for c in range(4)]
        for k, value in enumerate(summed_fields(tables, codes[n], field)):
            u[n + 1, k] = value

    steps(0, levels, fill, 4)

    def shift(n):
        z = level_of(side, n, levels)
        fields = [codes[n].astype(F32)] + [it[z, c] for c in range(4)]
        fields += [rt[z, c] for c in range(4)] + [st[z]]
        for k, value in enumerate(fields):
            pre[n, k] = roll_lanes(roll_rows(value, 1), 1)

    steps(0, levels, shift, 8)

    def gather(n):
        for k in range(SUMMED):
            w = u[n + 1, k] + 0.5 * (u[n, k] + u[n + 2, k])
            g = wl * roll_rows(w, 2) + wu * w
            b = jnp.where(row >= 1, roll_rows(w, 1), 0.0) + g
            sown[n, k] = jnp.where(lane >= 1, roll_lanes(g, 1), 0.0) + (vl * roll_lanes(b, 2) + vu * b)

    steps(0, levels + 1, gather, 4)


def factor(m):
    rows = {(i, j): m[AT[i, j]] for i in range(4) for j in range(i + 1)}
    lower, inverse = {}, []
    for p in range(4):
        inverse.append(1.0 / rows[p, p])
        for i in range(p + 1, 4):
            lower[i, p] = rows[i, p] * inverse[p]
        for i in range(p + 1, 4):
            for j in range(p + 1, i + 1):
                rows[i, j] = rows[i, j] - lower[i, p] * rows[j, p]
    return lower, inverse


def forward(lower, column):
    out = []
    for i in range(4):
        value = column[i]
        for p in range(i):
            value = value - lower[i, p] * out[p]
        out.append(value)
    return out


def backward(lower, column):
    out = list(column)
    for i in (2, 1, 0):
        for p in range(3, i, -1):
            out[i] = out[i] - lower[p, i] * out[p]
    return out


def dot(a, b):
    return (a[0] * b[0] + a[1] * b[1]) + (a[2] * b[2] + a[3] * b[3])


def reduce_block(block, value, link):
    lower, inverse = factor(block)
    columns = [forward(lower, [link[AT[i, j]] for i in range(4)]) for j in range(4)]
    scaled = [[columns[j][i] * inverse[i] for i in range(4)] for j in range(4)]
    first = forward(lower, value)
    coupled = [dot(columns[i], scaled[j]) for i, j in PAIRS]
    carried = [dot(scaled[i], first) for i in range(4)]
    gain = [backward(lower, scaled[j]) for j in range(4)]
    rest = backward(lower, [first[i] * inverse[i] for i in range(4)])
    return [[gain[j][i] for j in range(4)] for i in range(4)], rest, coupled, carried


def solve_block(block, value):
    lower, inverse = factor(block)
    first = forward(lower, value)
    return backward(lower, [first[i] * inverse[i] for i in range(4)])


def line_sum(values):
    return values + 0.5 * (roll_rows(values, 1) + roll_rows(values, -1))


def lane_sum(values):
    return values + 0.5 * (roll_lanes(values, 2) + roll_lanes(values, -2))


def lengthen(values, rows):
    return jnp.concatenate([values, jnp.zeros((rows - values.shape[0], LANES), F32)], axis=0)


def line_kernel(levels, sown, pre, xm, tables, sums, moved, xw, xl):
    line = levels + PAD
    first_x = lax.axis_index("lx") == 0
    first_y = lax.axis_index("ly") == 0
    row = row_index()
    wl1 = jnp.where(first_x, 0.0, 0.5).astype(F32)
    lane = lax.broadcasted_iota(jnp.int32, (line, LANES), 1)
    vl = jnp.where(lane >= 2, 0.5, 0.0).astype(F32)
    vu = jnp.where(first_y & (lane == 0), 0.0, 0.5).astype(F32)
    lines = []
    for r in range(2):
        codes = lengthen(xm[10 * r], line).astype(jnp.int32)
        lines.append(summed_fields(tables, codes, [lengthen(xm[10 * r + 1 + c], line) for c in range(4)]))
    for k in range(SUMMED):
        near, far = line_sum(lines[0][k]), line_sum(lines[1][k])
        g0, g1 = 0.5 * far, wl1 * near
        for r, (g, b) in enumerate(((g0, near + g0), (g1, g1))):
            at = (2 * k + r) * line
            xw[at : at + line, :] = jnp.where(lane >= 1, roll_lanes(g, 1), 0.0) + (
                vl * roll_lanes(b, 2) + vu * b
            )
    for k in range(10):
        xl[k] = roll_lanes(xm[k], 1)

    def add(n):
        for k in range(SUMMED):
            beyond = xw[pl.ds(2 * k * line + n, ROWS, stride=line), :]
            sums[n, k] = sown[n, k] + jnp.where(row < 2, beyond, 0.0)

    def fill(n):
        for k in range(10):
            moved[n, k] = jnp.where(row < 1, xl[k, pl.ds(n, 1), :], pre[n, k])

    steps(0, levels + 1, add, 4)
    steps(0, levels, fill, 8)


def sweep_kernel(
    levels, sown, pre, ym, dm, codes, tables,
    gains, rests, message, codes_s,
    yv, ys, fs, rs, ss, ps, ms, qs, vs, total,
):
    first_x = lax.axis_index("lx") == 0
    first_y = lax.axis_index("ly") == 0
    row, lane = row_index(), lane_index()
    wl = jnp.where(first_x & (row == 1), 0.0, 0.5).astype(F32)
    wu = jnp.where(first_x & (row == 0), 0.0, 0.5).astype(F32)
    vl1 = jnp.where(first_y, 0.0, 0.5).astype(F32)
    even = lane % 2 == 0

    corner = [lengthen(dm[k], ROWS) for k in range(10)]
    for k in range(10):
        ys[k] = jnp.where(row < 1, roll_rows(corner[k], -1), roll_rows(ym[k], 1))
    side_u = summed_fields(tables, ym[0].astype(jnp.int32), [ym[1 + c] for c in range(4)])
    corner_u = summed_fields(tables, corner[0].astype(jnp.int32), corner[1:5])
    for k in range(SUMMED):
        one = jnp.where(row < 1, roll_rows(corner_u[k], -1), roll_rows(side_u[k], 1))
        two = jnp.where(row < 2, corner_u[k], roll_rows(side_u[k], 2))
        g = wl * two + wu * side_u[k]
        b = one + g
        summed = lane_sum(b)
        across = roll_lanes(g, -1) + 0.5 * (roll_lanes(g, 1) + roll_lanes(g, -3))
        yv[k] = jnp.where(even, across + 0.5 * summed, vl1 * summed)

    def shift(n):
        moved = [jnp.where(lane < 1, roll_lanes(ys[k], -2 * n - 1), pre[n, k]) for k in range(10)]
        codes_s[n] = moved[0].astype(jnp.int32)
        for c in range(4):
            fs[n + 1, c] = moved[1 + c]
            rs[n, c] = moved[5 + c]
        ss[n] = moved[9]

    for c in range(4):
        vs[0, c] = zero()
    for k in range(10):
        ms[0, k] = zero()

    def gather(n):
        for k in range(SUMMED):
            total[n, k] = sown[n, k] + jnp.where(lane < 2, roll_lanes(yv[k], -2 * n), 0.0)

    def assemble(n, last=False):
        sums = [total[n, k] for k in range(SUMMED)]
        act = activity(codes_s[n])
        half = 0.5 * act
        lateral = lookup(tables, 0, codes_s[n])
        below = [ms[n, k] for k in range(10)]
        if last:
            above = [zero() for _ in range(10)]
        else:
            both = half * activity(codes_s[n + 1])
            here = lookup(tables, 1, codes_s[n])
            there = lookup(tables, 1, codes_s[n + 1])
            above = [both * (here[k] + there[k]) for k in range(10)]
        block = []
        for k, (i, j) in enumerate(PAIRS):
            value = half * (lateral[k] * sums[0] + sums[1 + k]) + (below[k] + above[k])
            block.append(value + ss[n] if i == j else value)
        field = [fs[n + 1, c] for c in range(4)]
        if last:
            flux = [zero() for _ in range(4)]
        else:
            flux = apply_sym(above, [field[c] - fs[n + 2, c] for c in range(4)])
        flow = apply_sym(lateral, [sums[0] * field[c] - sums[11 + c] for c in range(4)])
        flow_back = apply_sym(sums[1:11], field)
        stored = ss[n]
        for c in range(4):
            out = half * (flow[c] + (flow_back[c] - sums[15 + c])) + (flux[c] - vs[n, c])
            qs[n, c] = act * (rs[n, c] - (stored * field[c] + out))
        for k in range(10):
            ms[n + 1, k] = above[k]
            ps[n, k] = block[k]
        for c in range(4):
            vs[n + 1, c] = flux[c]

    def eliminate(n, carry):
        coupled, carried = carry
        block = [ps[n, k] for k in range(10)]
        link = [ms[n + 1, k] for k in range(10)]
        value = [qs[n, c] + carried[c] for c in range(4)]
        gain, rest, coupled, carried = reduce_block(
            [block[k] - coupled[k] for k in range(10)], value, link
        )
        for i in range(4):
            rests[n, i] = rest[i]
            for j in range(4):
                gains[n, 4 * i + j] = gain[i][j]
        return coupled, carried

    for n in range(3):
        shift(n)
    for n in range(2):
        gather(n)
    assemble(0)

    def advance(n, carry):
        carry = eliminate(n, carry)
        assemble(n + 1)
        shift(n + 3)
        gather(n + 2)
        return carry

    zeros = [zero() for _ in range(10)]
    carry = lax.fori_loop(
        0, (levels - 3) // 2, lambda i, c: advance(2 * i + 1, advance(2 * i, c)), (zeros, zeros[:4])
    )
    carry = advance(levels - 4, carry)
    gather(levels - 1)
    gather(levels)
    carry = eliminate(levels - 3, carry)
    assemble(levels - 2)
    carry = eliminate(levels - 2, carry)
    assemble(levels - 1, True)
    coupled, carried = carry
    end_n = levels - 1
    for k in range(10):
        message[k] = ps[end_n, k] - coupled[k]
    for c in range(4):
        message[10 + c] = qs[end_n, c] + carried[c]
        message[33 + c] = fs[levels, c]
        message[56 + c] = rests[end_n - 1, c]
    for k in range(SUMMED):
        message[14 + k] = total[levels, k]
    message[37] = codes_s[end_n].astype(F32)
    message[38] = codes_s[end_n - 1].astype(F32)
    message[39] = codes[end_n].astype(F32)
    for k in range(16):
        message[40 + k] = gains[end_n - 1, k]


def back_kernel(levels, gains, rests, message, got, codes_s, tables, xs, kx, x3, y3, d3):
    lane = lane_index()
    planes = levels + 2

    def carry_on(gain, rest, x):
        out = []
        for i in range(4):
            out.append(
                rest[i] + ((gain[4 * i] * x[0] + gain[4 * i + 1] * x[1])
                           + (gain[4 * i + 2] * x[2] + gain[4 * i + 3] * x[3]))
            )
        return out

    def end_of(ref):
        code = ref[37].astype(jnp.int32)
        act = activity(code)
        part = lambda at, count: [ref[at + k] for k in range(count)]
        return code, act, part(0, 10), part(10, 4), part(14, SUMMED), part(33, 4)

    here, there = end_of(message), end_of(got)
    both = 0.5 * here[1] * there[1]
    link_here = lookup(tables, 1, here[0])
    link_there = lookup(tables, 1, there[0])
    link = [both * (link_here[k] + link_there[k]) for k in range(10)]

    def complete(one, other):
        code, act, block, value, _, field = one
        _, _, _, _, sums, field_there = other
        half = 0.5 * act
        lateral = lookup(tables, 0, code)
        added = [half * (lateral[k] * sums[0] + sums[1 + k]) + link[k] for k in range(10)]
        across = apply_sym(link, field_there)
        flow = apply_sym(lateral, sums[11:15])
        diagonal = apply_sym(added, field)
        full = [
            value[c] + act * ((across[c] + half * (flow[c] + sums[15 + c])) - diagonal[c])
            for c in range(4)
        ]
        return [block[k] + added[k] for k in range(10)], full

    block, value = complete(here, there)
    block_there, value_there = complete(there, here)
    gain, rest, coupled, carried = reduce_block(block_there, value_there, link)
    x = solve_block(
        [block[k] - coupled[k] for k in range(10)], [value[c] + carried[c] for c in range(4)]
    )
    x_met = carry_on([gain[i][j] for i in range(4) for j in range(4)], rest, x)
    x_far = carry_on([got[40 + k] for k in range(16)], [got[56 + c] for c in range(4)], x_met)
    for c in range(4):
        xs[levels - 1, c] = x[c]
        xs[levels, c] = x_met[c]
        xs[levels + 1, c] = x_far[c]

    def retreat(step, x):
        n = levels - 2 - step
        x = carry_on([gains[n, k] for k in range(16)], [rests[n, c] for c in range(4)], x)
        for c in range(4):
            xs[n, c] = x[c]
        return x

    lax.fori_loop(0, levels - 1, retreat, x)

    acc = [zero() for _ in range(8)]
    for n in range(planes):
        field = [xs[n, c] for c in range(4)]
        code = codes_s[n] if n < levels else got[37 + n - levels].astype(jnp.int32)
        act = activity(code)
        flow = [act * value for value in apply_sym(lookup(tables, 0, code), field)]
        for c in range(4):
            kx[n, c] = flow[c]
        for k, value in enumerate(field + [code.astype(F32)]):
            for r in range(2):
                at = (2 * k + r) * planes + n
                x3[at : at + 1, :] = value[r : r + 1]
        for k, value in enumerate(field + flow):
            acc[k] = jnp.where(lane // 2 == n, roll_lanes(value, 2 * n), acc[k])
    for k in range(8):
        y3[k] = acc[k]
        d3[k] = acc[k][0:2]


def own_back_kernel(levels, xs, kx, sown, pre):
    first_x = lax.axis_index("lx") == 0
    first_y = lax.axis_index("ly") == 0
    row, lane = row_index(), lane_index()
    wl = jnp.where(first_x & (row == 0), 0.0, 0.5).astype(F32)
    wu = jnp.where(row < 6, 0.5, 0.0).astype(F32)
    vl = jnp.where(first_y & (lane == 0), 0.0, 0.5).astype(F32)
    vu = jnp.where(lane < 126, 0.5, 0.0).astype(F32)

    def gather(n, first=False):
        for k in range(8):
            ref, c = (xs, k) if k < 4 else (kx, k - 4)
            outer = ref[n + 1, c] if first else ref[n - 1, c] + ref[n + 1, c]
            w = ref[n, c] + 0.5 * outer
            g = wl * w + wu * roll_rows(w, -2)
            b = jnp.where(row < 7, roll_rows(w, -1), 0.0) + g
            sown[n, k] = jnp.where(lane < 127, roll_lanes(g, -1), 0.0) + (vu * roll_lanes(b, -2) + vl * b)

    gather(0, True)
    steps(1, levels + 1, gather, 4)

    def shift(n):
        for c in range(4):
            pre[n, c] = roll_lanes(roll_rows(xs[n, c], -1), -1)

    steps(0, levels, shift, 8)


def line_back_kernel(levels, sown, pre, x3, tables, sums, moved, xw, xl):
    line = levels + PAD
    planes = levels + 2
    last_x = lax.axis_index("lx") == lax.axis_size("lx") - 1
    first_y = lax.axis_index("ly") == 0
    row = row_index()
    wu7 = jnp.where(last_x, 0.0, 0.5).astype(F32)
    lane = lax.broadcasted_iota(jnp.int32, (line, LANES), 1)
    vl = jnp.where(first_y & (lane == 0), 0.0, 0.5).astype(F32)
    vu = jnp.where(lane < 126, 0.5, 0.0).astype(F32)
    lines = []
    for r in range(2):
        parts = [
            lengthen(x3[(2 * k + r) * planes : (2 * k + r + 1) * planes, :], line) for k in range(5)
        ]
        codes = parts[4].astype(jnp.int32)
        act = activity(codes)
        flow = apply_sym(lookup(tables, 0, codes), parts[:4])
        lines.append(parts[:4] + [act * value for value in flow])
    for k in range(8):
        near, far = lines[0][k], lines[1][k]
        if k < 4:
            xl[k] = roll_lanes(near, -1)
        near, far = line_sum(near), line_sum(far)
        g6, g7 = 0.5 * near, wu7 * far
        for r, (g, b) in enumerate(((g6, g6), (g7, near + g7))):
            at = (2 * k + r + 6) * line
            xw[at : at + line, :] = jnp.where(lane < 127, roll_lanes(g, -1), 0.0) + (
                vu * roll_lanes(b, -2) + vl * b
            )

    def add(n):
        for k in range(8):
            beyond = xw[pl.ds(2 * k * line + n, ROWS, stride=line), :]
            sums[n, k] = sown[n, k] + jnp.where(row >= 6, beyond, 0.0)

    def fill(n):
        for c in range(4):
            moved[n, c] = jnp.where(row == 7, xl[c, pl.ds(n, 1), :], pre[n, c])

    steps(0, levels + 1, add, 8)
    steps(0, levels, fill, 8)


def finish_kernel(
    levels, sown, pre, y3, d3, it, codes, got, tables,
    updated, coarse, yv, ys, sm, up, co, sems,
):
    side = lax.axis_index("depth")
    first_x = lax.axis_index("lx") == 0
    last_y = lax.axis_index("ly") == lax.axis_size("ly") - 1
    last_x = lax.axis_index("lx") == lax.axis_size("lx") - 1
    row, lane = row_index(), lane_index()
    wl = jnp.where(first_x & (row == 0), 0.0, 0.5).astype(F32)
    wu = jnp.where(last_x & (row == 7), 0.0, 0.5).astype(F32)
    vu127 = jnp.where(last_y, 0.0, 0.5).astype(F32)
    even = lane % 2 == 0

    corner = [lengthen(d3[k], ROWS) for k in range(8)]
    for c in range(4):
        ys[c] = roll_rows(jnp.where(row < 1, corner[c], y3[c]), -1)

    def place(n):
        z = level_of(side, n, levels)
        for c in range(4):
            x = jnp.where(lane == 127, roll_lanes(ys[c], 127 - 2 * n), pre[n, c])
            up[z, c] = it[z, c] + x

    for n in range(levels):
        place(n)
    send_updated = pltpu.make_async_copy(up, updated, sems.at[0])
    send_updated.start()

    for k in range(8):
        two = roll_rows(jnp.where(row < 2, corner[k], y3[k]), -2)
        one = roll_rows(jnp.where(row < 1, corner[k], y3[k]), -1)
        g = wl * y3[k] + wu * two
        b = one + g
        summed = lane_sum(b)
        across = roll_lanes(g, 1) + 0.5 * (roll_lanes(g, -1) + roll_lanes(g, 3))
        yv[k] = jnp.where(even, 0.5 * summed, across + vu127 * summed)

    def smooth(n, code):
        sums = [
            sown[n, k] + jnp.where(lane >= 126, roll_lanes(yv[k], 126 - 2 * n), 0.0) for k in range(8)
        ]
        half = 0.5 * activity(code)
        flow = apply_sym(lookup(tables, 0, code), sums[:4])
        for c in range(4):
            sm[n + 1, c] = half * (flow[c] + sums[4 + c])

    for c in range(4):
        sm[0, c] = zero()
    for n in range(levels):
        smooth(n, codes[n])
    smooth(levels, got[39].astype(jnp.int32))

    step = 1 - 2 * side
    for k in range(levels // 2):
        at = side * (levels + 1) + step * 2 * k
        for c in range(4):
            co[k, c] = sm[at + step, c] + 0.5 * (sm[at, c] + sm[at + 2 * step, c])
    send_coarse = pltpu.make_async_copy(co, coarse, sems.at[1])
    send_coarse.start()
    send_updated.wait()
    send_coarse.wait()


def call(kernel, outs, *args, scratch=(), far_in=False, far_out=False):
    vmem = pl.BlockSpec(memory_space=pltpu.VMEM)
    if far_in:
        args = [pltpu.with_memory_space_constraint(x, pltpu.HBM) for x in args]
    far = pl.BlockSpec(memory_space=pltpu.HBM)
    return pl.pallas_call(
        kernel,
        out_shape=[jax.ShapeDtypeStruct(s, t) for s, t in outs],
        in_specs=[far if far_in else vmem] * len(args),
        out_specs=[far if far_out else vmem] * len(outs),
        scratch_shapes=list(scratch),
        compiler_params=pltpu.CompilerParams(vmem_limit_bytes=VMEM_LIMIT),
    )(*args)


def around(x, dx, dy):
    nx, ny = lax.axis_size("lx"), lax.axis_size("ly")
    pairs = [
        (i * ny + j, ((i + dx) % nx) * ny + (j + dy) % ny) for i in range(nx) for j in range(ny)
    ]
    return lax.ppermute(x, ("lx", "ly"), pairs)


def swap(x):
    return lax.ppermute(x, "depth", [(0, 1), (1, 0)])


def local(iterate, right_side, storage, zones, counts, materials):
    levels = zones.shape[0]
    line, planes = levels + PAD, levels + 2
    tile = (ROWS, LANES)
    vmem = lambda *shape: pltpu.VMEM(shape, F32)
    tables = jnp.broadcast_to(
        materials.transpose(0, 2, 3, 1).reshape(32, ROWS, 1), (32, ROWS, LANES)
    )
    it, rt, st, codes, xm = call(
        functools.partial(rows_kernel, levels),
        [((levels, 4) + tile, F32), ((levels, 4) + tile, F32), ((levels,) + tile, F32),
         ((levels,) + tile, jnp.int32),
         ((15, levels, LANES), F32)],
        iterate, right_side, storage, zones, counts,
        scratch=[
            pltpu.VMEM((levels,) + tile, jnp.int32), pltpu.VMEM(tile, jnp.int32),
            pltpu.SemaphoreType.DMA((5,)),
        ],
        far_in=True,
    )
    ym, dm = call(
        functools.partial(columns_kernel, levels),
        [((10,) + tile, F32), ((10, 2, LANES), F32)],
        it, rt, st, codes,
    )
    xm_in, ym_in, dm_in = around(xm, 1, 0), around(ym, 0, 1), around(dm, 1, 1)
    sown, pre = call(
        functools.partial(own_kernel, levels),
        [((levels + 1, SUMMED) + tile, F32), ((levels, 10) + tile, F32)],
        it, rt, st, codes, tables,
        scratch=[vmem(levels + 3, SUMMED, *tile)],
    )
    sums, moved = call(
        functools.partial(line_kernel, levels),
        [((levels + 1, SUMMED) + tile, F32), ((levels, 10) + tile, F32)],
        sown, pre, xm_in, tables,
        scratch=[vmem((2 * SUMMED + 12) * line, LANES), vmem(10, levels, LANES)],
    )
    gains, rests, message, codes_s = call(
        functools.partial(sweep_kernel, levels),
        [((levels - 1, 16) + tile, F32), ((levels - 1, 4) + tile, F32), ((MESSAGE,) + tile, F32),
         ((levels,) + tile, jnp.int32)],
        sums, moved, ym_in, dm_in, codes, tables,
        scratch=[
            vmem(SUMMED, *tile), vmem(10, *tile),
            vmem(planes, 4, *tile), vmem(levels, 4, *tile), vmem(levels, *tile),
            vmem(levels, 10, *tile), vmem(levels + 1, 10, *tile), vmem(levels, 4, *tile),
            vmem(levels + 1, 4, *tile), vmem(levels + 1, SUMMED, *tile),
        ],
    )
    got = swap(message)
    xs, kx, x3, y3, d3 = call(
        functools.partial(back_kernel, levels),
        [((planes, 4) + tile, F32), ((planes, 4) + tile, F32),
         ((10 * planes, LANES), F32), ((8,) + tile, F32), ((8, 2, LANES), F32)],
        gains, rests, message, got, codes_s, tables,
    )
    x3_in, y3_in, d3_in = around(x3, -1, 0), around(y3, 0, -1), around(d3, -1, -1)
    sown3, pre3 = call(
        functools.partial(own_back_kernel, levels),
        [((levels + 1, 8) + tile, F32), ((levels, 4) + tile, F32)],
        xs, kx,
    )
    sums3, moved3 = call(
        functools.partial(line_back_kernel, levels),
        [((levels + 1, 8) + tile, F32), ((levels, 4) + tile, F32)],
        sown3, pre3, x3_in, tables,
        scratch=[vmem((16 + 6) * line, LANES), vmem(4, line, LANES)],
    )
    updated, coarse = call(
        functools.partial(finish_kernel, levels),
        [((levels, 4) + tile, F32), ((levels // 2, 4) + tile, F32)],
        sums3, moved3, y3_in, d3_in, it, codes, got, tables,
        scratch=[
            vmem(8, *tile), vmem(4, *tile),
            vmem(levels + 2, 4, *tile), vmem(levels, 4, *tile), vmem(levels // 2, 4, *tile),
            pltpu.SemaphoreType.DMA((2,)),
        ],
        far_out=True,
    )
    return updated, coarse


def solution(mesh):
    placed = (
        P("depth", None, "lx", "ly"),
        P("depth", None, "lx", "ly"),
        P("depth", "lx", "ly"),
        P("depth", "lx", "ly"),
        P("lx", "ly"),
        P(),
    )
    return jax.shard_map(
        local,
        mesh=mesh,
        in_specs=placed,
        out_specs=(P("depth", None, "lx", "ly"), P("depth", None, "lx", "ly")),
        check_vma=False,
    )
```
